128 devices in a mesh: dp: 2 (over core), mx: 16 (over y, x), my: 4 (over z).
Axes of the slice: x: 4, y: 4, z: 4, core: 2. Of those that a mesh axis runs over, the one named last changes fastest.
Arguments:
- features: bfloat16 [1024, 6144], P('dp', ('mx', 'my')), may hold values from -9 to 9
- w_qkv: bfloat16 [6144, 24, 384], P('mx', 'my'), may hold values from -0.078125 to 0.078125
- w_up: bfloat16 [6144, 12288], P('mx', 'my'), may hold values from -0.078125 to 0.078125
- w_out: bfloat16 [24, 128, 6144], P('my', None, 'mx'), may hold values from -0.109375 to 0.109375
- w_down: bfloat16 [12288, 6144], P('my', 'mx'), may hold values from -0.0546875 to 0.0546875
- grad_out: bfloat16 [1024, 6144], P('dp', ('mx', 'my')), may hold values from -6 to 6
Outputs:
- layer_out: bfloat16 [1024, 6144], P('dp', ('mx', 'my'))
- grad_in: bfloat16 [1024, 6144], P('dp', ('mx', 'my'))
- grad_qkv: float32 [6144, 24, 384], P(('mx', 'dp'), 'my')
- grad_up: float32 [6144, 12288], P(('mx', 'dp'), 'my')
- grad_attn_out: float32 [24, 128, 6144], P('my', None, ('mx', 'dp'))
- grad_down: float32 [12288, 6144], P('my', ('mx', 'dp'))
The draws below stay inside these ranges and needn't reach their ends.
All inputs are finite; a program needn't handle non-finite values.
Results may differ from the reference program's by a relative error of at most 0.0094.
Values may be sent and summed in bfloat16 or wider, within the bound.
A program may use at most 128 MiB of HBM per device.

```python
import math
import jax
import jax.numpy as jnp
from jax import lax

D = 6144
K = 128
H = 24
FF = 12288
TOK = 512
TOKENS = 1024
N_DP = 2


def draw_features(key, part):
    key = jax.random.fold_in(key, 11)
    base_key, column_key, token_key = jax.random.split(key, 3)
    position = jnp.arange(D, dtype=jnp.float32) / D
    column_scale = 10.0 ** jax.random.uniform(column_key, (D,), minval=-0.5, maxval=0.5) * 3.0 ** (position - 0.5)
    token_scale = 10.0 ** jax.random.uniform(token_key, (TOKENS,), minval=-0.3, maxval=0.3)
    base = jnp.clip(jax.random.normal(base_key, (TOKENS, D)), -3.0, 3.0)
    return (0.25 * base * token_scale[:, None] * column_scale[None, :]).astype(jnp.bfloat16)


def steps_of(rng, dims, cuts, low, largest):
    def one(dim, blocks):
        steps = jax.random.uniform(jax.random.fold_in(jax.random.fold_in(rng, 6), dim), (blocks,), jnp.float32, low / len(cuts), largest / len(cuts))
        return jnp.repeat(jnp.exp(steps), dims[dim] // blocks).reshape((-1,) + (1,) * (len(dims) - dim - 1))

    loudness = one(*cuts[0])
    for cut in cuts[1:]:
        loudness = loudness * one(*cut)
    return loudness


def bell_draw(rng, extent, deviation, bound, shards=(), kind=jnp.bfloat16):
    values = deviation * jax.random.normal(rng, extent, jnp.float32)
    if shards:
        values = values * steps_of(rng, extent, shards, -0.22, 0.18)
    return jnp.clip(values, -bound, bound).astype(kind)


def setup_inputs(seed: int = 0) -> dict:
    keys = jax.random.split(jax.random.key(seed), 7)
    features = draw_features(jax.random.fold_in(keys[6], 71), 0)
    w_qkv = bell_draw(keys[1], (D, H, 3 * K), D ** -0.5, 0.078125, ((0, 16), (1, 4)))
    w_up = bell_draw(keys[2], (D, FF), D ** -0.5, 0.078125, ((0, 16), (1, 4)))
    w_out = bell_draw(keys[3], (H, K, D), (H * K) ** -0.5, 0.109375, ((0, 4), (2, 16)))
    w_down = bell_draw(keys[4], (FF, D), FF ** -0.5, 0.0546875, ((0, 4), (1, 16)))
    grad_out = bell_draw(keys[5], (TOKENS, D), 1.0, 6.0, ((0, 2), (1, 64)))
    return {"features": features, "w_qkv": w_qkv, "w_up": w_up, "w_out": w_out, "w_down": w_down, "grad_out": grad_out}


epsilon = 1e-06

def norm_last(values):
    average = lax.optimization_barrier(jnp.mean(values, -1, keepdims=True))
    spread = lax.optimization_barrier(jnp.mean(values * values, -1, keepdims=True)) - average * average
    inverse = lax.rsqrt(spread + epsilon)
    return ((values - average) * inverse, inverse)

def norm_back(gradient, normal, inverse):
    first_mean = lax.optimization_barrier(jnp.mean(gradient, -1, keepdims=True))
    second_mean = lax.optimization_barrier(jnp.mean(gradient * normal, -1, keepdims=True))
    return inverse * (gradient - first_mean - normal * second_mean)

def gelu_value(values):
    return 0.5 * values * (1.0 + jax.scipy.special.erf(values / math.sqrt(2.0)))

def gelu_slope(values):
    return 0.5 * (1.0 + jax.scipy.special.erf(values / math.sqrt(2.0))) + values * jnp.exp(-0.5 * values * values) / math.sqrt(2.0 * math.pi)

def contract_first(left_side, right_side):
    return lax.dot_general(left_side, right_side, (((0,), (0,)), ((), ())), preferred_element_type=jnp.float32)

def contract_last(left_side, right_side):
    return lax.dot_general(left_side, right_side, (((1,), (1,)), ((), ())), preferred_element_type=jnp.float32)

def reference(features, w_qkv, w_up, w_out, w_down, grad_out):
    factor = 1.0 / math.sqrt(K)
    own = features.astype(jnp.float32)
    normal_in, inverse_in = norm_last(own)
    normed = normal_in.astype(jnp.bfloat16)
    qkv_flat = w_qkv.reshape(D, H * 3 * K)
    out_flat = w_out.reshape(H * K, D)
    joined = jnp.dot(normed, qkv_flat, preferred_element_type=jnp.float32).reshape(N_DP, TOK, H, 3 * K)
    hidden_pre = jnp.dot(normed, w_up, preferred_element_type=jnp.float32)
    query_norm, query_inv = norm_last(joined[..., :K])
    key_norm, key_inv = norm_last(joined[..., K:2 * K])
    query_b = query_norm.astype(jnp.bfloat16)
    key_b = key_norm.astype(jnp.bfloat16)
    value_b = joined[..., 2 * K:].astype(jnp.bfloat16)
    hidden_act = gelu_value(hidden_pre).astype(jnp.bfloat16)
    scores = jnp.einsum('bqhc,bkhc->bhqk', query_b.astype(jnp.float32), key_b.astype(jnp.float32)) * factor
    raised = jnp.exp(scores)
    probs = raised / lax.optimization_barrier(jnp.sum(raised, -1, keepdims=True))
    probs_b = probs.astype(jnp.bfloat16)
    attended = jnp.einsum('bhqk,bkhc->bqhc', probs_b.astype(jnp.float32), value_b.astype(jnp.float32))
    attended = attended.astype(jnp.bfloat16).reshape(TOKENS, H * K)
    branches = jnp.dot(attended, out_flat, preferred_element_type=jnp.float32) + jnp.dot(hidden_act, w_down, preferred_element_type=jnp.float32)
    layer_out = (own + branches).astype(jnp.bfloat16)
    grad_attended = contract_last(grad_out, out_flat).astype(jnp.bfloat16).reshape(N_DP, TOK, H, K)
    grad_hidden = contract_last(grad_out, w_down) * gelu_slope(hidden_pre)
    grad_probs = jnp.einsum('bqhc,bkhc->bhqk', grad_attended.astype(jnp.float32), value_b.astype(jnp.float32))
    row_dot = lax.optimization_barrier(jnp.sum(probs * grad_probs, -1, keepdims=True))
    grad_scores = (probs * (grad_probs - row_dot)).astype(jnp.bfloat16).astype(jnp.float32)
    grad_query = jnp.einsum('bhqk,bkhc->bqhc', grad_scores, key_b.astype(jnp.float32)) * factor
    grad_key = jnp.einsum('bhqk,bqhc->bkhc', grad_scores, query_b.astype(jnp.float32)) * factor
    grad_value = jnp.einsum('bhqk,bqhc->bkhc', probs_b.astype(jnp.float32), grad_attended.astype(jnp.float32))
    grad_joined = jnp.concatenate([norm_back(grad_query, query_norm, query_inv), norm_back(grad_key, key_norm, key_inv), grad_value], -1)
    grad_joined = grad_joined.astype(jnp.bfloat16).reshape(TOKENS, H * 3 * K)
    grad_hidden_b = grad_hidden.astype(jnp.bfloat16)
    grad_normed = contract_last(grad_joined, qkv_flat) + contract_last(grad_hidden_b, w_up)
    grad_in = (grad_out.astype(jnp.float32) + norm_back(grad_normed, normal_in, inverse_in)).astype(jnp.bfloat16)
    grad_qkv = contract_first(normed, grad_joined).reshape(D, H, 3 * K)
    grad_up = contract_first(normed, grad_hidden_b)
    grad_attn_out = contract_first(attended, grad_out).reshape(H, K, D)
    grad_down = contract_first(hidden_act, grad_out)
    return (layer_out, grad_in, grad_qkv, grad_up, grad_attn_out, grad_down)
```

```python
import math

import jax
import jax.numpy as jnp
from jax import lax
from jax.experimental import pallas as pl
from jax.experimental.pallas import tpu as pltpu
from jax.sharding import PartitionSpec as P

D = 6144
EPS = 1e-06
F32 = jnp.float32
BF16 = jnp.bfloat16
MESH = pl.DeviceIdType.MESH
HEADS = 6
HS = 128
TOK = 512
OWN = 32
BLK = 384
ZC = 96
FACTOR = 1.0 / math.sqrt(HS)
N_SEMS = 300
TILE = 768


def mm(a, b):
    return lax.dot_general(a, b, (((1,), (0,)), ((), ())), preferred_element_type=F32)


def mmt(a, b):
    return lax.dot_general(a, b, (((1,), (1,)), ((), ())), preferred_element_type=F32)


def mtm(a, b):
    return lax.dot_general(a, b, (((0,), (0,)), ((), ())), preferred_element_type=F32)


def gelu_value(values):
    return 0.5 * values * (1.0 + lax.erf(values / math.sqrt(2.0)))


def gelu_slope(values):
    return 0.5 * (1.0 + lax.erf(values / math.sqrt(2.0))) + values * jnp.exp(
        -0.5 * values * values
    ) / math.sqrt(2.0 * math.pi)


def head_norm(values):
    average = jnp.mean(values, -1, keepdims=True)
    spread = jnp.mean(values * values, -1, keepdims=True) - average * average
    inverse = lax.rsqrt(spread + EPS)
    return ((values - average) * inverse, inverse)


def head_norm_back(gradient, normal, inverse):
    first_mean = jnp.mean(gradient, -1, keepdims=True)
    second_mean = jnp.mean(gradient * normal, -1, keepdims=True)
    return inverse * (gradient - first_mean - normal * second_mean)


def placed(rows, columns, shift):
    row = lax.broadcasted_iota(jnp.int32, (rows, columns), 0)
    column = lax.broadcasted_iota(jnp.int32, (rows, columns), 1)
    return jnp.where(row + shift == column, 1.0, 0.0).astype(BF16)


def add_to(ref, more):
    ref[...] = (ref[...].astype(F32) + more[...].astype(F32)).astype(BF16)


class Links:
    def __init__(self, send, recv):
        self.send_sems, self.recv_sems, self.count, self.started = send, recv, 0, []
        mx = lax.axis_index("mx")
        self.x, self.y = lax.rem(mx, 4), lax.div(mx, 4)
        self.z, self.core = lax.axis_index("my"), lax.axis_index("dp")
        x, y, z = self.x, self.y, self.z
        self.xs = [lax.rem(x + i, 4) for i in range(4)]
        self.ys = [lax.rem(y + i, 4) for i in range(4)]
        self.zs = [lax.rem(z + i, 4) for i in range(4)]
        self.xd = [{"mx": y * 4 + v} for v in self.xs]
        self.yd = [{"mx": v * 4 + x} for v in self.ys]
        self.zd = [{"my": v} for v in self.zs]
        self.cd = {"dp": 1 - self.core}

    def send(self, src, dst, device):
        i = self.count
        self.count += 1
        copy = pltpu.make_async_remote_copy(
            src_ref=src,
            dst_ref=dst,
            send_sem=self.send_sems.at[i],
            recv_sem=self.recv_sems.at[i],
            device_id=device,
            device_id_type=MESH,
        )
        copy.start()
        self.started.append(copy)
        return copy

    def barrier(self):
        sem = pltpu.get_barrier_semaphore()
        peers = self.xd[1:] + self.yd[1:] + self.zd[1:] + [self.cd]
        for peer in peers:
            pl.semaphore_signal(sem, inc=1, device_id=peer, device_id_type=MESH)
        pl.semaphore_wait(sem, len(peers))


def rows_of(start, size):
    return pl.ds(pl.multiple_of(start, 16), size)


class RingSum:
    def __init__(self, links, ring, devices, chunk, first, second, opp, near):
        self.k, self.ring, self.dev = links, ring, devices
        self.chunk, self.first, self.second, self.opp, self.near = chunk, first, second, opp, near

    def start(self):
        far = self.chunk(self.ring[2])
        self.to_left = self.k.send(self.first(far), self.opp.at[1], self.dev[3])
        self.to_right = self.k.send(self.second(far), self.opp.at[0], self.dev[1])

    def middle(self):
        left, right = self.chunk(self.ring[3]), self.chunk(self.ring[1])
        self.to_left.wait_recv()
        add_to(self.first(left), self.opp.at[1])
        self.near_left = self.k.send(left, self.near.at[1], self.dev[3])
        self.to_right.wait_recv()
        add_to(self.second(right), self.opp.at[0])
        self.near_right = self.k.send(right, self.near.at[0], self.dev[1])

    def arrive(self):
        self.near_left.wait_recv()
        self.near_right.wait_recv()

    def total(self):
        self.arrive()
        own = self.chunk(self.ring[0])
        return own[...].astype(F32) + self.near[0].astype(F32) + self.near[1].astype(F32)

    def fold(self):
        own = self.chunk(self.ring[0])
        own[...] = self.total().astype(BF16)


class RingGather:
    def __init__(self, links, ring, devices, chunk, first, second):
        self.k, self.ring, self.dev = links, ring, devices
        self.chunk, self.first, self.second = chunk, first, second

    def start(self):
        own = self.chunk(self.ring[0])
        self.to_left = self.k.send(own, own, self.dev[3])
        self.to_right = self.k.send(own, own, self.dev[1])

    def middle(self):
        self.to_right.wait_recv()
        part = self.first(self.chunk(self.ring[3]))
        self.on_right = self.k.send(part, part, self.dev[1])
        self.to_left.wait_recv()
        part = self.second(self.chunk(self.ring[1]))
        self.on_left = self.k.send(part, part, self.dev[3])

    def finish(self):
        self.on_right.wait_recv()
        self.on_left.wait_recv()


def split_rows(n):
    return (lambda r: r.at[pl.ds(0, n)]), (lambda r: r.at[pl.ds(n, n)])


class Scatter:
    def __init__(self, links, part, bufs):
        k, h = links, part.shape[2] // 2
        a, b = pl.ds(0, h), pl.ds(h, h)
        a1o, a1n, b1o, b1n, o2, n2 = bufs
        x, y = k.x, k.y
        self.a1 = RingSum(k, k.ys, k.yd, lambda j: part.at[j, :, a], *split_rows(64), a1o, a1n)
        self.b1 = RingSum(
            k, k.xs, k.xd, lambda j: part.at[:, rows_of(j * 32, 32), b], *split_rows(2), b1o, b1n
        )
        self.a2 = RingSum(
            k,
            k.xs,
            k.xd,
            lambda j: part.at[y, rows_of(j * 32, 32), a],
            *split_rows(16),
            o2.at[0],
            n2.at[0],
        )
        self.b2 = RingSum(
            k,
            k.ys,
            k.yd,
            lambda j: part.at[j, rows_of(x * 32, 32), b],
            *split_rows(16),
            o2.at[1],
            n2.at[1],
        )

    def s1(self):
        self.a1.start()
        self.b1.start()

    def s2(self):
        self.a1.middle()
        self.b1.middle()

    def s3(self):
        self.a1.fold()
        self.a2.start()
        self.b1.fold()
        self.b2.start()

    def s4(self):
        self.a2.middle()
        self.b2.middle()

    def fin(self):
        return self.a2.total(), self.b2.total()


def scatter_scratch(c):
    h = c // 2
    return [
        pltpu.VMEM((4, 128, c), BF16),
        pltpu.VMEM((2, 64, h), BF16),
        pltpu.VMEM((2, 128, h), BF16),
        pltpu.VMEM((2, 2, 32, h), BF16),
        pltpu.VMEM((2, 4, 32, h), BF16),
        pltpu.VMEM((2, 2, 16, h), BF16),
        pltpu.VMEM((2, 2, 32, h), BF16),
    ]


class Gather:
    def __init__(self, links, full):
        k, h = links, full.shape[2] // 2
        a, b = pl.ds(0, h), pl.ds(h, h)
        x, y = k.x, k.y
        self.full, self.a, self.b = full, a, b
        self.a1 = RingGather(
            k, k.xs, k.xd, lambda j: full.at[y, rows_of(j * 32, 32), a], *split_rows(16)
        )
        self.b1 = RingGather(
            k, k.ys, k.yd, lambda j: full.at[j, rows_of(x * 32, 32), b], *split_rows(16)
        )
        self.a2 = RingGather(k, k.ys, k.yd, lambda j: full.at[j, :, a], *split_rows(64))
        self.b2 = RingGather(
            k, k.xs, k.xd, lambda j: full.at[:, rows_of(j * 32, 32), b], *split_rows(2)
        )
        self.k = k

    def put(self, start, value):
        self.full[self.k.y, rows_of(self.k.x * 32, 32), pl.ds(start, value.shape[1])] = value

    def s1(self):
        self.a1.start()
        self.b1.start()

    def s2(self):
        self.a1.middle()
        self.b1.middle()

    def s3(self):
        self.a1.finish()
        self.a2.start()
        self.b1.finish()
        self.b2.start()

    def s4(self):
        self.a2.middle()
        self.b2.middle()

    def fin(self):
        self.a2.finish()
        self.b2.finish()


def tiles(n, body):
    if n == 1:
        body(0)
    else:
        pl.loop(0, n)(body)


def cols(t):
    return pl.ds(pl.multiple_of(t * TILE, TILE), TILE)


def exchange(links, ring, devices, buf, value):
    me = ring[0]
    buf[me] = value
    return [links.send(buf.at[me], buf.at[me], devices[i]) for i in (1, 2, 3)]


def collect(copies, buf):
    for copy in copies:
        copy.wait_recv()
    return (buf[0] + buf[1]) + (buf[2] + buf[3])


def row_pack(first, second):
    width = first.shape[1]
    row = lax.broadcasted_iota(jnp.int32, (8, width), 0)
    one = jnp.where(row == 0, 1.0, 0.0).astype(BF16)
    two = jnp.where(row == 1, 1.0, 0.0).astype(BF16)

    def summed(pick, values):
        high = values.astype(BF16)
        rest = values - high.astype(F32)
        middle = rest.astype(BF16)
        low = (rest - middle.astype(F32)).astype(BF16)
        return mmt(pick, high) + (mmt(pick, middle) + mmt(pick, low))

    return summed(one, first) + summed(two, second)


def unpack_rows(packed):
    wide = jnp.concatenate([packed, jnp.zeros((120, packed.shape[1]), F32)], 0)
    return jnp.transpose(wide)


def scratch():
    s = {
        "send": pltpu.SemaphoreType.DMA((N_SEMS,)),
        "recv": pltpu.SemaphoreType.DMA((N_SEMS,)),
        "local": pltpu.SemaphoreType.DMA((16,)),
        "wqkv": pltpu.VMEM((BLK, 2304), BF16),
        "wup": pltpu.VMEM((BLK, 3072), BF16),
        "wout": pltpu.VMEM((768, BLK), BF16),
        "wdown": pltpu.VMEM((3072, BLK), BF16),
        "fg": pltpu.VMEM((4, TOK, ZC), BF16),
        "gg": pltpu.VMEM((4, TOK, ZC), BF16),
        "fw": pltpu.VMEM((TOK, BLK), BF16),
        "gw": pltpu.VMEM((TOK, BLK), BF16),
        "gwh": pltpu.VMEM((2, TOK, 192), BF16),
        "normed": pltpu.VMEM((TOK, BLK), BF16),
        "nT": pltpu.VMEM((BLK, TOK), BF16),
        "stx": pltpu.VMEM((4, 8, TOK), F32),
        "sty": pltpu.VMEM((4, 8, TOK), F32),
        "btx": pltpu.VMEM((4, 8, TOK), F32),
        "bty": pltpu.VMEM((4, 8, TOK), F32),
        "btz": pltpu.VMEM((4, 8, TOK), F32),
        "stat": pltpu.VMEM((TOK, 128), F32),
        "slope": pltpu.VMEM((OWN, 3072), F32),
        "joined": pltpu.VMEM((OWN, 2304), F32),
        "oacc": pltpu.VMEM((TOK, BLK), F32),
        "gacc": pltpu.VMEM((TOK, BLK), F32),
        "zp": pltpu.VMEM((2, 4, TOK, ZC), BF16),
        "zo": pltpu.VMEM((2, 2, 256, ZC), BF16),
        "zn": pltpu.VMEM((2, 2, TOK, ZC), BF16),
        "sdown": pltpu.VMEM((2, 3072, 192), BF16),
        "sattn": pltpu.VMEM((2, 768, 192), BF16),
        "sup": pltpu.VMEM((2, 192, 3072), BF16),
        "sqkv": pltpu.VMEM((2, 192, 2304), BF16),
    }
    for name, c in STREAMS:
        for i, item in enumerate(scatter_scratch(c)):
            s[name + str(i)] = item
    for name, c in GATHERS:
        s[name] = pltpu.VMEM((4, 128, c), BF16)
    return s


STREAMS = (
    ("Ba", 768),
    ("Bh1", 1536),
    ("Bh2", 1536),
    ("Fq", 2304),
    ("Fh1", 1536),
    ("Fh2", 1536),
    ("Dk", 1536),
)
GATHERS = (
    ("KV", 1536),
    ("H1", 1536),
    ("H2", 1536),
    ("G1", 1536),
    ("G2", 1536),
    ("AT", 768),
    ("GJ", 2304),
)


def kernel(names, feat, gout, w_qkv, w_up, w_out, w_down, *rest):
    layer_o, gin_o = rest[:2]
    (own_qkv, got_qkv, own_up, got_up, own_attn, got_attn, own_down, got_down) = rest[2:10]
    s = dict(zip(names, rest[10:]))
    k = Links(s["send"], s["recv"])
    z, core = k.z, k.core
    local = s["local"]
    fg, gg, fw, gw = s["fg"], s["gg"], s["fw"], s["gw"]

    loads = [
        pltpu.make_async_copy(src, dst, local.at[i])
        for i, (src, dst) in enumerate(
            (
                (gout, gg.at[z]),
                (feat, fg.at[z]),
                (w_out, s["wout"]),
                (w_down, s["wdown"]),
                (w_qkv, s["wqkv"]),
                (w_up, s["wup"]),
            )
        )
    ]
    for load in loads:
        load.start()
    k.barrier()

    def zgather(buf):
        return RingGather(k, k.zs, k.zd, lambda j: buf.at[j], *split_rows(256))

    def widen(buf, out):
        total = mm(buf[0], placed(ZC, BLK, 0))
        for j in (1, 2, 3):
            total += mm(buf[j], placed(ZC, BLK, j * ZC))
        out[...] = total.astype(BF16)

    zg, zf = zgather(gg), zgather(fg)
    loads[0].wait()
    zg.start()
    loads[1].wait()
    zf.start()
    zg.middle()
    zf.middle()
    zg.finish()
    widen(gg, gw)

    R = {}
    for name, c in STREAMS:
        part = s[name + "0"]
        R[name] = Scatter(k, part, [s[name + str(i)] for i in range(1, 7)])
    G = {name: Gather(k, s[name]) for name, c in GATHERS}

    def product(name, fn, n):
        part = s[name + "0"]

        def body(t):
            part[:, :, cols(t)] = fn(t).astype(BF16).reshape(4, 128, TILE)

        tiles(n, body)

    def back(base):
        return lambda t: mmt(
            gw[...], s["wdown"][pl.ds(pl.multiple_of(base + t * TILE, TILE), TILE), :]
        )

    def forth(name, base):
        return lambda t: mm(
            s["normed"][...], s[name][:, pl.ds(pl.multiple_of(base + t * TILE, TILE), TILE)]
        )

    loads[2].wait()
    product("Ba", lambda t: mmt(gw[...], s["wout"][...]), 1)
    R["Ba"].s1()
    loads[3].wait()
    product("Bh1", back(0), 2)
    R["Bh1"].s1()

    zf.finish()
    widen(fg, fw)
    wide = fw[...].astype(F32)
    ex = exchange(k, k.xs, k.xd, s["stx"], row_pack(wide, wide * wide))
    R["Ba"].s2()
    ey = exchange(k, k.ys, k.yd, s["sty"], collect(ex, s["stx"]))
    R["Bh1"].s2()
    stat = unpack_rows(collect(ey, s["sty"]))
    average = stat[:, 0:1] / D
    spread = stat[:, 1:2] / D - average * average
    inverse = lax.rsqrt(spread + EPS)
    lane = lax.broadcasted_iota(jnp.int32, (TOK, 128), 1)
    s["stat"][...] = jnp.where(lane == 0, average, inverse)
    s["normed"][...] = ((fw[...].astype(F32) - average) * inverse).astype(BF16)

    loads[4].wait()
    product("Fq", forth("wqkv", 0), 3)
    R["Fq"].s1()
    R["Ba"].s3()
    loads[5].wait()
    product("Fh1", forth("wup", 0), 2)
    R["Fh1"].s1()
    R["Bh1"].s3()
    R["Fq"].s2()
    R["Ba"].s4()
    product("Fh2", forth("wup", 1536), 2)
    R["Fh2"].s1()
    R["Fh1"].s2()
    R["Fq"].s3()
    R["Bh1"].s4()
    product("Bh2", back(1536), 2)
    R["Bh2"].s1()
    R["Fq"].s4()
    R["Fh2"].s2()
    R["Fh1"].s3()

    joined = s["joined"]
    low, high = R["Fq"].fin()
    joined[:, 0:1152] = low
    joined[:, 1152:2304] = high
    for h in range(HEADS):
        base = h * 3 * HS
        normal, _ = head_norm(joined[:, base + HS : base + 2 * HS])
        G["KV"].put(h * HS, normal.astype(BF16))
        G["KV"].put(768 + h * HS, joined[:, base + 2 * HS : base + 3 * HS].astype(BF16))
    G["KV"].s1()
    R["Fh1"].s4()
    R["Bh2"].s2()
    G["KV"].s2()
    R["Fh2"].s3()
    G["KV"].s3()

    slope = s["slope"]

    def activate(stream, gather, base):
        for i, value in enumerate(R[stream].fin()):
            G[gather].put(i * 768, gelu_value(value).astype(BF16))
            slope[:, base + i * 768 : base + (i + 1) * 768] = gelu_slope(value)

    def deactivate(stream, gather, base):
        for i, value in enumerate(R[stream].fin()):
            G[gather].put(
                i * 768, (value * slope[:, base + i * 768 : base + (i + 1) * 768]).astype(BF16)
            )

    activate("Fh1", "H1", 0)
    G["H1"].s1()
    R["Fh2"].s4()
    deactivate("Bh1", "G1", 0)
    G["G1"].s1()
    G["KV"].s4()
    R["Bh2"].s3()
    G["H1"].s2()
    G["G1"].s2()
    G["H1"].s3()
    s["nT"][...] = mmt(placed(BLK, BLK, 0), s["normed"][...]).astype(BF16)
    for c in range(2):
        s["gwh"][c] = (
            mm(gg[2 * c], placed(ZC, 192, 0)) + mm(gg[2 * c + 1], placed(ZC, 192, ZC))
        ).astype(BF16)

    G["KV"].fin()
    ba = R["Ba"].fin()
    kv = s["KV"]
    grads = s["joined"]
    dk0 = s["Dk0"]
    for h in range(HEADS):
        base = h * 3 * HS
        q_norm, q_inv = head_norm(joined[:, base : base + HS])
        q_b = q_norm.astype(BF16)
        keys = kv[:, :, h * HS : (h + 1) * HS].reshape(TOK, HS)
        values = kv[:, :, 768 + h * HS : 768 + (h + 1) * HS].reshape(TOK, HS)
        raised = jnp.exp(mmt(q_b, keys) * FACTOR)
        probs = raised / jnp.sum(raised, -1, keepdims=True)
        probs_b = probs.astype(BF16)
        G["AT"].put(h * HS, mm(probs_b, values).astype(BF16))
        part = ba[h // 3][:, (h % 3) * HS : (h % 3 + 1) * HS].astype(BF16)
        grad_probs = mmt(part, values)
        row_dot = jnp.sum(probs * grad_probs, -1, keepdims=True)
        grad_scores = (probs * (grad_probs - row_dot)).astype(BF16)
        grad_query = mm(grad_scores, keys) * FACTOR
        dk0[:, :, h * HS : (h + 1) * HS] = (
            (mtm(grad_scores, q_b) * FACTOR).astype(BF16).reshape(4, 128, HS)
        )
        dk0[:, :, 768 + h * HS : 768 + (h + 1) * HS] = (
            mtm(probs_b, part).astype(BF16).reshape(4, 128, HS)
        )
        grads[:, base : base + HS] = head_norm_back(grad_query, q_norm, q_inv)
    R["Dk"].s1()
    G["AT"].s1()
    activate("Fh2", "H2", 1536)
    G["H2"].s1()
    R["Bh2"].s4()
    R["Dk"].s2()
    G["AT"].s2()
    G["G1"].s3()
    G["H1"].s4()
    G["H2"].s2()
    R["Dk"].s3()
    deactivate("Bh2", "G2", 1536)
    G["G2"].s1()
    G["AT"].s3()
    G["G1"].s4()
    R["Dk"].s4()
    G["H2"].s3()
    G["G2"].s2()
    G["AT"].s4()

    key_grad, value_grad = R["Dk"].fin()
    for h in range(HEADS):
        base = h * 3 * HS
        k_norm, k_inv = head_norm(joined[:, base + HS : base + 2 * HS])
        G["GJ"].put(base, grads[:, base : base + HS].astype(BF16))
        G["GJ"].put(
            base + HS,
            head_norm_back(key_grad[:, h * HS : (h + 1) * HS], k_norm, k_inv).astype(BF16),
        )
        G["GJ"].put(base + 2 * HS, value_grad[:, h * HS : (h + 1) * HS].astype(BF16))
    G["GJ"].s1()
    G["G2"].s3()

    oacc, gacc = s["oacc"], s["gacc"]

    def rows_tile(name, t):
        return s[name][:, :, cols(t)].reshape(TOK, TILE)

    copies = []
    shares = []

    def share(stage, own_out, got_out, index, slot):
        mine = pltpu.make_async_copy(stage.at[core, *index], own_out.at[index], local.at[slot])
        mine.start()
        copies.append(mine)
        shares.append(k.send(stage.at[1 - core, *index], got_out.at[index], k.cd))

    def use_hidden(name, weight, stage, base, n, first):
        if first:
            oacc[...] = jnp.zeros_like(oacc)

        def body(t):
            block = rows_tile(name, t)
            at = pl.ds(pl.multiple_of(base + t * TILE, TILE), TILE)
            oacc[...] += mm(block, s[weight][at, :])
            for c in range(2):
                s[stage][c, at, :] = mtm(block, s["gwh"][c]).astype(BF16)

        tiles(n, body)

    def use_grads(name, weight, stage, base, n, first):
        if first:
            gacc[...] = jnp.zeros_like(gacc)

        def body(t):
            block = rows_tile(name, t)
            at = pl.ds(pl.multiple_of(base + t * TILE, TILE), TILE)
            gacc[...] += mmt(block, s[weight][:, at])
            both = mm(s["nT"][...], block).astype(BF16)
            s[stage][0, :, at] = both[0:192]
            s[stage][1, :, at] = both[192:384]

        tiles(n, body)

    G["H1"].fin()
    use_hidden("H1", "wdown", "sdown", 0, 2, True)
    share(s["sdown"], own_down, got_down, (pl.ds(0, 1536), slice(None)), 6)
    G["GJ"].s2()
    G["H2"].s4()
    G["G1"].fin()
    use_grads("G1", "wup", "sup", 0, 2, True)
    share(s["sup"], own_up, got_up, (slice(None), pl.ds(0, 1536)), 7)
    G["G2"].s4()
    G["GJ"].s3()
    G["AT"].fin()
    use_hidden("AT", "wout", "sattn", 0, 1, False)
    share(s["sattn"], own_attn, got_attn, (slice(None), slice(None)), 8)
    G["H2"].fin()
    use_hidden("H2", "wdown", "sdown", 1536, 2, False)
    share(s["sdown"], own_down, got_down, (pl.ds(1536, 1536), slice(None)), 9)

    def zscatter(i, total):
        part = s["zp"].at[i]
        rounded = total.astype(BF16)
        for j in range(4):
            row = lax.broadcasted_iota(jnp.int32, (BLK, ZC), 0)
            column = lax.broadcasted_iota(jnp.int32, (BLK, ZC), 1)
            pick = jnp.where(row == column + j * ZC, 1.0, 0.0).astype(BF16)
            part[j] = mm(rounded, pick).astype(BF16)
        return RingSum(
            k, k.zs, k.zd, lambda j: part.at[j], *split_rows(256), s["zo"].at[i], s["zn"].at[i]
        )

    zl = zscatter(0, oacc[...])
    zl.start()
    G["GJ"].s4()
    G["G2"].fin()
    use_grads("G2", "wup", "sup", 1536, 2, False)
    share(s["sup"], own_up, got_up, (slice(None), pl.ds(1536, 1536)), 10)
    zl.middle()
    layer_o[...] = (fg[z].astype(F32) + zl.total()).astype(BF16)

    G["GJ"].fin()
    use_grads("GJ", "wqkv", "sqkv", 0, 3, False)
    total = gacc[...]
    average, inverse = s["stat"][:, 0:1], s["stat"][:, 1:2]
    normal = (fw[...].astype(F32) - average) * inverse
    zi = zscatter(1, total)
    zi.start()
    ez = exchange(k, k.zs, k.zd, s["btz"], row_pack(total, total * normal))
    share(s["sqkv"], own_qkv, got_qkv, (slice(None), slice(None)), 11)
    zi.middle()
    ex = exchange(k, k.xs, k.xd, s["btx"], collect(ez, s["btz"]))
    ey = exchange(k, k.ys, k.yd, s["bty"], collect(ex, s["btx"]))
    summed = zi.total()
    sums = unpack_rows(collect(ey, s["bty"]))
    normal_own = (fg[z].astype(F32) - average) * inverse
    correction = summed - sums[:, 0:1] / D - normal_own * (sums[:, 1:2] / D)
    gin_o[...] = (gg[z].astype(F32) + inverse * correction).astype(BF16)

    for copy in copies:
        copy.wait()
    for copy in shares:
        copy.wait_recv()
    for copy in k.started:
        copy.wait_send()


def on_device(features, w_qkv, w_up, w_out, w_down, grad_out):
    qkv_flat = w_qkv.reshape(BLK, 2304)
    out_flat = w_out.reshape(768, BLK)
    shapes = scratch()
    any_spec = pl.BlockSpec(memory_space=pl.ANY)
    vmem_spec = pl.BlockSpec(memory_space=pltpu.VMEM)

    def pair(*shape):
        return [jax.ShapeDtypeStruct(shape, BF16)] * 2

    names = tuple(shapes)
    outs = pl.pallas_call(
        lambda *refs: kernel(names, *refs),
        out_shape=[jax.ShapeDtypeStruct((TOK, ZC), BF16)] * 2
        + pair(192, 2304)
        + pair(192, 3072)
        + pair(768, 192)
        + pair(3072, 192),
        in_specs=[any_spec] * 6,
        out_specs=[vmem_spec] * 2 + [any_spec] * 8,
        scratch_shapes=list(shapes.values()),
        compiler_params=pltpu.CompilerParams(
            collective_id=0, has_side_effects=True, vmem_limit_bytes=60 * 1024 * 1024
        ),
        cost_estimate=pl.CostEstimate(
            flops=11_000_000_000, bytes_accessed=20_000_000, transcendentals=1_000_000
        ),
    )(features, grad_out, qkv_flat, w_up, out_flat, w_down)
    layer_out, grad_in = outs[:2]

    def both(i):
        return outs[i].astype(F32) + outs[i + 1].astype(F32)

    return (
        layer_out,
        grad_in,
        both(2).reshape(192, HEADS, 3 * HS),
        both(4),
        both(6).reshape(HEADS, HS, 192),
        both(8),
    )


def solution(mesh):
    in_specs = (
        P("dp", ("mx", "my")),
        P("mx", "my", None),
        P("mx", "my"),
        P("my", None, "mx"),
        P("my", "mx"),
        P("dp", ("mx", "my")),
    )
    out_specs = (
        P("dp", ("mx", "my")),
        P("dp", ("mx", "my")),
        P(("mx", "dp"), "my", None),
        P(("mx", "dp"), "my"),
        P("my", None, ("mx", "dp")),
        P("my", ("mx", "dp")),
    )
    return jax.shard_map(
        on_device, mesh=mesh, in_specs=in_specs, out_specs=out_specs, check_vma=False
    )
```

```python
import math

import jax
import jax.numpy as jnp
from jax import lax
from jax.experimental import pallas as pl
from jax.experimental.pallas import tpu as pltpu
from jax.sharding import PartitionSpec as P

D = 6144
EPS = 1e-06
F32 = jnp.float32
BF16 = jnp.bfloat16
MESH = pl.DeviceIdType.MESH
HEADS = 6
HS = 128
TOK = 512
OWN = 32
BLK = 384
ZC = 96
FACTOR = 1.0 / math.sqrt(HS)
N_SEMS = 340
TILE = 768
SETTLE = 16


def mm(a, b):
    return lax.dot_general(a, b, (((1,), (0,)), ((), ())), preferred_element_type=F32)


def mmt(a, b):
    return lax.dot_general(a, b, (((1,), (1,)), ((), ())), preferred_element_type=F32)


def mtm(a, b):
    return lax.dot_general(a, b, (((0,), (0,)), ((), ())), preferred_element_type=F32)


def gelu_value(values):
    return 0.5 * values * (1.0 + lax.erf(values / math.sqrt(2.0)))


def gelu_slope(values):
    return 0.5 * (1.0 + lax.erf(values / math.sqrt(2.0))) + values * jnp.exp(
        -0.5 * values * values
    ) / math.sqrt(2.0 * math.pi)


def head_norm(values):
    average = jnp.mean(values, -1, keepdims=True)
    spread = jnp.mean(values * values, -1, keepdims=True) - average * average
    inverse = lax.rsqrt(spread + EPS)
    return ((values - average) * inverse, inverse)


def head_norm_back(gradient, normal, inverse):
    first_mean = jnp.mean(gradient, -1, keepdims=True)
    second_mean = jnp.mean(gradient * normal, -1, keepdims=True)
    return inverse * (gradient - first_mean - normal * second_mean)


def identity(n):
    row = lax.broadcasted_iota(jnp.int32, (n, n), 0)
    column = lax.broadcasted_iota(jnp.int32, (n, n), 1)
    return jnp.where(row == column, 1.0, 0.0).astype(BF16)


def add_to(ref, more):
    ref[...] = (ref[...].astype(F32) + more[...].astype(F32)).astype(ref.dtype)


class Links:
    def __init__(self, send, recv):
        self.send_sems, self.recv_sems, self.count, self.started = send, recv, 0, []
        self.turn = 0
        mx = lax.axis_index("mx")
        self.x, self.y = lax.rem(mx, 4), lax.div(mx, 4)
        self.z, self.core = lax.axis_index("my"), lax.axis_index("dp")
        x, y, z = self.x, self.y, self.z
        self.xs = [lax.rem(x + i, 4) for i in range(4)]
        self.ys = [lax.rem(y + i, 4) for i in range(4)]
        self.zs = [lax.rem(z + i, 4) for i in range(4)]
        self.xd = [{"mx": y * 4 + v} for v in self.xs]
        self.yd = [{"mx": v * 4 + x} for v in self.ys]
        self.zd = [{"my": v} for v in self.zs]
        self.cd = {"dp": 1 - self.core}

    def send(self, src, dst, device):
        i = self.count
        self.count += 1
        copy = pltpu.make_async_remote_copy(
            src_ref=src,
            dst_ref=dst,
            send_sem=self.send_sems.at[i],
            recv_sem=self.recv_sems.at[i],
            device_id=device,
            device_id_type=MESH,
        )
        copy.start()
        self.started.append((self.turn, copy))
        return copy

    def settle(self, turn):
        self.turn = turn + 1
        while self.started and self.started[0][0] <= turn - SETTLE:
            self.started.pop(0)[1].wait_send()

    def barrier(self):
        sem = pltpu.get_barrier_semaphore()
        peers = self.xd[1:] + self.yd[1:] + self.zd[1:] + [self.cd]
        for peer in peers:
            pl.semaphore_signal(sem, inc=1, device_id=peer, device_id_type=MESH)
        pl.semaphore_wait(sem, len(peers))


def rows_of(start, size):
    return pl.ds(pl.multiple_of(start, 16), size)


class RingSum:
    def __init__(self, links, ring, devices, chunk, first, second, opp, near):
        self.k, self.ring, self.dev = links, ring, devices
        self.chunk, self.first, self.second, self.opp, self.near = chunk, first, second, opp, near

    def start(self):
        far, left, right = (self.chunk(self.ring[i]) for i in (2, 3, 1))
        to_left, to_right = self.near.at[1], self.near.at[0]
        self.far_left = self.k.send(self.first(far), self.opp.at[1], self.dev[3])
        self.far_right = self.k.send(self.second(far), self.opp.at[0], self.dev[1])
        self.near_copies = [
            self.k.send(self.second(left), self.second(to_left), self.dev[3]),
            self.k.send(self.first(right), self.first(to_right), self.dev[1]),
        ]

    def middle(self):
        left, right = self.chunk(self.ring[3]), self.chunk(self.ring[1])
        self.far_left.wait_recv()
        part = self.first(left)
        add_to(part, self.opp.at[1])
        self.near_copies.append(self.k.send(part, self.first(self.near.at[1]), self.dev[3]))
        self.far_right.wait_recv()
        part = self.second(right)
        add_to(part, self.opp.at[0])
        self.near_copies.append(self.k.send(part, self.second(self.near.at[0]), self.dev[1]))

    def total(self):
        for copy in self.near_copies:
            copy.wait_recv()
        own = self.chunk(self.ring[0])
        return own[...].astype(F32) + self.near[0].astype(F32) + self.near[1].astype(F32)


class RingGather:
    def __init__(self, links, ring, devices, chunk, first, second):
        self.k, self.ring, self.dev = links, ring, devices
        self.chunk, self.first, self.second = chunk, first, second

    def start(self):
        own = self.chunk(self.ring[0])
        self.to_left = self.k.send(own, own, self.dev[3])
        self.to_right = self.k.send(own, own, self.dev[1])

    def middle(self):
        self.to_right.wait_recv()
        part = self.first(self.chunk(self.ring[3]))
        self.on_right = self.k.send(part, part, self.dev[1])
        self.to_left.wait_recv()
        part = self.second(self.chunk(self.ring[1]))
        self.on_left = self.k.send(part, part, self.dev[3])

    def finish(self):
        self.on_right.wait_recv()
        self.on_left.wait_recv()


def split_rows(n):
    return (lambda r: r.at[pl.ds(0, n)]), (lambda r: r.at[pl.ds(n, n)])


class Scatter:
    def __init__(self, links, part, bufs, ca, cb, w):
        k = links
        a, b = pl.ds(0, ca), pl.ds(ca, cb)
        a1o, a1n, b1o, b1n, a2, b2, a2o, a2n, b2o, b2n = bufs
        self.mid_a, self.mid_b = a2, b2
        if w:
            a2_chunk, a2_split = (lambda j: a2.at[:, part_of(j, w)]), split_rows(64)
            b2_chunk, b2_split = (
                lambda j: b2.at[pl.ds(lax.rem(j, 2) * 2, 2), :, part_of(lax.div(j, 2), w)]
            ), split_rows(1)
        else:
            a2_chunk, a2_split = (lambda j: a2.at[rows_of(j * 32, 32), :]), split_rows(16)
            b2_chunk, b2_split = (lambda j: b2.at[j]), split_rows(16)
        self.a1 = RingSum(k, k.ys, k.yd, lambda j: part.at[j, :, a], *split_rows(64), a1o, a1n)
        self.b1 = RingSum(
            k, k.xs, k.xd, lambda j: part.at[:, rows_of(j * 32, 32), b], *split_rows(2), b1o, b1n
        )
        self.a2 = RingSum(k, k.xs, k.xd, a2_chunk, *a2_split, a2o, a2n)
        self.b2 = RingSum(k, k.ys, k.yd, b2_chunk, *b2_split, b2o, b2n)

    def s1(self):
        self.a1.start()
        self.b1.start()

    def s2(self):
        self.a1.middle()
        self.b1.middle()

    def s3(self):
        self.mid_a[...] = self.a1.total().astype(self.mid_a.dtype)
        self.a2.start()
        self.mid_b[...] = self.b1.total().astype(self.mid_b.dtype)
        self.b2.start()

    def s4(self):
        self.a2.middle()
        self.b2.middle()

    def fin(self):
        return self.a2.total(), self.b2.total()


def part_of(j, w):
    return pl.ds(pl.multiple_of(j * w, 128), w)


def scatter_scratch(ca, cb, w, kind):
    found = [
        pltpu.VMEM((4, 128, ca + cb), BF16),
        pltpu.VMEM((2, 64, ca), BF16),
        pltpu.VMEM((2, 128, ca), BF16),
        pltpu.VMEM((2, 2, 32, cb), BF16),
        pltpu.VMEM((2, 4, 32, cb), BF16),
        pltpu.VMEM((128, ca), kind),
        pltpu.VMEM((4, 32, cb), kind),
    ]
    if w:
        return found + [
            pltpu.VMEM((2, 64, w), kind),
            pltpu.VMEM((2, 128, w), kind),
            pltpu.VMEM((2, 1, 32, w), kind),
            pltpu.VMEM((2, 2, 32, w), kind),
        ]
    return found + [
        pltpu.VMEM((2, 16, ca), kind),
        pltpu.VMEM((2, 32, ca), kind),
        pltpu.VMEM((2, 16, cb), kind),
        pltpu.VMEM((2, 32, cb), kind),
    ]


class Gather:
    def __init__(self, links, full, ca, cb, w):
        k = links
        a, b = pl.ds(0, ca), pl.ds(ca, cb)
        x, y = k.x, k.y
        self.full, self.ca, self.w, self.k = full, ca, w, k
        if w:
            a1_chunk, a1_split = (lambda j: full.at[y, :, part_of(j, w)]), split_rows(64)
            b1_chunk, b1_split = (
                lambda j: full.at[
                    pl.ds(lax.rem(j, 2) * 2, 2),
                    rows_of(x * 32, 32),
                    part_of(4 + lax.div(j, 2), w),
                ]
            ), split_rows(1)
        else:
            a1_chunk, a1_split = (lambda j: full.at[y, rows_of(j * 32, 32), a]), split_rows(16)
            b1_chunk, b1_split = (lambda j: full.at[j, rows_of(x * 32, 32), b]), split_rows(16)
        self.a1 = RingGather(k, k.xs, k.xd, a1_chunk, *a1_split)
        self.b1 = RingGather(k, k.ys, k.yd, b1_chunk, *b1_split)
        self.a2 = RingGather(k, k.ys, k.yd, lambda j: full.at[j, :, a], *split_rows(64))
        self.b2 = RingGather(
            k, k.xs, k.xd, lambda j: full.at[:, rows_of(j * 32, 32), b], *split_rows(2)
        )

    def put(self, i, value):
        at = pl.ds(0, self.ca) if i == 0 else pl.ds(self.ca, value.shape[1])
        self.full[self.k.y, rows_of(self.k.x * 32, 32), at] = value

    def put_head(self, i, start, value):
        x, y, n = self.k.x, self.k.y, value.shape[1]
        if i == 0:
            self.full[y, :, pl.ds(pl.multiple_of(x * self.w + start, 128), n)] = value
        else:
            at = pl.ds(pl.multiple_of((4 + lax.div(y, 2)) * self.w + start, 128), n)
            half = pl.ds(lax.rem(y, 2) * 2, 2)
            self.full[half, rows_of(x * 32, 32), at] = value.reshape(2, 32, n)

    def s1(self):
        self.a1.start()
        self.b1.start()

    def s2(self):
        self.a1.middle()
        self.b1.middle()

    def s3(self):
        self.a1.finish()
        self.a2.start()
        self.b1.finish()
        self.b2.start()

    def s4(self):
        self.a2.middle()
        self.b2.middle()

    def fin(self):
        self.a2.finish()
        self.b2.finish()


class KeyValue:
    def __init__(self, links, s):
        k = links
        x, y = k.x, k.y
        self.k = k
        a, b, da, db = s["KVa"], s["KVb"], s["DKa"], s["DKb"]
        self.a, self.b, self.da, self.db, self.mid, self.got = a, b, da, db, s["DKm"], s["DKg"]
        self.mine = pl.ds(lax.rem(y, 2) * 2, 2)
        self.other = pl.ds(2 - lax.rem(y, 2) * 2, 2)
        self.mate = {"mx": (y + 1 - 2 * lax.rem(y, 2)) * 4 + x}
        self.ga = RingGather(k, k.ys, k.yd, lambda j: a.at[j], *split_rows(64))
        self.gb = RingGather(k, k.xs, k.xd, lambda j: b.at[j], *split_rows(2))
        self.ra = RingSum(
            k, k.ys, k.yd, lambda j: da.at[j], *split_rows(64), s["DKao"], s["DKan"]
        )
        self.rb = RingSum(k, k.xs, k.xd, lambda j: db.at[j], *split_rows(2), s["DKbo"], s["DKbn"])

    def s1(self):
        own = self.b.at[self.k.x, self.mine]
        self.pair = self.k.send(own, own, self.mate)
        self.ga.start()

    def s2(self):
        self.pair.wait_recv()
        self.gb.start()
        self.ga.middle()

    def s3(self):
        self.gb.middle()

    def fin(self):
        self.ga.finish()
        self.gb.finish()

    def d1(self):
        self.rb.start()
        self.ra.start()

    def d2(self):
        self.rb.middle()
        self.ra.middle()

    def d3(self):
        self.mid[...] = self.rb.total()
        self.back = self.k.send(self.mid.at[self.other], self.got, self.mate)
        return self.ra.total()

    def d4(self):
        self.back.wait_recv()
        return self.mid[self.mine] + self.got[...]


def tiles(n, body):
    if n == 1:
        body(0)
    else:
        pl.loop(0, n)(body)


def cols(t):
    return pl.ds(pl.multiple_of(t * TILE, TILE), TILE)


def exchange(links, ring, devices, buf, value):
    me = ring[0]
    buf[me] = value
    return [links.send(buf.at[me], buf.at[me], devices[i]) for i in (1, 2, 3)]


def collect(copies, buf):
    for copy in copies:
        copy.wait_recv()
    return (buf[0] + buf[1]) + (buf[2] + buf[3])


def row_pack(first, second):
    row = lax.broadcasted_iota(jnp.int32, (2, TOK), 0)
    return jnp.where(row == 0, first, second)


STREAMS = (
    ("Ba", 512, 256, HS, F32),
    ("Bh1", 640, 896, 0, BF16),
    ("Bh2", 640, 896, 0, BF16),
    ("Fq", 1536, 768, 3 * HS, F32),
    ("Fh1", 640, 896, 0, BF16),
    ("Fh2", 640, 896, 0, BF16),
)
GATHERS = (
    ("H1", 640, 896, 0),
    ("H2", 640, 896, 0),
    ("G1", 640, 896, 0),
    ("G2", 640, 896, 0),
    ("AT", 512, 256, HS),
    ("GJ", 1536, 768, 3 * HS),
)


ORDER = (
    "enter",
    "zf start",
    "zg mid",
    "zf mid",
    "zg_end",
    "load 3",
    "M Bh1",
    "Bh1 s1",
    "zf_end",
    "M Bh2",
    "Bh2 s1",
    "clear",
    "load 2",
    "M Ba",
    "Bh1 s2",
    "Ba s1",
    "stat_y",
    "Bh2 s2",
    "norm",
    "load 4",
    "M Fq",
    "Fq s1",
    "load 5",
    "M Fh1",
    "M Fh2",
    "Bh2 s3",
    "Fh1 s1",
    "Bh1 s3",
    "Fq s2",
    "Fh2 s1",
    "Ba s2",
    "Bh2 s4",
    "Fh1 s2",
    "Bh1 s4",
    "Fq s3",
    "Fh2 s2",
    "Ba s3",
    "Fh1 s3",
    "Fq s4",
    "Fh2 s3",
    "Fh1 s4",
    "Ba s4",
    "project",
    "KV s1",
    "act Fh1",
    "H1 s1",
    "deact Bh1",
    "KV s2",
    "Fh2 s4",
    "G1 s1",
    "H1 s2",
    "KV s3",
    "act Fh2",
    "H1 s3",
    "KV fin",
    "attend",
    "KV d1",
    "G1 s2",
    "deact Bh2",
    "AT s1",
    "G2 s1",
    "H1 s4",
    "KV d2",
    "H2 s1",
    "G1 s3",
    "AT s2",
    "G2 s2",
    "H1 fin",
    "acc H1",
    "dw H1",
    "KV d3",
    "H2 s2",
    "KV d4",
    "GJ s1",
    "G1 s4",
    "G2 s3",
    "H2 s3",
    "AT s3",
    "GJ s2",
    "G1 fin",
    "dw G1",
    "acc G1",
    "G2 s4",
    "H2 s4",
    "AT s4",
    "GJ s3",
    "G2 fin",
    "acc G2",
    "dw G2",
    "H2 fin",
    "acc H2",
    "AT fin",
    "dw AT",
    "acc AT",
    "zl_start",
    "dw H2",
    "GJ s4",
    "zl_mid",
    "layer_out",
    "GJ fin",
    "acc GJ",
    "gin",
    "dw GJ",
    "zi_mid",
    "back_x",
    "back_y",
    "gin_out",
)


def scratch():
    s = {
        "send": pltpu.SemaphoreType.DMA((N_SEMS,)),
        "recv": pltpu.SemaphoreType.DMA((N_SEMS,)),
        "local": pltpu.SemaphoreType.DMA((16,)),
        "wqkv": pltpu.VMEM((HEADS, BLK, 3 * HS), BF16),
        "wup": pltpu.VMEM((BLK, 3072), BF16),
        "wout": pltpu.VMEM((768, BLK), BF16),
        "wdown": pltpu.VMEM((3072, BLK), BF16),
        "fg": pltpu.VMEM((4, ZC, TOK), BF16),
        "gg": pltpu.VMEM((4, ZC, TOK), BF16),
        "gw": pltpu.VMEM((TOK, BLK), BF16),
        "normed": pltpu.VMEM((TOK, BLK), BF16),
        "nT": pltpu.VMEM((BLK, TOK), BF16),
        "stx": pltpu.VMEM((4, 2, TOK), F32),
        "sty": pltpu.VMEM((4, 2, TOK), F32),
        "btx": pltpu.VMEM((4, 2, TOK), F32),
        "bty": pltpu.VMEM((4, 2, TOK), F32),
        "btz": pltpu.VMEM((4, 2, TOK), F32),
        "stat": pltpu.VMEM((2, TOK), F32),
        "slope": pltpu.VMEM((OWN, 3072), F32),
        "oacc": pltpu.VMEM((TOK, BLK), F32),
        "gacc": pltpu.VMEM((TOK, BLK), F32),
        "zp": pltpu.VMEM((2, 4, ZC, TOK), BF16),
        "zo": pltpu.VMEM((2, 2, 48, TOK), BF16),
        "zn": pltpu.VMEM((2, 2, ZC, TOK), BF16),
        "sdown": pltpu.VMEM((2, 192, 3072), BF16),
        "sattn": pltpu.VMEM((2, HEADS, 192, HS), BF16),
        "sup": pltpu.VMEM((2, 192, 3072), BF16),
        "sqkv": pltpu.VMEM((2, HEADS, 192, 3 * HS), BF16),
    }
    for name, ca, cb, w, kind in STREAMS:
        for i, item in enumerate(scatter_scratch(ca, cb, w, kind)):
            s[name + str(i)] = item
    for name, ca, cb, w in GATHERS:
        s[name] = pltpu.VMEM((4, 128, ca + cb), BF16)
    for name, shape, kind in (
        ("KVa", (4, 128, 256), BF16),
        ("KVb", (4, 4, 32, 256), BF16),
        ("DKa", (4, 128, 256), BF16),
        ("DKb", (4, 4, 32, 256), BF16),
        ("DKao", (2, 64, 256), BF16),
        ("DKan", (2, 128, 256), BF16),
        ("DKbo", (2, 2, 32, 256), BF16),
        ("DKbn", (2, 4, 32, 256), BF16),
        ("DKm", (4, 32, 256), F32),
        ("DKg", (2, 32, 256), F32),
        ("ja", (128, 3 * HS), F32),
        ("jb", (64, 3 * HS), F32),
    ):
        s[name] = pltpu.VMEM(shape, kind)
    return s


def kernel(names, feat, gout, w_qkv, w_up, w_out, w_down, *rest):
    layer_o, gin_o = rest[:2]
    (own_qkv, got_qkv, own_up, got_up, own_attn, got_attn, own_down, got_down) = rest[2:10]
    s = dict(zip(names, rest[10:]))
    k = Links(s["send"], s["recv"])
    z, core = k.z, k.core
    local = s["local"]
    fg, gg, gw = s["fg"], s["gg"], s["gw"]

    loads = [
        pltpu.make_async_copy(src, dst, local.at[i])
        for i, (src, dst) in enumerate(
            (
                (gout, gg.at[z]),
                (feat, fg.at[z]),
                (w_out, s["wout"]),
                (w_down, s["wdown"]),
                (w_qkv, s["wqkv"]),
                (w_up, s["wup"]),
            )
        )
    ]
    for load in loads:
        load.start()
    k.barrier()

    def wide(buf):
        return buf[...].reshape(BLK, TOK)

    def ring_z(buf):
        return RingGather(k, k.zs, k.zd, lambda j: buf.at[j], *split_rows(48))

    R = {}
    for name, ca, cb, w, _ in STREAMS:
        bufs = [s[name + str(i)] for i in range(1, 11)]
        R[name] = Scatter(k, s[name + "0"], bufs, ca, cb, w)
    G = {name: Gather(k, s[name], ca, cb, w) for name, ca, cb, w in GATHERS}
    KV = KeyValue(k, s)
    ops = {}
    held = {}
    for table in (R, G):
        for name, stream in table.items():
            for step in ("s1", "s2", "s3", "s4", "fin"):
                ops[name + " " + step] = getattr(stream, step)
    for step in ("s1", "s2", "s3", "fin", "d1", "d2"):
        ops["KV " + step] = getattr(KV, step)
    every = slice(None)
    oacc, gacc, slope = s["oacc"], s["gacc"], s["slope"]
    zf, zg = ring_z(fg), ring_z(gg)

    def op(function):
        ops[function.__name__] = function
        return function

    @op
    def enter():
        loads[0].wait()
        zg.start()
        loads[1].wait()

    ops["zf start"] = zf.start
    ops["zg mid"] = zg.middle
    ops["zf mid"] = zf.middle

    @op
    def clear():
        oacc[...] = jnp.zeros_like(oacc)
        gacc[...] = jnp.zeros_like(gacc)

    @op
    def zf_end():
        zf.finish()
        values = wide(fg).astype(F32)
        packed = row_pack(
            jnp.sum(values, 0, keepdims=True), jnp.sum(values * values, 0, keepdims=True)
        )
        held["ex"] = exchange(k, k.xs, k.xd, s["stx"], packed)

    @op
    def zg_end():
        zg.finish()
        gw[...] = mmt(identity(TOK), wide(gg)).astype(BF16)

    @op
    def stat_y():
        held["ey"] = exchange(k, k.ys, k.yd, s["sty"], collect(held["ex"], s["stx"]))

    @op
    def norm():
        stat = collect(held["ey"], s["sty"])
        average = stat[0:1] / D
        spread = stat[1:2] / D - average * average
        inverse = lax.rsqrt(spread + EPS)
        s["stat"][...] = row_pack(average, inverse)
        s["nT"][...] = ((wide(fg).astype(F32) - average) * inverse).astype(BF16)
        s["normed"][...] = mmt(identity(TOK), s["nT"][...]).astype(BF16)

    def tile_at(base, t):
        return pl.ds(pl.multiple_of(base + t * TILE, TILE), TILE)

    def head_cols(t):
        return pl.ds(pl.multiple_of(t * 3 * HS, 3 * HS), 3 * HS)

    def product(name, fn, n):
        part = s[name + "0"]

        def run():
            def body(t):
                part[:, :, cols(t)] = fn(t).astype(BF16).reshape(4, 128, TILE)

            tiles(n, body)

        ops["M " + name] = run

    def back(base):
        return lambda t: mmt(gw[...], s["wdown"][tile_at(base, t), :])

    def forth(base):
        return lambda t: mm(s["normed"][...], s["wup"][:, tile_at(base, t)])

    product("Ba", lambda t: mmt(gw[...], s["wout"][...]), 1)
    product("Bh1", back(0), 2)
    product("Bh2", back(1536), 2)
    product("Fh1", forth(0), 2)
    product("Fh2", forth(1536), 2)

    def product_query():
        def body(h):
            s["Fq0"][:, :, head_cols(h)] = (
                mm(s["normed"][...], s["wqkv"][h]).astype(BF16).reshape(4, 128, 3 * HS)
            )

        tiles(HEADS, body)

    ops["M Fq"] = product_query
    for i in range(2, 6):
        ops["load " + str(i)] = loads[i].wait

    def activate(stream, gather, base):
        for i, value in enumerate(R[stream].fin()):
            G[gather].put(i, gelu_value(value).astype(BF16))
            at = base + i * G[gather].ca
            slope[:, at : at + value.shape[1]] = gelu_slope(value)

    def deactivate(stream, gather, base):
        for i, value in enumerate(R[stream].fin()):
            at = base + i * G[gather].ca
            G[gather].put(i, (value * slope[:, at : at + value.shape[1]]).astype(BF16))

    ops["act Fh1"] = lambda: activate("Fh1", "H1", 0)
    ops["act Fh2"] = lambda: activate("Fh2", "H2", 1536)
    ops["deact Bh1"] = lambda: deactivate("Bh1", "G1", 0)
    ops["deact Bh2"] = lambda: deactivate("Bh2", "G2", 1536)

    @op
    def project():
        ja, jb = R["Fq"].fin()
        s["ja"][...] = ja
        s["jb"][...] = jb.reshape(64, 3 * HS)
        normal, _ = head_norm(s["ja"][:, HS : 2 * HS])
        s["KVa"][k.y, :, 0:HS] = normal.astype(BF16)
        s["KVa"][k.y, :, HS : 2 * HS] = s["ja"][:, 2 * HS :].astype(BF16)
        normal, _ = head_norm(s["jb"][:, HS : 2 * HS])
        s["KVb"][k.x, KV.mine, :, 0:HS] = normal.astype(BF16).reshape(2, 32, HS)
        s["KVb"][k.x, KV.mine, :, HS : 2 * HS] = (
            s["jb"][:, 2 * HS :].astype(BF16).reshape(2, 32, HS)
        )

    @op
    def attend():
        parts = R["Ba"].fin()
        for i, (kv, dk, own) in enumerate(
            ((s["KVa"], s["DKa"], s["ja"]), (s["KVb"], s["DKb"], s["jb"]))
        ):
            shape = kv.shape[:-1] + (HS,)
            q_norm, q_inv = head_norm(own[:, 0:HS])
            q_b = q_norm.astype(BF16)
            keys = kv[..., 0:HS].reshape(TOK, HS)
            values = kv[..., HS : 2 * HS].reshape(TOK, HS)
            raised = jnp.exp(mmt(q_b, keys) * FACTOR)
            probs = raised / jnp.sum(raised, -1, keepdims=True)
            probs_b = probs.astype(BF16)
            part = parts[i].astype(BF16).reshape(own.shape[0], HS)
            grad_probs = mmt(part, values)
            row_dot = jnp.sum(probs * grad_probs, -1, keepdims=True)
            grad_scores = (probs * (grad_probs - row_dot)).astype(BF16)
            dk[..., 0:HS] = (mtm(grad_scores, q_b) * FACTOR).astype(BF16).reshape(shape)
            dk[..., HS : 2 * HS] = mtm(probs_b, part).astype(BF16).reshape(shape)
            G["AT"].put_head(i, 0, mm(probs_b, values).astype(BF16))
            grad_query = mm(grad_scores, keys) * FACTOR
            G["GJ"].put_head(i, 0, head_norm_back(grad_query, q_norm, q_inv).astype(BF16))

    def key_value_back(i, own, value):
        k_norm, k_inv = head_norm(own[:, HS : 2 * HS])
        G["GJ"].put_head(i, HS, head_norm_back(value[:, 0:HS], k_norm, k_inv).astype(BF16))
        G["GJ"].put_head(i, 2 * HS, value[:, HS:].astype(BF16))

    ops["KV d3"] = lambda: key_value_back(0, s["ja"], KV.d3())
    ops["KV d4"] = lambda: key_value_back(1, s["jb"], KV.d4().reshape(64, 2 * HS))

    copies = []
    shares = []

    def share(stage, own_out, got_out, index):
        slot = 6 + len(copies)
        mine = pltpu.make_async_copy(stage.at[core, *index], own_out.at[index], local.at[slot])
        mine.start()
        copies.append(mine)
        shares.append(k.send(stage.at[1 - core, *index], got_out.at[index], k.cd))

    def rows_tile(name, t):
        return s[name][:, :, cols(t)].reshape(TOK, TILE)

    def per_tile(name, body, n):
        ops[name] = lambda: tiles(n, body)

    def with_hidden(name, base):
        def total(t):
            oacc[...] += mm(rows_tile(name, t), s["wdown"][tile_at(base, t), :])

        def weights(t):
            both = mm(wide(gg), rows_tile(name, t)).astype(BF16)
            s["sdown"][0, :, tile_at(base, t)] = both[0:192]
            s["sdown"][1, :, tile_at(base, t)] = both[192:384]

        def run():
            tiles(2, weights)
            share(s["sdown"], own_down, got_down, (every, pl.ds(base, 1536)))

        per_tile("acc " + name, total, 2)
        ops["dw " + name] = run

    def with_grads(name, base):
        def total(t):
            gacc[...] += mmt(rows_tile(name, t), s["wup"][:, tile_at(base, t)])

        def weights(t):
            both = mm(s["nT"][...], rows_tile(name, t)).astype(BF16)
            s["sup"][0, :, tile_at(base, t)] = both[0:192]
            s["sup"][1, :, tile_at(base, t)] = both[192:384]

        def run():
            tiles(2, weights)
            share(s["sup"], own_up, got_up, (every, pl.ds(base, 1536)))

        per_tile("acc " + name, total, 2)
        ops["dw " + name] = run

    with_hidden("H1", 0)
    with_hidden("H2", 1536)
    with_grads("G1", 0)
    with_grads("G2", 1536)

    def total_attended(t):
        oacc[...] += mm(rows_tile("AT", 0), s["wout"][...])

    def total_joined(h):
        gacc[...] += mmt(s["GJ"][:, :, head_cols(h)].reshape(TOK, 3 * HS), s["wqkv"][h])

    per_tile("acc AT", total_attended, 1)
    per_tile("acc GJ", total_joined, HEADS)

    def weights_attended():
        both = mm(wide(gg), rows_tile("AT", 0)).astype(BF16)
        for c in range(2):
            for h in range(HEADS):
                s["sattn"][c, h] = both[c * 192 : (c + 1) * 192, h * HS : (h + 1) * HS]
        share(s["sattn"], own_attn, got_attn, (every, every, every))

    ops["dw AT"] = weights_attended

    def zscatter(i, total):
        part = s["zp"].at[i]
        turned = mmt(identity(BLK), total.astype(BF16))
        part[...] = turned.astype(BF16).reshape(4, ZC, TOK)
        ring = RingSum(
            k, k.zs, k.zd, lambda j: part.at[j], *split_rows(48), s["zo"].at[i], s["zn"].at[i]
        )
        return ring, turned

    @op
    def gin():
        average, inverse = s["stat"][0:1], s["stat"][1:2]
        held["zi"], turned = zscatter(1, gacc[...])
        held["zi"].start()
        normal = (wide(fg).astype(F32) - average) * inverse
        packed = row_pack(
            jnp.sum(turned, 0, keepdims=True), jnp.sum(turned * normal, 0, keepdims=True)
        )
        held["bz"] = exchange(k, k.zs, k.zd, s["btz"], packed)

    def weights_joined():
        def body(h):
            block = s["GJ"][:, :, head_cols(h)].reshape(TOK, 3 * HS)
            both = mm(s["nT"][...], block).astype(BF16)
            s["sqkv"][0, h] = both[0:192]
            s["sqkv"][1, h] = both[192:384]

        tiles(HEADS, body)
        share(s["sqkv"], own_qkv, got_qkv, (every, every, every))

    ops["dw GJ"] = weights_joined

    @op
    def zi_mid():
        held["zi"].middle()

    @op
    def back_x():
        held["bx"] = exchange(k, k.xs, k.xd, s["btx"], collect(held["bz"], s["btz"]))

    @op
    def back_y():
        held["by"] = exchange(k, k.ys, k.yd, s["bty"], collect(held["bx"], s["btx"]))

    @op
    def gin_out():
        average, inverse = s["stat"][0:1], s["stat"][1:2]
        summed = held["zi"].total()
        sums = collect(held["by"], s["bty"])
        normal_own = (fg[z].astype(F32) - average) * inverse
        correction = summed - sums[0:1] / D - normal_own * (sums[1:2] / D)
        gin_o[...] = (gg[z].astype(F32) + inverse * correction).astype(BF16)

    @op
    def zl_start():
        held["zl"], _ = zscatter(0, oacc[...])
        held["zl"].start()

    @op
    def zl_mid():
        held["zl"].middle()

    @op
    def layer_out():
        layer_o[...] = (fg[z].astype(F32) + held["zl"].total()).astype(BF16)

    for i, name in enumerate(ORDER):
        ops[name]()
        k.settle(i)

    for copy in copies:
        copy.wait()
    for copy in shares:
        copy.wait_recv()
    k.settle(len(ORDER) + SETTLE)


def on_device(features, w_qkv, w_up, w_out, w_down, grad_out):
    out_flat = w_out.reshape(768, BLK)
    shapes = scratch()
    any_spec = pl.BlockSpec(memory_space=pl.ANY)
    vmem_spec = pl.BlockSpec(memory_space=pltpu.VMEM)

    def pair(*shape):
        return [jax.ShapeDtypeStruct(shape, BF16)] * 2

    names = tuple(shapes)
    outs = pl.pallas_call(
        lambda *refs: kernel(names, *refs),
        out_shape=pair(ZC, TOK)
        + pair(HEADS, 192, 3 * HS)
        + pair(192, 3072)
        + pair(HEADS, 192, HS)
        + pair(192, 3072),
        in_specs=[any_spec] * 6,
        out_specs=[vmem_spec] * 2 + [any_spec] * 8,
        scratch_shapes=list(shapes.values()),
        compiler_params=pltpu.CompilerParams(
            collective_id=0, has_side_effects=True, vmem_limit_bytes=60 * 1024 * 1024
        ),
        cost_estimate=pl.CostEstimate(
            flops=11_000_000_000, bytes_accessed=20_000_000, transcendentals=1_000_000
        ),
    )(features.T, grad_out.T, w_qkv.transpose(1, 0, 2), w_up, out_flat, w_down)

    def both(i):
        return outs[i].astype(F32) + outs[i + 1].astype(F32)

    return (
        outs[0].T,
        outs[1].T,
        both(2).transpose(1, 0, 2),
        both(4),
        both(6).transpose(0, 2, 1),
        both(8).T,
    )


def solution(mesh):
    in_specs = (
        P("dp", ("mx", "my")),
        P("mx", "my", None),
        P("mx", "my"),
        P("my", None, "mx"),
        P("my", "mx"),
        P("dp", ("mx", "my")),
    )
    out_specs = (
        P("dp", ("mx", "my")),
        P("dp", ("mx", "my")),
        P(("mx", "dp"), "my", None),
        P(("mx", "dp"), "my"),
        P("my", None, ("mx", "dp")),
        P("my", ("mx", "dp")),
    )
    return jax.shard_map(
        on_device, mesh=mesh, in_specs=in_specs, out_specs=out_specs, check_vma=False
    )
```

```python
import math

import jax
import jax.numpy as jnp
from jax import lax
from jax.experimental import pallas as pl
from jax.experimental.pallas import tpu as pltpu
from jax.sharding import PartitionSpec as P

D = 6144
EPS = 1e-06
F32 = jnp.float32
BF16 = jnp.bfloat16
MESH = pl.DeviceIdType.MESH
HEADS = 6
HS = 128
TOK = 512
OWN = 32
BLK = 384
ZC = 96
FACTOR = 1.0 / math.sqrt(HS)
N_SEND = 75
N_RECV = 86
TILE = 768
SETTLE = 16


def mm(a, b):
    return lax.dot_general(a, b, (((1,), (0,)), ((), ())), preferred_element_type=F32)


def mmt(a, b):
    return lax.dot_general(a, b, (((1,), (1,)), ((), ())), preferred_element_type=F32)


def mtm(a, b):
    return lax.dot_general(a, b, (((0,), (0,)), ((), ())), preferred_element_type=F32)


def gelu_value(values):
    return 0.5 * values * (1.0 + lax.erf(values / math.sqrt(2.0)))


def gelu_slope(values):
    return 0.5 * (1.0 + lax.erf(values / math.sqrt(2.0))) + values * jnp.exp(
        -0.5 * values * values
    ) / math.sqrt(2.0 * math.pi)


def head_norm(values):
    average = jnp.mean(values, -1, keepdims=True)
    spread = jnp.mean(values * values, -1, keepdims=True) - average * average
    inverse = lax.rsqrt(spread + EPS)
    return ((values - average) * inverse, inverse)


def head_norm_back(gradient, normal, inverse):
    first_mean = jnp.mean(gradient, -1, keepdims=True)
    second_mean = jnp.mean(gradient * normal, -1, keepdims=True)
    return inverse * (gradient - first_mean - normal * second_mean)


def identity(n):
    row = lax.broadcasted_iota(jnp.int32, (n, n), 0)
    column = lax.broadcasted_iota(jnp.int32, (n, n), 1)
    return jnp.where(row == column, 1.0, 0.0).astype(BF16)


def add_to(ref, more):
    ref[...] = (ref[...].astype(F32) + more[...].astype(F32)).astype(ref.dtype)


class Message:
    def __init__(self, links, copy, way, sems):
        self.links, self.copy, self.way, self.sems = links, copy, way, sems
        self.began, self.arrived = links.tick(), None

    def wait_recv(self):
        self.copy.wait_recv()
        self.arrived = self.links.tick()


class Links:
    def __init__(self, send, recv):
        self.send_sems, self.recv_sems = send, recv
        self.log, self.started, self.clock, self.turn = [], [], 0, 0
        self.free_send, self.used_send, self.last_on = [], 0, []
        mx = lax.axis_index("mx")
        self.x, self.y = lax.rem(mx, 4), lax.div(mx, 4)
        self.z, self.core = lax.axis_index("my"), lax.axis_index("dp")
        x, y, z = self.x, self.y, self.z
        self.xs = [lax.rem(x + i, 4) for i in range(4)]
        self.ys = [lax.rem(y + i, 4) for i in range(4)]
        self.zs = [lax.rem(z + i, 4) for i in range(4)]
        self.xd = [{"mx": y * 4 + v, "way": ("x", i)} for i, v in enumerate(self.xs)]
        self.yd = [{"mx": v * 4 + x, "way": ("y", i)} for i, v in enumerate(self.ys)]
        self.zd = [{"my": v, "way": ("z", i)} for i, v in enumerate(self.zs)]
        self.cd = {"dp": 1 - self.core, "way": ("core", 0)}

    def tick(self):
        self.clock += 1
        return self.clock

    def ready(self, last, way):
        if last.arrived is None:
            return False
        back = (way[0], (4 - way[1]) % 4)
        return any(
            m.way == back and m.began > last.arrived and m.arrived is not None for m in self.log
        )

    def take_recv(self, way):
        for i, last in enumerate(self.last_on):
            if self.ready(last, way):
                return i
        self.last_on.append(None)
        return len(self.last_on) - 1

    def send(self, src, dst, device):
        way = device["way"]
        to = {axis: v for axis, v in device.items() if axis != "way"}
        if self.free_send:
            i = self.free_send.pop(0)
        else:
            i = self.used_send
            self.used_send += 1
        j = self.take_recv(way)
        copy = pltpu.make_async_remote_copy(
            src_ref=src,
            dst_ref=dst,
            send_sem=self.send_sems.at[i],
            recv_sem=self.recv_sems.at[j],
            device_id=to,
            device_id_type=MESH,
        )
        copy.start()
        message = Message(self, copy, way, (i, j))
        self.last_on[j] = message
        self.log.append(message)
        self.started.append((self.turn, message))
        return message

    def settle(self, turn):
        self.turn = turn + 1
        while self.started and self.started[0][0] <= turn - SETTLE:
            message = self.started.pop(0)[1]
            message.copy.wait_send()
            self.free_send.append(message.sems[0])

    def barrier(self):
        sem = pltpu.get_barrier_semaphore()
        peers = self.xd[1:] + self.yd[1:] + self.zd[1:] + [self.cd]
        for peer in peers:
            peer = {axis: v for axis, v in peer.items() if axis != "way"}
            pl.semaphore_signal(sem, inc=1, device_id=peer, device_id_type=MESH)
        pl.semaphore_wait(sem, len(peers))


def rows_of(start, size):
    return pl.ds(pl.multiple_of(start, 16), size)


class RingSum:
    def __init__(self, links, ring, devices, chunk, first, second, opp, near):
        self.k, self.ring, self.dev = links, ring, devices
        self.chunk, self.first, self.second, self.opp, self.near = chunk, first, second, opp, near

    def start(self):
        far, left, right = (self.chunk(self.ring[i]) for i in (2, 3, 1))
        to_left, to_right = self.near.at[1], self.near.at[0]
        self.far_left = self.k.send(self.first(far), self.opp.at[1], self.dev[3])
        self.far_right = self.k.send(self.second(far), self.opp.at[0], self.dev[1])
        self.near_copies = [
            self.k.send(self.second(left), self.second(to_left), self.dev[3]),
            self.k.send(self.first(right), self.first(to_right), self.dev[1]),
        ]

    def middle(self):
        left, right = self.chunk(self.ring[3]), self.chunk(self.ring[1])
        self.far_left.wait_recv()
        part = self.first(left)
        add_to(part, self.opp.at[1])
        self.near_copies.append(self.k.send(part, self.first(self.near.at[1]), self.dev[3]))
        self.far_right.wait_recv()
        part = self.second(right)
        add_to(part, self.opp.at[0])
        self.near_copies.append(self.k.send(part, self.second(self.near.at[0]), self.dev[1]))

    def total(self):
        for copy in self.near_copies:
            copy.wait_recv()
        own = self.chunk(self.ring[0])
        return own[...].astype(F32) + self.near[0].astype(F32) + self.near[1].astype(F32)


class RingGather:
    def __init__(self, links, ring, devices, chunk, first, second):
        self.k, self.ring, self.dev = links, ring, devices
        self.chunk, self.first, self.second = chunk, first, second

    def start(self):
        own = self.chunk(self.ring[0])
        self.to_left = self.k.send(own, own, self.dev[3])
        self.to_right = self.k.send(own, own, self.dev[1])

    def middle(self):
        self.to_right.wait_recv()
        part = self.first(self.chunk(self.ring[3]))
        self.on_right = self.k.send(part, part, self.dev[1])
        self.to_left.wait_recv()
        part = self.second(self.chunk(self.ring[1]))
        self.on_left = self.k.send(part, part, self.dev[3])

    def finish(self):
        self.on_right.wait_recv()
        self.on_left.wait_recv()


def split_rows(n):
    return (lambda r: r.at[pl.ds(0, n)]), (lambda r: r.at[pl.ds(n, n)])


class Scatter:
    def __init__(self, links, part, bufs, ca, cb, w):
        k = links
        a, b = pl.ds(0, ca), pl.ds(ca, cb)
        a1o, a1n, b1o, b1n, a2, b2, a2o, a2n, b2o, b2n = bufs
        self.mid_a, self.mid_b = a2, b2
        if w:
            a2_chunk, a2_split = (lambda j: a2.at[:, part_of(j, w)]), split_rows(64)
            b2_chunk, b2_split = (
                lambda j: b2.at[pl.ds(lax.rem(j, 2) * 2, 2), :, part_of(lax.div(j, 2), w)]
            ), split_rows(1)
        else:
            a2_chunk, a2_split = (lambda j: a2.at[rows_of(j * 32, 32), :]), split_rows(16)
            b2_chunk, b2_split = (lambda j: b2.at[j]), split_rows(16)
        self.a1 = RingSum(k, k.ys, k.yd, lambda j: part.at[j, :, a], *split_rows(64), a1o, a1n)
        self.b1 = RingSum(
            k, k.xs, k.xd, lambda j: part.at[:, rows_of(j * 32, 32), b], *split_rows(2), b1o, b1n
        )
        self.a2 = RingSum(k, k.xs, k.xd, a2_chunk, *a2_split, a2o, a2n)
        self.b2 = RingSum(k, k.ys, k.yd, b2_chunk, *b2_split, b2o, b2n)

    def s1(self):
        self.a1.start()
        self.b1.start()

    def s2(self):
        self.a1.middle()
        self.b1.middle()

    def s3(self):
        self.mid_a[...] = self.a1.total().astype(self.mid_a.dtype)
        self.a2.start()
        self.mid_b[...] = self.b1.total().astype(self.mid_b.dtype)
        self.b2.start()

    def s4(self):
        self.a2.middle()
        self.b2.middle()

    def fin(self):
        return self.a2.total(), self.b2.total()


def part_of(j, w):
    return pl.ds(pl.multiple_of(j * w, 128), w)


def scatter_scratch(ca, cb, w, kind):
    found = [
        pltpu.VMEM((4, 128, ca + cb), BF16),
        pltpu.VMEM((2, 64, ca), BF16),
        pltpu.VMEM((2, 128, ca), BF16),
        pltpu.VMEM((2, 2, 32, cb), BF16),
        pltpu.VMEM((2, 4, 32, cb), BF16),
        pltpu.VMEM((128, ca), kind),
        pltpu.VMEM((4, 32, cb), kind),
    ]
    if w:
        return found + [
            pltpu.VMEM((2, 64, w), kind),
            pltpu.VMEM((2, 128, w), kind),
            pltpu.VMEM((2, 1, 32, w), kind),
            pltpu.VMEM((2, 2, 32, w), kind),
        ]
    return found + [
        pltpu.VMEM((2, 16, ca), kind),
        pltpu.VMEM((2, 32, ca), kind),
        pltpu.VMEM((2, 16, cb), kind),
        pltpu.VMEM((2, 32, cb), kind),
    ]


class Gather:
    def __init__(self, links, full, ca, cb, w):
        k = links
        a, b = pl.ds(0, ca), pl.ds(ca, cb)
        x, y = k.x, k.y
        self.full, self.ca, self.w, self.k = full, ca, w, k
        if w:
            a1_chunk, a1_split = (lambda j: full.at[y, :, part_of(j, w)]), split_rows(64)
            b1_chunk, b1_split = (
                lambda j: full.at[
                    pl.ds(lax.rem(j, 2) * 2, 2),
                    rows_of(x * 32, 32),
                    part_of(4 + lax.div(j, 2), w),
                ]
            ), split_rows(1)
        else:
            a1_chunk, a1_split = (lambda j: full.at[y, rows_of(j * 32, 32), a]), split_rows(16)
            b1_chunk, b1_split = (lambda j: full.at[j, rows_of(x * 32, 32), b]), split_rows(16)
        self.a1 = RingGather(k, k.xs, k.xd, a1_chunk, *a1_split)
        self.b1 = RingGather(k, k.ys, k.yd, b1_chunk, *b1_split)
        self.a2 = RingGather(k, k.ys, k.yd, lambda j: full.at[j, :, a], *split_rows(64))
        self.b2 = RingGather(
            k, k.xs, k.xd, lambda j: full.at[:, rows_of(j * 32, 32), b], *split_rows(2)
        )

    def put(self, i, value):
        at = pl.ds(0, self.ca) if i == 0 else pl.ds(self.ca, value.shape[1])
        self.full[self.k.y, rows_of(self.k.x * 32, 32), at] = value

    def put_head(self, i, start, value):
        x, y, n = self.k.x, self.k.y, value.shape[1]
        if i == 0:
            self.full[y, :, pl.ds(pl.multiple_of(x * self.w + start, 128), n)] = value
        else:
            at = pl.ds(pl.multiple_of((4 + lax.div(y, 2)) * self.w + start, 128), n)
            half = pl.ds(lax.rem(y, 2) * 2, 2)
            self.full[half, rows_of(x * 32, 32), at] = value.reshape(2, 32, n)

    def s1(self):
        self.a1.start()
        self.b1.start()

    def s2(self):
        self.a1.middle()
        self.b1.middle()

    def s3(self):
        self.a1.finish()
        self.a2.start()
        self.b1.finish()
        self.b2.start()

    def s4(self):
        self.a2.middle()
        self.b2.middle()

    def fin(self):
        self.a2.finish()
        self.b2.finish()


class KeyValue:
    def __init__(self, links, s):
        k = links
        x, y = k.x, k.y
        self.k = k
        a, b, da, db = s["KVa"], s["KVb"], s["DKa"], s["DKb"]
        self.a, self.b, self.da, self.db, self.mid, self.got = a, b, da, db, s["DKm"], s["DKg"]
        self.mine = pl.ds(lax.rem(y, 2) * 2, 2)
        self.other = pl.ds(2 - lax.rem(y, 2) * 2, 2)
        self.mate = {"mx": (y + 1 - 2 * lax.rem(y, 2)) * 4 + x, "way": ("mate", 0)}
        self.ga = RingGather(k, k.ys, k.yd, lambda j: a.at[j], *split_rows(64))
        self.gb = RingGather(k, k.xs, k.xd, lambda j: b.at[j], *split_rows(2))
        self.ra = RingSum(
            k, k.ys, k.yd, lambda j: da.at[j], *split_rows(64), s["DKao"], s["DKan"]
        )
        self.rb = RingSum(k, k.xs, k.xd, lambda j: db.at[j], *split_rows(2), s["DKbo"], s["DKbn"])

    def s1(self):
        own = self.b.at[self.k.x, self.mine]
        self.pair = self.k.send(own, own, self.mate)
        self.ga.start()

    def s2(self):
        self.pair.wait_recv()
        self.gb.start()
        self.ga.middle()

    def s3(self):
        self.gb.middle()

    def fin(self):
        self.ga.finish()
        self.gb.finish()

    def d1(self):
        self.rb.start()
        self.ra.start()

    def d2(self):
        self.rb.middle()
        self.ra.middle()

    def d3(self):
        self.mid[...] = self.rb.total()
        self.back = self.k.send(self.mid.at[self.other], self.got, self.mate)
        return self.ra.total()

    def d4(self):
        self.back.wait_recv()
        return self.mid[self.mine] + self.got[...]


def tiles(n, body):
    if n == 1:
        body(0)
    else:
        pl.loop(0, n)(body)


def cols(t):
    return pl.ds(pl.multiple_of(t * TILE, TILE), TILE)


def exchange(links, ring, devices, buf, value):
    me = ring[0]
    buf[me] = value
    return [links.send(buf.at[me], buf.at[me], devices[i]) for i in (1, 2, 3)]


def collect(copies, buf):
    for copy in copies:
        copy.wait_recv()
    return (buf[0] + buf[1]) + (buf[2] + buf[3])


def row_pack(first, second):
    row = lax.broadcasted_iota(jnp.int32, (2, TOK), 0)
    return jnp.where(row == 0, first, second)


STREAMS = (
    ("Ba", 512, 256, HS, F32),
    ("Bh1", 640, 896, 0, BF16),
    ("Bh2", 640, 896, 0, BF16),
    ("Fq", 1536, 768, 3 * HS, F32),
    ("Fh1", 640, 896, 0, BF16),
    ("Fh2", 640, 896, 0, BF16),
)
GATHERS = (
    ("H1", 640, 896, 0),
    ("H2", 640, 896, 0),
    ("G1", 640, 896, 0),
    ("G2", 640, 896, 0),
    ("AT", 512, 256, HS),
    ("GJ", 1536, 768, 3 * HS),
)


ORDER = (
    "enter",
    "zg mid",
    "zf start",
    "zg_end",
    "load 2",
    "M Ba",
    "Ba s1",
    "load 3",
    "M Bh2",
    "Bh2 s1",
    "zf mid",
    "M Bh1",
    "zf_end",
    "Bh2 s2",
    "stat_y",
    "Bh1 s1",
    "norm",
    "load 5",
    "M Fh2",
    "Fh2 s1",
    "load 4",
    "M Fq",
    "Bh2 s3",
    "Fh2 s2",
    "Fq s1",
    "Fh2 s3",
    "Bh2 s4",
    "M Fh1",
    "Fq s2",
    "clear",
    "Fh2 s4",
    "Ba s2",
    "Fh1 s1",
    "Fq s3",
    "act Fh2",
    "Bh1 s2",
    "deact Bh2",
    "Fq s4",
    "Fh1 s2",
    "G2 s1",
    "Bh1 s3",
    "project",
    "KV s1",
    "Fh1 s3",
    "G2 s2",
    "KV s2",
    "Ba s3",
    "KV s3",
    "Ba s4",
    "G2 s3",
    "Fh1 s4",
    "KV fin",
    "H2 s1",
    "attend",
    "KV d1",
    "Bh1 s4",
    "G2 s4",
    "act Fh1",
    "KV d2",
    "H1 s1",
    "H2 s2",
    "deact Bh1",
    "G1 s1",
    "KV d3",
    "AT s1",
    "H1 s2",
    "G1 s2",
    "KV d4",
    "GJ s1",
    "H1 s3",
    "G2 fin",
    "dw G2",
    "GJ s2",
    "G1 s3",
    "H1 s4",
    "GJ s3",
    "G1 s4",
    "H1 fin",
    "AT s2",
    "dw H1",
    "GJ s4",
    "acc H1",
    "acc G2",
    "H2 s3",
    "G1 fin",
    "dw G1",
    "acc G1",
    "GJ fin",
    "AT s3",
    "acc GJ",
    "gin",
    "H2 s4",
    "dw GJ",
    "AT s4",
    "back_x",
    "zi_mid",
    "H2 fin",
    "acc H2",
    "AT fin",
    "dw AT",
    "acc AT",
    "zl_start",
    "dw H2",
    "back_y",
    "zl_mid",
    "gin_out",
    "layer_out",
)


def scratch():
    s = {
        "send": pltpu.SemaphoreType.DMA((N_SEND,)),
        "recv": pltpu.SemaphoreType.DMA((N_RECV,)),
        "local": pltpu.SemaphoreType.DMA((16,)),
        "wqkv": pltpu.VMEM((HEADS, BLK, 3 * HS), BF16),
        "wup": pltpu.VMEM((BLK, 3072), BF16),
        "wout": pltpu.VMEM((768, BLK), BF16),
        "wdown": pltpu.VMEM((3072, BLK), BF16),
        "fg": pltpu.VMEM((4, ZC, TOK), BF16),
        "gg": pltpu.VMEM((4, ZC, TOK), BF16),
        "gw": pltpu.VMEM((TOK, BLK), BF16),
        "normed": pltpu.VMEM((TOK, BLK), BF16),
        "nT": pltpu.VMEM((BLK, TOK), BF16),
        "stx": pltpu.VMEM((4, 2, TOK), F32),
        "sty": pltpu.VMEM((4, 2, TOK), F32),
        "btx": pltpu.VMEM((4, 2, TOK), F32),
        "bty": pltpu.VMEM((4, 2, TOK), F32),
        "btz": pltpu.VMEM((4, 2, TOK), F32),
        "stat": pltpu.VMEM((2, TOK), F32),
        "slope": pltpu.VMEM((OWN, 3072), F32),
        "oacc": pltpu.VMEM((TOK, BLK), F32),
        "gacc": pltpu.VMEM((TOK, BLK), F32),
        "zp": pltpu.VMEM((2, 4, ZC, TOK), BF16),
        "zo": pltpu.VMEM((2, 2, 48, TOK), BF16),
        "zn": pltpu.VMEM((2, 2, ZC, TOK), BF16),
        "sdown": pltpu.VMEM((2, 192, 3072), BF16),
        "sattn": pltpu.VMEM((2, HEADS, 192, HS), BF16),
        "sup": pltpu.VMEM((2, 192, 3072), BF16),
        "sqkv": pltpu.VMEM((2, HEADS, 192, 3 * HS), BF16),
    }
    for name, ca, cb, w, kind in STREAMS:
        for i, item in enumerate(scatter_scratch(ca, cb, w, kind)):
            s[name + str(i)] = item
    for name, ca, cb, w in GATHERS:
        s[name] = pltpu.VMEM((4, 128, ca + cb), BF16)
    for name, shape, kind in (
        ("KVa", (4, 128, 256), BF16),
        ("KVb", (4, 4, 32, 256), BF16),
        ("DKa", (4, 128, 256), BF16),
        ("DKb", (4, 4, 32, 256), BF16),
        ("DKao", (2, 64, 256), BF16),
        ("DKan", (2, 128, 256), BF16),
        ("DKbo", (2, 2, 32, 256), BF16),
        ("DKbn", (2, 4, 32, 256), BF16),
        ("DKm", (4, 32, 256), F32),
        ("DKg", (2, 32, 256), F32),
        ("ja", (128, 3 * HS), F32),
        ("jb", (64, 3 * HS), F32),
    ):
        s[name] = pltpu.VMEM(shape, kind)
    return s


def kernel(names, feat, gout, w_qkv, w_up, w_out, w_down, *rest):
    layer_o, gin_o = rest[:2]
    (own_qkv, got_qkv, own_up, got_up, own_attn, got_attn, own_down, got_down) = rest[2:10]
    s = dict(zip(names, rest[10:]))
    k = Links(s["send"], s["recv"])
    z, core = k.z, k.core
    local = s["local"]
    fg, gg, gw = s["fg"], s["gg"], s["gw"]

    loads = [
        pltpu.make_async_copy(src, dst, local.at[i])
        for i, (src, dst) in enumerate(
            (
                (gout, gg.at[z]),
                (feat, fg.at[z]),
                (w_out, s["wout"]),
                (w_down, s["wdown"]),
                (w_qkv, s["wqkv"]),
                (w_up, s["wup"]),
            )
        )
    ]
    for load in loads:
        load.start()
    k.barrier()

    def wide(buf):
        return buf[...].reshape(BLK, TOK)

    class GatherZ:
        def __init__(self, buf):
            self.rings = [
                RingGather(
                    k, k.zs, k.zd, lambda j, t=t: buf.at[j, :, pl.ds(t, TOK // 2)], *split_rows(48)
                )
                for t in (0, TOK // 2)
            ]

        def start(self):
            for ring in self.rings:
                ring.start()

        def middle(self):
            for ring in self.rings:
                ring.middle()

        def finish(self):
            for ring in self.rings:
                ring.finish()

    R = {}
    for name, ca, cb, w, _ in STREAMS:
        bufs = [s[name + str(i)] for i in range(1, 11)]
        R[name] = Scatter(k, s[name + "0"], bufs, ca, cb, w)
    G = {name: Gather(k, s[name], ca, cb, w) for name, ca, cb, w in GATHERS}
    KV = KeyValue(k, s)
    ops = {}
    held = {}
    for table in (R, G):
        for name, stream in table.items():
            for step in ("s1", "s2", "s3", "s4", "fin"):
                ops[name + " " + step] = getattr(stream, step)
    for step in ("s1", "s2", "s3", "fin", "d1", "d2"):
        ops["KV " + step] = getattr(KV, step)
    every = slice(None)
    oacc, gacc, slope = s["oacc"], s["gacc"], s["slope"]
    zf, zg = GatherZ(fg), GatherZ(gg)

    def op(function):
        ops[function.__name__] = function
        return function

    @op
    def enter():
        loads[0].wait()
        zg.start()
        loads[1].wait()

    ops["zf start"] = zf.start
    ops["zg mid"] = zg.middle
    ops["zf mid"] = zf.middle

    @op
    def clear():
        oacc[...] = jnp.zeros_like(oacc)
        gacc[...] = jnp.zeros_like(gacc)

    @op
    def zf_end():
        zf.finish()
        values = wide(fg).astype(F32)
        packed = row_pack(
            jnp.sum(values, 0, keepdims=True), jnp.sum(values * values, 0, keepdims=True)
        )
        held["ex"] = exchange(k, k.xs, k.xd, s["stx"], packed)

    @op
    def zg_end():
        zg.finish()
        gw[...] = mmt(identity(TOK), wide(gg)).astype(BF16)

    @op
    def stat_y():
        held["ey"] = exchange(k, k.ys, k.yd, s["sty"], collect(held["ex"], s["stx"]))

    @op
    def norm():
        stat = collect(held["ey"], s["sty"])
        average = stat[0:1] / D
        spread = stat[1:2] / D - average * average
        inverse = lax.rsqrt(spread + EPS)
        s["stat"][...] = row_pack(average, inverse)
        s["nT"][...] = ((wide(fg).astype(F32) - average) * inverse).astype(BF16)
        s["normed"][...] = mmt(identity(TOK), s["nT"][...]).astype(BF16)

    def tile_at(base, t):
        return pl.ds(pl.multiple_of(base + t * TILE, TILE), TILE)

    def head_cols(t):
        return pl.ds(pl.multiple_of(t * 3 * HS, 3 * HS), 3 * HS)

    def product(name, fn, n):
        part = s[name + "0"]

        def run():
            def body(t):
                part[:, :, cols(t)] = fn(t).astype(BF16).reshape(4, 128, TILE)

            tiles(n, body)

        ops["M " + name] = run

    def back(base):
        return lambda t: mmt(gw[...], s["wdown"][tile_at(base, t), :])

    def forth(base):
        return lambda t: mm(s["normed"][...], s["wup"][:, tile_at(base, t)])

    product("Ba", lambda t: mmt(gw[...], s["wout"][...]), 1)
    product("Bh1", back(0), 2)
    product("Bh2", back(1536), 2)
    product("Fh1", forth(0), 2)
    product("Fh2", forth(1536), 2)

    def product_query():
        def body(h):
            s["Fq0"][:, :, head_cols(h)] = (
                mm(s["normed"][...], s["wqkv"][h]).astype(BF16).reshape(4, 128, 3 * HS)
            )

        tiles(HEADS, body)

    ops["M Fq"] = product_query
    for i in range(2, 6):
        ops["load " + str(i)] = loads[i].wait

    def activate(stream, gather, base):
        for i, value in enumerate(R[stream].fin()):
            G[gather].put(i, gelu_value(value).astype(BF16))
            at = base + i * G[gather].ca
            slope[:, at : at + value.shape[1]] = gelu_slope(value)

    def deactivate(stream, gather, base):
        for i, value in enumerate(R[stream].fin()):
            at = base + i * G[gather].ca
            G[gather].put(i, (value * slope[:, at : at + value.shape[1]]).astype(BF16))

    ops["act Fh1"] = lambda: activate("Fh1", "H1", 0)
    ops["act Fh2"] = lambda: activate("Fh2", "H2", 1536)
    ops["deact Bh1"] = lambda: deactivate("Bh1", "G1", 0)
    ops["deact Bh2"] = lambda: deactivate("Bh2", "G2", 1536)

    @op
    def project():
        ja, jb = R["Fq"].fin()
        s["ja"][...] = ja
        s["jb"][...] = jb.reshape(64, 3 * HS)
        normal, _ = head_norm(s["ja"][:, HS : 2 * HS])
        s["KVa"][k.y, :, 0:HS] = normal.astype(BF16)
        s["KVa"][k.y, :, HS : 2 * HS] = s["ja"][:, 2 * HS :].astype(BF16)
        normal, _ = head_norm(s["jb"][:, HS : 2 * HS])
        s["KVb"][k.x, KV.mine, :, 0:HS] = normal.astype(BF16).reshape(2, 32, HS)
        s["KVb"][k.x, KV.mine, :, HS : 2 * HS] = (
            s["jb"][:, 2 * HS :].astype(BF16).reshape(2, 32, HS)
        )

    @op
    def attend():
        parts = R["Ba"].fin()
        for i, (kv, dk, own) in enumerate(
            ((s["KVa"], s["DKa"], s["ja"]), (s["KVb"], s["DKb"], s["jb"]))
        ):
            shape = kv.shape[:-1] + (HS,)
            q_norm, q_inv = head_norm(own[:, 0:HS])
            q_b = q_norm.astype(BF16)
            keys = kv[..., 0:HS].reshape(TOK, HS)
            values = kv[..., HS : 2 * HS].reshape(TOK, HS)
            raised = jnp.exp(mmt(q_b, keys) * FACTOR)
            probs = raised / jnp.sum(raised, -1, keepdims=True)
            probs_b = probs.astype(BF16)
            part = parts[i].astype(BF16).reshape(own.shape[0], HS)
            grad_probs = mmt(part, values)
            row_dot = jnp.sum(probs * grad_probs, -1, keepdims=True)
            grad_scores = (probs * (grad_probs - row_dot)).astype(BF16)
            dk[..., 0:HS] = (mtm(grad_scores, q_b) * FACTOR).astype(BF16).reshape(shape)
            dk[..., HS : 2 * HS] = mtm(probs_b, part).astype(BF16).reshape(shape)
            G["AT"].put_head(i, 0, mm(probs_b, values).astype(BF16))
            grad_query = mm(grad_scores, keys) * FACTOR
            G["GJ"].put_head(i, 0, head_norm_back(grad_query, q_norm, q_inv).astype(BF16))

    def key_value_back(i, own, value):
        k_norm, k_inv = head_norm(own[:, HS : 2 * HS])
        G["GJ"].put_head(i, HS, head_norm_back(value[:, 0:HS], k_norm, k_inv).astype(BF16))
        G["GJ"].put_head(i, 2 * HS, value[:, HS:].astype(BF16))

    ops["KV d3"] = lambda: key_value_back(0, s["ja"], KV.d3())
    ops["KV d4"] = lambda: key_value_back(1, s["jb"], KV.d4().reshape(64, 2 * HS))

    copies = []
    shares = []

    def share(stage, own_out, got_out, index):
        slot = 6 + len(copies)
        mine = pltpu.make_async_copy(stage.at[core, *index], own_out.at[index], local.at[slot])
        mine.start()
        copies.append(mine)
        shares.append(k.send(stage.at[1 - core, *index], got_out.at[index], k.cd))

    def rows_tile(name, t):
        return s[name][:, :, cols(t)].reshape(TOK, TILE)

    def per_tile(name, body, n):
        ops[name] = lambda: tiles(n, body)

    def with_hidden(name, base):
        def total(t):
            oacc[...] += mm(rows_tile(name, t), s["wdown"][tile_at(base, t), :])

        def weights(t):
            both = mm(wide(gg), rows_tile(name, t)).astype(BF16)
            s["sdown"][0, :, tile_at(base, t)] = both[0:192]
            s["sdown"][1, :, tile_at(base, t)] = both[192:384]

        def run():
            tiles(2, weights)
            share(s["sdown"], own_down, got_down, (every, pl.ds(base, 1536)))

        per_tile("acc " + name, total, 2)
        ops["dw " + name] = run

    def with_grads(name, base):
        def total(t):
            gacc[...] += mmt(rows_tile(name, t), s["wup"][:, tile_at(base, t)])

        def weights(t):
            both = mm(s["nT"][...], rows_tile(name, t)).astype(BF16)
            s["sup"][0, :, tile_at(base, t)] = both[0:192]
            s["sup"][1, :, tile_at(base, t)] = both[192:384]

        def run():
            tiles(2, weights)
            share(s["sup"], own_up, got_up, (every, pl.ds(base, 1536)))

        per_tile("acc " + name, total, 2)
        ops["dw " + name] = run

    with_hidden("H1", 0)
    with_hidden("H2", 1536)
    with_grads("G1", 0)
    with_grads("G2", 1536)

    def total_attended(t):
        oacc[...] += mm(rows_tile("AT", 0), s["wout"][...])

    def total_joined(h):
        gacc[...] += mmt(s["GJ"][:, :, head_cols(h)].reshape(TOK, 3 * HS), s["wqkv"][h])

    per_tile("acc AT", total_attended, 1)
    per_tile("acc GJ", total_joined, HEADS)

    def weights_attended():
        both = mm(wide(gg), rows_tile("AT", 0)).astype(BF16)
        for c in range(2):
            for h in range(HEADS):
                s["sattn"][c, h] = both[c * 192 : (c + 1) * 192, h * HS : (h + 1) * HS]
        share(s["sattn"], own_attn, got_attn, (every, every, every))

    ops["dw AT"] = weights_attended

    def zscatter(i, total):
        part = s["zp"].at[i]
        turned = mmt(identity(BLK), total.astype(BF16))
        part[...] = turned.astype(BF16).reshape(4, ZC, TOK)
        ring = RingSum(
            k, k.zs, k.zd, lambda j: part.at[j], *split_rows(48), s["zo"].at[i], s["zn"].at[i]
        )
        return ring, turned

    @op
    def gin():
        average, inverse = s["stat"][0:1], s["stat"][1:2]
        held["zi"], turned = zscatter(1, gacc[...])
        held["zi"].start()
        normal = (wide(fg).astype(F32) - average) * inverse
        packed = row_pack(
            jnp.sum(turned, 0, keepdims=True), jnp.sum(turned * normal, 0, keepdims=True)
        )
        held["bz"] = exchange(k, k.zs, k.zd, s["btz"], packed)

    def weights_joined():
        def body(h):
            block = s["GJ"][:, :, head_cols(h)].reshape(TOK, 3 * HS)
            both = mm(s["nT"][...], block).astype(BF16)
            s["sqkv"][0, h] = both[0:192]
            s["sqkv"][1, h] = both[192:384]

        tiles(HEADS, body)
        share(s["sqkv"], own_qkv, got_qkv, (every, every, every))

    ops["dw GJ"] = weights_joined

    @op
    def zi_mid():
        held["zi"].middle()

    @op
    def back_x():
        held["bx"] = exchange(k, k.xs, k.xd, s["btx"], collect(held["bz"], s["btz"]))

    @op
    def back_y():
        held["by"] = exchange(k, k.ys, k.yd, s["bty"], collect(held["bx"], s["btx"]))

    @op
    def gin_out():
        average, inverse = s["stat"][0:1], s["stat"][1:2]
        summed = held["zi"].total()
        sums = collect(held["by"], s["bty"])
        normal_own = (fg[z].astype(F32) - average) * inverse
        correction = summed - sums[0:1] / D - normal_own * (sums[1:2] / D)
        gin_o[...] = (gg[z].astype(F32) + inverse * correction).astype(BF16)

    @op
    def zl_start():
        held["zl"], _ = zscatter(0, oacc[...])
        held["zl"].start()

    @op
    def zl_mid():
        held["zl"].middle()

    @op
    def layer_out():
        layer_o[...] = (fg[z].astype(F32) + held["zl"].total()).astype(BF16)

    for i, name in enumerate(ORDER):
        ops[name]()
        k.settle(i)

    for copy in copies:
        copy.wait()
    for copy in shares:
        copy.wait_recv()
    k.settle(len(ORDER) + SETTLE)


def on_device(features, w_qkv, w_up, w_out, w_down, grad_out):
    out_flat = w_out.reshape(768, BLK)
    shapes = scratch()
    any_spec = pl.BlockSpec(memory_space=pl.ANY)
    vmem_spec = pl.BlockSpec(memory_space=pltpu.VMEM)

    def pair(*shape):
        return [jax.ShapeDtypeStruct(shape, BF16)] * 2

    names = tuple(shapes)
    outs = pl.pallas_call(
        lambda *refs: kernel(names, *refs),
        out_shape=pair(ZC, TOK)
        + pair(HEADS, 192, 3 * HS)
        + pair(192, 3072)
        + pair(HEADS, 192, HS)
        + pair(192, 3072),
        in_specs=[any_spec] * 6,
        out_specs=[vmem_spec] * 2 + [any_spec] * 8,
        scratch_shapes=list(shapes.values()),
        compiler_params=pltpu.CompilerParams(
            collective_id=0, has_side_effects=True, vmem_limit_bytes=60 * 1024 * 1024
        ),
        cost_estimate=pl.CostEstimate(
            flops=11_000_000_000, bytes_accessed=20_000_000, transcendentals=1_000_000
        ),
    )(features.T, grad_out.T, w_qkv.transpose(1, 0, 2), w_up, out_flat, w_down)

    layer_out, grad_in, *grads = finish(outs)
    grad_qkv, grad_up, grad_attn, grad_down = grads
    return (
        layer_out.T,
        grad_in.T,
        grad_qkv.transpose(1, 0, 2),
        grad_up,
        grad_attn.transpose(0, 2, 1),
        grad_down.T,
    )


PIECES = 3


def add_halves(*refs):
    ins, outs, scr = refs[:10], refs[10:16], refs[16:]
    own, got, total, sem = scr[0:4], scr[4:8], scr[8:12], scr[12]
    reads, writes = [], []

    def piece(i, ref, p):
        if ref.shape[0] == HEADS:
            return ref.at[pl.ds(p * HEADS // PIECES, HEADS // PIECES)]
        return ref.at[pl.ds(p * 192 // PIECES, 192 // PIECES)]

    def move(src, dst):
        copy = pltpu.make_async_copy(src, dst, sem.at[len(reads) + len(writes)])
        copy.start()
        return copy

    for i in range(4):
        for p in range(PIECES):
            for j, into in enumerate((own, got)):
                reads.append(move(piece(i, ins[2 + 2 * i + j], p), piece(i, into[i], p)))
    for i in range(2):
        reads.append(move(ins[i], scr[13 + i]))
    turn = iter(reads)
    for i in range(4):
        for p in range(PIECES):
            next(turn).wait()
            next(turn).wait()
            into = piece(i, total[i], p)
            into[...] = piece(i, own[i], p)[...].astype(F32) + piece(i, got[i], p)[...].astype(F32)
            writes.append(move(into, piece(i, outs[2 + i], p)))
    for i in range(2):
        next(turn).wait()
        writes.append(move(scr[13 + i], outs[i]))
    for copy in writes:
        copy.wait()


def finish(arrays):
    grads = arrays[2::2]
    any_spec = pl.BlockSpec(memory_space=pl.ANY)
    return pl.pallas_call(
        add_halves,
        out_shape=[jax.ShapeDtypeStruct((ZC, TOK), BF16)] * 2
        + [jax.ShapeDtypeStruct(array.shape, F32) for array in grads],
        in_specs=[any_spec] * 10,
        out_specs=[any_spec] * 6,
        scratch_shapes=[pltpu.VMEM(array.shape, BF16) for array in grads] * 2
        + [pltpu.VMEM(array.shape, F32) for array in grads]
        + [pltpu.SemaphoreType.DMA((64,))]
        + [pltpu.VMEM((ZC, TOK), BF16)] * 2,
        compiler_params=pltpu.CompilerParams(vmem_limit_bytes=60 * 1024 * 1024),
        cost_estimate=pl.CostEstimate(
            flops=2_000_000, bytes_accessed=14_500_000, transcendentals=0
        ),
    )(*arrays)


def solution(mesh):
    in_specs = (
        P("dp", ("mx", "my")),
        P("mx", "my", None),
        P("mx", "my"),
        P("my", None, "mx"),
        P("my", "mx"),
        P("dp", ("mx", "my")),
    )
    out_specs = (
        P("dp", ("mx", "my")),
        P("dp", ("mx", "my")),
        P(("mx", "dp"), "my", None),
        P(("mx", "dp"), "my"),
        P("my", None, ("mx", "dp")),
        P("my", ("mx", "dp")),
    )
    return jax.shard_map(
        on_device, mesh=mesh, in_specs=in_specs, out_specs=out_specs, check_vma=False
    )
```

```python
import math

import jax
import jax.numpy as jnp
from jax import lax
from jax.experimental import pallas as pl
from jax.experimental.pallas import tpu as pltpu
from jax.sharding import PartitionSpec as P

D = 6144
EPS = 1e-06
F32 = jnp.float32
BF16 = jnp.bfloat16
MESH = pl.DeviceIdType.MESH
HEADS = 6
HS = 128
TOK = 512
OWN = 32
BLK = 384
ZC = 96
FACTOR = 1.0 / math.sqrt(HS)
N_SEND = 48
N_RECV = 88
TILE = 768
SETTLE = 8


def mm(a, b):
    return lax.dot_general(a, b, (((1,), (0,)), ((), ())), preferred_element_type=F32)


def mmt(a, b):
    return lax.dot_general(a, b, (((1,), (1,)), ((), ())), preferred_element_type=F32)


def mtm(a, b):
    return lax.dot_general(a, b, (((0,), (0,)), ((), ())), preferred_element_type=F32)


def gelu_value(values):
    return 0.5 * values * (1.0 + lax.erf(values / math.sqrt(2.0)))


def gelu_slope(values):
    return 0.5 * (1.0 + lax.erf(values / math.sqrt(2.0))) + values * jnp.exp(
        -0.5 * values * values
    ) / math.sqrt(2.0 * math.pi)


def head_norm(values):
    average = jnp.mean(values, -1, keepdims=True)
    spread = jnp.mean(values * values, -1, keepdims=True) - average * average
    inverse = lax.rsqrt(spread + EPS)
    return ((values - average) * inverse, inverse)


def head_norm_back(gradient, normal, inverse):
    first_mean = jnp.mean(gradient, -1, keepdims=True)
    second_mean = jnp.mean(gradient * normal, -1, keepdims=True)
    return inverse * (gradient - first_mean - normal * second_mean)


def identity(n):
    row = lax.broadcasted_iota(jnp.int32, (n, n), 0)
    column = lax.broadcasted_iota(jnp.int32, (n, n), 1)
    return jnp.where(row == column, 1.0, 0.0).astype(BF16)


def add_to(ref, more):
    ref[...] = (ref[...].astype(F32) + more[...].astype(F32)).astype(ref.dtype)


class Message:
    def __init__(self, links, copy, way, sems):
        self.links, self.copy, self.way, self.sems = links, copy, way, sems
        self.began, self.arrived = links.tick(), None

    def wait_recv(self):
        self.copy.wait_recv()
        self.arrived = self.links.tick()


class Links:
    def __init__(self, send, recv):
        self.send_sems, self.recv_sems = send, recv
        self.log, self.started, self.clock, self.turn = [], [], 0, 0
        self.free_send, self.used_send, self.last_on = [], 0, []
        mx = lax.axis_index("mx")
        self.x, self.y = lax.rem(mx, 4), lax.div(mx, 4)
        self.z, self.core = lax.axis_index("my"), lax.axis_index("dp")
        x, y, z = self.x, self.y, self.z
        self.xs = [lax.rem(x + i, 4) for i in range(4)]
        self.ys = [lax.rem(y + i, 4) for i in range(4)]
        self.zs = [lax.rem(z + i, 4) for i in range(4)]
        self.xd = [{"mx": y * 4 + v, "way": ("x", i)} for i, v in enumerate(self.xs)]
        self.yd = [{"mx": v * 4 + x, "way": ("y", i)} for i, v in enumerate(self.ys)]
        self.zd = [{"my": v, "way": ("z", i)} for i, v in enumerate(self.zs)]
        self.cd = {"dp": 1 - self.core, "way": ("core", 0)}

    def tick(self):
        self.clock += 1
        return self.clock

    def ready(self, last, way):
        if last.arrived is None:
            return False
        back = (way[0], (4 - way[1]) % 4)
        return any(
            m.way == back and m.began > last.arrived and m.arrived is not None for m in self.log
        )

    def take_recv(self, way):
        for i, last in enumerate(self.last_on):
            if self.ready(last, way):
                return i
        self.last_on.append(None)
        return len(self.last_on) - 1

    def send(self, src, dst, device):
        way = device["way"]
        to = {axis: v for axis, v in device.items() if axis != "way"}
        if self.free_send:
            i = self.free_send.pop(0)
        else:
            i = self.used_send
            self.used_send += 1
        j = self.take_recv(way)
        copy = pltpu.make_async_remote_copy(
            src_ref=src,
            dst_ref=dst,
            send_sem=self.send_sems.at[i],
            recv_sem=self.recv_sems.at[j],
            device_id=to,
            device_id_type=MESH,
        )
        copy.start()
        message = Message(self, copy, way, (i, j))
        self.last_on[j] = message
        self.log.append(message)
        self.started.append((self.turn, message))
        return message

    def settle(self, turn):
        self.turn = turn + 1
        while self.started and self.started[0][0] <= turn - SETTLE:
            message = self.started.pop(0)[1]
            message.copy.wait_send()
            self.free_send.append(message.sems[0])

    def barrier(self):
        sem = pltpu.get_barrier_semaphore()
        peers = self.xd[1:] + self.yd[1:] + self.zd[1:] + [self.cd]
        for peer in peers:
            peer = {axis: v for axis, v in peer.items() if axis != "way"}
            pl.semaphore_signal(sem, inc=1, device_id=peer, device_id_type=MESH)
        pl.semaphore_wait(sem, len(peers))


def rows_of(start, size):
    return pl.ds(pl.multiple_of(start, 16), size)


class RingSum:
    def __init__(self, links, ring, devices, chunk, first, second, opp, near, exact=None):
        self.k, self.ring, self.dev = links, ring, devices
        self.chunk, self.first, self.second, self.opp, self.near = chunk, first, second, opp, near
        self.exact = exact or chunk

    def start(self):
        far, left, right = (self.chunk(self.ring[i]) for i in (2, 3, 1))
        to_left, to_right = self.near.at[1], self.near.at[0]
        self.far_left = self.k.send(self.first(far), self.opp.at[1], self.dev[3])
        self.far_right = self.k.send(self.second(far), self.opp.at[0], self.dev[1])
        self.near_copies = [
            self.k.send(self.second(left), self.second(to_left), self.dev[3]),
            self.k.send(self.first(right), self.first(to_right), self.dev[1]),
        ]

    def relay(self, side, half, slot, arrived):
        j = self.ring[side]
        part = half(self.chunk(j))
        arrived.wait_recv()
        total = half(self.exact(j))[...].astype(F32) + self.opp[slot].astype(F32)
        part[...] = total.astype(part.dtype)
        self.near_copies.append(self.k.send(part, half(self.near.at[slot]), self.dev[side]))

    def middle(self):
        self.relay(3, self.first, 1, self.far_left)
        self.relay(1, self.second, 0, self.far_right)

    def total(self):
        for copy in self.near_copies:
            copy.wait_recv()
        own = self.exact(self.ring[0])
        return own[...].astype(F32) + self.near[0].astype(F32) + self.near[1].astype(F32)


class RingGather:
    def __init__(self, links, ring, devices, chunk, first, second):
        self.k, self.ring, self.dev = links, ring, devices
        self.chunk, self.first, self.second = chunk, first, second

    def start(self):
        own = self.chunk(self.ring[0])
        self.to_left = self.k.send(own, own, self.dev[3])
        self.to_right = self.k.send(own, own, self.dev[1])

    def middle(self):
        self.to_right.wait_recv()
        part = self.first(self.chunk(self.ring[3]))
        self.on_right = self.k.send(part, part, self.dev[1])
        self.to_left.wait_recv()
        part = self.second(self.chunk(self.ring[1]))
        self.on_left = self.k.send(part, part, self.dev[3])

    def finish(self):
        self.on_right.wait_recv()
        self.on_left.wait_recv()


def split_rows(n):
    return (lambda r: r.at[pl.ds(0, n)]), (lambda r: r.at[pl.ds(n, n)])


class Scatter:
    def __init__(self, links, part, bufs, ca, cb, w):
        k = links
        a, b = pl.ds(0, ca), pl.ds(ca, cb)
        a1o, a1n, b1o, b1n, a2, b2, a2o, a2n, b2o, b2n, *whole = bufs
        part_x, a2_x, b2_x = whole or (part, a2, b2)
        self.mids = ((a2, a2_x), (b2, b2_x))
        if w:

            def a2_chunk(ref):
                return lambda j: ref.at[:, part_of(j, w)]

            def b2_chunk(ref):
                return lambda j: ref.at[pl.ds(lax.rem(j, 2) * 2, 2), :, part_of(lax.div(j, 2), w)]

            a2_split, b2_split = split_rows(64), split_rows(1)
        else:

            def a2_chunk(ref):
                return lambda j: ref.at[rows_of(j * 32, 32), :]

            def b2_chunk(ref):
                return lambda j: ref.at[j]

            a2_split = b2_split = split_rows(16)

        def a1_chunk(ref):
            return lambda j: ref.at[j, :, a]

        def b1_chunk(ref):
            return lambda j: ref.at[:, rows_of(j * 32, 32), b]

        def ring(axis, devices, chunk, split, opp, near, ref, ref_x):
            return RingSum(k, axis, devices, chunk(ref), *split, opp, near, chunk(ref_x))

        self.a1 = ring(k.ys, k.yd, a1_chunk, split_rows(64), a1o, a1n, part, part_x)
        self.b1 = ring(k.xs, k.xd, b1_chunk, split_rows(2), b1o, b1n, part, part_x)
        self.a2 = ring(k.xs, k.xd, a2_chunk, a2_split, a2o, a2n, a2, a2_x)
        self.b2 = ring(k.ys, k.yd, b2_chunk, b2_split, b2o, b2n, b2, b2_x)

    def s1(self):
        self.a1.start()
        self.b1.start()

    def s2(self):
        self.a1.middle()
        self.b1.middle()

    def s3(self):
        for before, after, mids in zip((self.a1, self.b1), (self.a2, self.b2), self.mids):
            total = before.total()
            for mid in mids:
                mid[...] = total.astype(mid.dtype)
            after.start()

    def s4(self):
        self.a2.middle()
        self.b2.middle()

    def fin(self):
        return self.a2.total(), self.b2.total()


def part_of(j, w):
    return pl.ds(pl.multiple_of(j * w, 128), w)


def scatter_scratch(ca, cb, w, exact):
    found = [
        pltpu.VMEM((4, 128, ca + cb), BF16),
        pltpu.VMEM((2, 64, ca), BF16),
        pltpu.VMEM((2, 128, ca), BF16),
        pltpu.VMEM((2, 2, 32, cb), BF16),
        pltpu.VMEM((2, 4, 32, cb), BF16),
        pltpu.VMEM((128, ca), BF16),
        pltpu.VMEM((4, 32, cb), BF16),
    ]
    if w:
        found += [
            pltpu.VMEM((2, 64, w), BF16),
            pltpu.VMEM((2, 128, w), BF16),
            pltpu.VMEM((2, 1, 32, w), BF16),
            pltpu.VMEM((2, 2, 32, w), BF16),
        ]
    else:
        found += [
            pltpu.VMEM((2, 16, ca), BF16),
            pltpu.VMEM((2, 32, ca), BF16),
            pltpu.VMEM((2, 16, cb), BF16),
            pltpu.VMEM((2, 32, cb), BF16),
        ]
    if exact:
        found += [
            pltpu.VMEM((4, 128, ca + cb), F32),
            pltpu.VMEM((128, ca), F32),
            pltpu.VMEM((4, 32, cb), F32),
        ]
    return found


class Gather:
    def __init__(self, links, full, ca, cb, w):
        k = links
        a, b = pl.ds(0, ca), pl.ds(ca, cb)
        x, y = k.x, k.y
        self.full, self.ca, self.w, self.k = full, ca, w, k
        if w:
            a1_chunk, a1_split = (lambda j: full.at[y, :, part_of(j, w)]), split_rows(64)
            b1_chunk, b1_split = (
                lambda j: full.at[
                    pl.ds(lax.rem(j, 2) * 2, 2),
                    rows_of(x * 32, 32),
                    part_of(4 + lax.div(j, 2), w),
                ]
            ), split_rows(1)
        else:
            a1_chunk, a1_split = (lambda j: full.at[y, rows_of(j * 32, 32), a]), split_rows(16)
            b1_chunk, b1_split = (lambda j: full.at[j, rows_of(x * 32, 32), b]), split_rows(16)
        self.a1 = RingGather(k, k.xs, k.xd, a1_chunk, *a1_split)
        self.b1 = RingGather(k, k.ys, k.yd, b1_chunk, *b1_split)
        self.a2 = RingGather(k, k.ys, k.yd, lambda j: full.at[j, :, a], *split_rows(64))
        self.b2 = RingGather(
            k, k.xs, k.xd, lambda j: full.at[:, rows_of(j * 32, 32), b], *split_rows(2)
        )

    def put(self, i, value):
        at = pl.ds(0, self.ca) if i == 0 else pl.ds(self.ca, value.shape[1])
        self.full[self.k.y, rows_of(self.k.x * 32, 32), at] = value

    def put_head(self, i, start, value):
        x, y, n = self.k.x, self.k.y, value.shape[1]
        if i == 0:
            self.full[y, :, pl.ds(pl.multiple_of(x * self.w + start, 128), n)] = value
        else:
            at = pl.ds(pl.multiple_of((4 + lax.div(y, 2)) * self.w + start, 128), n)
            half = pl.ds(lax.rem(y, 2) * 2, 2)
            self.full[half, rows_of(x * 32, 32), at] = value.reshape(2, 32, n)

    def s1(self):
        self.a1.start()
        self.b1.start()

    def s2(self):
        self.a1.middle()
        self.b1.middle()

    def s3(self):
        self.a1.finish()
        self.a2.start()
        self.b1.finish()
        self.b2.start()

    def s4(self):
        self.a2.middle()
        self.b2.middle()

    def fin(self):
        self.a2.finish()
        self.b2.finish()


class KeyValue:
    def __init__(self, links, s):
        k = links
        x, y = k.x, k.y
        self.k = k
        a, b, da, db = s["KVa"], s["KVb"], s["DKa"], s["DKb"]
        self.a, self.b, self.da, self.db, self.mid, self.got = a, b, da, db, s["DKm"], s["DKg"]
        self.mine = pl.ds(lax.rem(y, 2) * 2, 2)
        self.other = pl.ds(2 - lax.rem(y, 2) * 2, 2)
        self.mate = {"mx": (y + 1 - 2 * lax.rem(y, 2)) * 4 + x, "way": ("mate", 0)}
        self.ga = RingGather(k, k.ys, k.yd, lambda j: a.at[j], *split_rows(64))
        self.gb = RingGather(k, k.xs, k.xd, lambda j: b.at[j], *split_rows(2))
        self.ra = RingSum(
            k,
            k.ys,
            k.yd,
            lambda j: da.at[j],
            *split_rows(64),
            s["DKao"],
            s["DKan"],
            lambda j: s["DKax"].at[j],
        )
        self.rb = RingSum(
            k,
            k.xs,
            k.xd,
            lambda j: db.at[j],
            *split_rows(2),
            s["DKbo"],
            s["DKbn"],
            lambda j: s["DKbx"].at[j],
        )

    def s1(self):
        own = self.b.at[self.k.x, self.mine]
        self.pair = self.k.send(own, own, self.mate)
        self.ga.start()

    def s2(self):
        self.pair.wait_recv()
        self.gb.start()
        self.ga.middle()

    def s3(self):
        self.gb.middle()

    def fin(self):
        self.ga.finish()
        self.gb.finish()

    def d1(self):
        self.rb.start()
        self.ra.start()

    def d2(self):
        self.rb.middle()
        self.ra.middle()

    def d3(self):
        self.mid[...] = self.rb.total()
        self.back = self.k.send(self.mid.at[self.other], self.got, self.mate)
        return self.ra.total()

    def d4(self):
        self.back.wait_recv()
        return self.mid[self.mine] + self.got[...]


def tiles(n, body):
    if n == 1:
        body(0)
    else:
        pl.loop(0, n)(body)


def cols(t):
    return pl.ds(pl.multiple_of(t * TILE, TILE), TILE)


def exchange(links, ring, devices, buf, value):
    me = ring[0]
    buf[me] = value
    return [links.send(buf.at[me], buf.at[me], devices[i]) for i in (1, 2, 3)]


def collect(copies, buf):
    for copy in copies:
        copy.wait_recv()
    return (buf[0] + buf[1]) + (buf[2] + buf[3])


def row_pack(first, second):
    row = lax.broadcasted_iota(jnp.int32, (2, TOK), 0)
    return jnp.where(row == 0, first, second)


STREAMS = (
    ("Ba", 512, 256, HS, True),
    ("Bh1", 640, 896, 0, False),
    ("Bh2", 640, 896, 0, False),
    ("Fq", 1536, 768, 3 * HS, True),
    ("Fh1", 640, 896, 0, False),
    ("Fh2", 640, 896, 0, False),
)
GATHERS = (
    ("H1", 640, 896, 0),
    ("H2", 640, 896, 0),
    ("G1", 640, 896, 0),
    ("G2", 640, 896, 0),
    ("AT", 512, 256, HS),
    ("GJ", 1536, 768, 3 * HS),
)


ORDER = (
    "enter",
    "zg mid",
    "zf start",
    "zg_end",
    "load 2",
    "M Ba",
    "Ba s1",
    "load 3",
    "M Bh2",
    "Bh2 s1",
    "zf mid",
    "zf_end",
    "Bh2 s2",
    "Ba s2",
    "M Bh1",
    "stat_y",
    "Bh1 s1",
    "Bh2 s3",
    "norm",
    "load 5",
    "M Fh2",
    "Fh2 s1",
    "M Fh1",
    "load 4",
    "M Fq",
    "Fq s1",
    "Fq s2",
    "Ba s3",
    "Fh2 s2",
    "Bh1 s2",
    "Ba s4",
    "Fq s3",
    "clear",
    "Fh2 s3",
    "Fq s4",
    "Bh2 s4",
    "Fh2 s4",
    "Fh1 s1",
    "project",
    "KV s1",
    "act Fh2",
    "Fh1 s2",
    "deact Bh2",
    "G2 s1",
    "Bh1 s3",
    "KV s2",
    "Fh1 s3",
    "G2 s2",
    "KV s3",
    "Bh1 s4",
    "H2 s1",
    "Fh1 s4",
    "KV fin",
    "G2 s3",
    "attend",
    "H2 s2",
    "KV d1",
    "AT s1",
    "act Fh1",
    "H1 s1",
    "KV d2",
    "G2 s4",
    "deact Bh1",
    "KV d3",
    "G1 s1",
    "AT s2",
    "H1 s2",
    "KV d4",
    "GJ s1",
    "G2 fin",
    "G1 s2",
    "H2 s3",
    "GJ s2",
    "dw G2",
    "G1 s3",
    "H2 s4",
    "GJ s3",
    "G1 s4",
    "GJ s4",
    "H2 fin",
    "H1 s3",
    "AT s3",
    "acc H2",
    "G1 fin",
    "dw G1",
    "dw H2",
    "acc G1",
    "GJ fin",
    "acc G2",
    "acc GJ",
    "gin",
    "H1 s4",
    "dw GJ",
    "sum G1",
    "AT s4",
    "zi_mid",
    "sum G2",
    "back_x",
    "H1 fin",
    "dw H1",
    "acc H1",
    "AT fin",
    "acc AT",
    "zl_start",
    "sum H2",
    "dw AT",
    "back_y",
    "zl_mid",
    "sum H1",
    "sum GJ",
    "gin_out",
    "sum AT",
    "layer_out",
)


def scratch():
    s = {
        "send": pltpu.SemaphoreType.DMA((N_SEND,)),
        "recv": pltpu.SemaphoreType.DMA((N_RECV,)),
        "local": pltpu.SemaphoreType.DMA((16,)),
        "wqkv": pltpu.VMEM((HEADS, BLK, 3 * HS), BF16),
        "wup": pltpu.VMEM((BLK, 3072), BF16),
        "wout": pltpu.VMEM((768, BLK), BF16),
        "wdown": pltpu.VMEM((3072, BLK), BF16),
        "fg": pltpu.VMEM((4, ZC, TOK), BF16),
        "gg": pltpu.VMEM((4, ZC, TOK), BF16),
        "gw": pltpu.VMEM((TOK, BLK), BF16),
        "normed": pltpu.VMEM((TOK, BLK), BF16),
        "nT": pltpu.VMEM((BLK, TOK), BF16),
        "stx": pltpu.VMEM((4, 2, TOK), F32),
        "sty": pltpu.VMEM((4, 2, TOK), F32),
        "btx": pltpu.VMEM((4, 2, TOK), F32),
        "bty": pltpu.VMEM((4, 2, TOK), F32),
        "btz": pltpu.VMEM((4, 2, TOK), F32),
        "stat": pltpu.VMEM((2, TOK), F32),
        "slope": pltpu.VMEM((OWN, 3072), F32),
        "zp": pltpu.VMEM((2, 4, ZC, TOK), BF16),
        "zo": pltpu.VMEM((2, 2, 48, TOK), BF16),
        "zn": pltpu.VMEM((2, 2, ZC, TOK), BF16),
        "sattn": pltpu.VMEM((2, HEADS, 192, HS), BF16),
        "sqkv": pltpu.VMEM((2, HEADS, 192, 3 * HS), BF16),
        "gotdown": pltpu.VMEM((2, 96, 3072), BF16),
        "gotattn": pltpu.VMEM((HEADS, 192, HS), BF16),
        "gotup": pltpu.VMEM((2, 96, 3072), BF16),
        "gotqkv": pltpu.VMEM((HEADS, 192, 3 * HS), BF16),
    }
    for name, ca, cb, w, exact in STREAMS:
        for i, item in enumerate(scatter_scratch(ca, cb, w, exact)):
            s[name + str(i)] = item
    for name, ca, cb, w in GATHERS:
        s[name] = pltpu.VMEM((4, 128, ca + cb), BF16)
    for name, shape, kind in (
        ("KVa", (4, 128, 256), BF16),
        ("KVb", (4, 4, 32, 256), BF16),
        ("DKa", (4, 128, 256), BF16),
        ("DKb", (4, 4, 32, 256), BF16),
        ("DKao", (2, 64, 256), BF16),
        ("DKan", (2, 128, 256), BF16),
        ("DKbo", (2, 2, 32, 256), BF16),
        ("DKbn", (2, 4, 32, 256), BF16),
        ("DKax", (4, 128, 256), F32),
        ("DKbx", (4, 4, 32, 256), F32),
        ("DKm", (4, 32, 256), F32),
        ("DKg", (2, 32, 256), F32),
        ("ja", (128, 3 * HS), F32),
        ("jb", (64, 3 * HS), F32),
    ):
        s[name] = pltpu.VMEM(shape, kind)
    return s


def kernel(names, feat, gout, w_qkv, w_up, w_out, w_down, *rest):
    layer_o, gin_o = rest[:2]
    sum_qkv, sum_up, sum_attn, sum_down = rest[2:6]
    s = dict(zip(names, rest[6:]))
    k = Links(s["send"], s["recv"])
    z, core = k.z, k.core
    local = s["local"]
    fg, gg, gw = s["fg"], s["gg"], s["gw"]

    loads = [
        pltpu.make_async_copy(src, dst, local.at[i])
        for i, (src, dst) in enumerate(
            (
                (gout, gg.at[z]),
                (feat, fg.at[z]),
                (w_out, s["wout"]),
                (w_down, s["wdown"]),
                (w_qkv, s["wqkv"]),
                (w_up, s["wup"]),
            )
        )
    ]
    for load in loads:
        load.start()
    k.barrier()

    def wide(buf):
        return buf[...].reshape(BLK, TOK)

    class GatherZ:
        def __init__(self, buf):
            self.rings = [
                RingGather(
                    k, k.zs, k.zd, lambda j, t=t: buf.at[j, :, pl.ds(t, TOK // 2)], *split_rows(48)
                )
                for t in (0, TOK // 2)
            ]

        def start(self):
            for ring in self.rings:
                ring.start()

        def middle(self):
            for ring in self.rings:
                ring.middle()

        def finish(self):
            for ring in self.rings:
                ring.finish()

    R = {}
    for name, ca, cb, w, exact in STREAMS:
        bufs = [s[name + str(i)] for i in range(1, 14 if exact else 11)]
        R[name] = Scatter(k, s[name + "0"], bufs, ca, cb, w)
    G = {name: Gather(k, s[name], ca, cb, w) for name, ca, cb, w in GATHERS}
    KV = KeyValue(k, s)
    ops = {}
    held = {}
    for table in (R, G):
        for name, stream in table.items():
            for step in ("s1", "s2", "s3", "s4", "fin"):
                ops[name + " " + step] = getattr(stream, step)
    for step in ("s1", "s2", "s3", "fin", "d1", "d2"):
        ops["KV " + step] = getattr(KV, step)
    slope = s["slope"]
    oacc, gacc = (s["Fq11"].at[:, :, pl.ds(i * BLK, BLK)] for i in range(2))

    def add_rows(ref, value):
        ref[...] += value.reshape(4, 128, BLK)

    zf, zg = GatherZ(fg), GatherZ(gg)

    def op(function):
        ops[function.__name__] = function
        return function

    @op
    def enter():
        loads[0].wait()
        zg.start()
        loads[1].wait()

    ops["zf start"] = zf.start
    ops["zg mid"] = zg.middle
    ops["zf mid"] = zf.middle

    @op
    def clear():
        for ref in (oacc, gacc):
            ref[...] = jnp.zeros(ref.shape, F32)

    @op
    def zf_end():
        zf.finish()
        values = wide(fg).astype(F32)
        packed = row_pack(
            jnp.sum(values, 0, keepdims=True), jnp.sum(values * values, 0, keepdims=True)
        )
        held["ex"] = exchange(k, k.xs, k.xd, s["stx"], packed)

    @op
    def zg_end():
        zg.finish()
        gw[...] = mmt(identity(TOK), wide(gg)).astype(BF16)

    @op
    def stat_y():
        held["ey"] = exchange(k, k.ys, k.yd, s["sty"], collect(held["ex"], s["stx"]))

    @op
    def norm():
        stat = collect(held["ey"], s["sty"])
        average = stat[0:1] / D
        spread = stat[1:2] / D - average * average
        inverse = lax.rsqrt(spread + EPS)
        s["stat"][...] = row_pack(average, inverse)
        s["nT"][...] = ((wide(fg).astype(F32) - average) * inverse).astype(BF16)
        s["normed"][...] = mmt(identity(TOK), s["nT"][...]).astype(BF16)

    def tile_at(base, t):
        return pl.ds(pl.multiple_of(base + t * TILE, TILE), TILE)

    def head_cols(t):
        return pl.ds(pl.multiple_of(t * 3 * HS, 3 * HS), 3 * HS)

    def store(name, at, value, n):
        s[name + "0"][:, :, at] = value.astype(BF16).reshape(4, 128, n)
        if name + "11" in s:
            s[name + "11"][:, :, at] = value.reshape(4, 128, n)

    def product(name, fn, n):
        def run():
            def body(t):
                store(name, cols(t), fn(t), TILE)

            tiles(n, body)

        ops["M " + name] = run

    def back(base):
        return lambda t: mmt(gw[...], s["wdown"][tile_at(base, t), :])

    def forth(base):
        return lambda t: mm(s["normed"][...], s["wup"][:, tile_at(base, t)])

    product("Ba", lambda t: mmt(gw[...], s["wout"][...]), 1)
    product("Bh1", back(0), 2)
    product("Bh2", back(1536), 2)
    product("Fh1", forth(0), 2)
    product("Fh2", forth(1536), 2)

    def product_query():
        def body(h):
            store("Fq", head_cols(h), mm(s["normed"][...], s["wqkv"][h]), 3 * HS)

        tiles(HEADS, body)

    ops["M Fq"] = product_query
    for i in range(2, 6):
        ops["load " + str(i)] = loads[i].wait

    def activate(stream, gather, base):
        for i, value in enumerate(R[stream].fin()):
            G[gather].put(i, gelu_value(value).astype(BF16))
            at = base + i * G[gather].ca
            slope[:, at : at + value.shape[1]] = gelu_slope(value)

    def deactivate(stream, gather, base):
        for i, value in enumerate(R[stream].fin()):
            at = base + i * G[gather].ca
            G[gather].put(i, (value * slope[:, at : at + value.shape[1]]).astype(BF16))

    ops["act Fh1"] = lambda: activate("Fh1", "H1", 0)
    ops["act Fh2"] = lambda: activate("Fh2", "H2", 1536)
    ops["deact Bh1"] = lambda: deactivate("Bh1", "G1", 0)
    ops["deact Bh2"] = lambda: deactivate("Bh2", "G2", 1536)

    @op
    def project():
        ja, jb = R["Fq"].fin()
        s["ja"][...] = ja
        s["jb"][...] = jb.reshape(64, 3 * HS)
        normal, _ = head_norm(s["ja"][:, HS : 2 * HS])
        s["KVa"][k.y, :, 0:HS] = normal.astype(BF16)
        s["KVa"][k.y, :, HS : 2 * HS] = s["ja"][:, 2 * HS :].astype(BF16)
        normal, _ = head_norm(s["jb"][:, HS : 2 * HS])
        s["KVb"][k.x, KV.mine, :, 0:HS] = normal.astype(BF16).reshape(2, 32, HS)
        s["KVb"][k.x, KV.mine, :, HS : 2 * HS] = (
            s["jb"][:, 2 * HS :].astype(BF16).reshape(2, 32, HS)
        )

    @op
    def attend():
        parts = R["Ba"].fin()
        for i, (kv, dk, dk_x, own) in enumerate(
            (
                (s["KVa"], s["DKa"], s["DKax"], s["ja"]),
                (s["KVb"], s["DKb"], s["DKbx"], s["jb"]),
            )
        ):
            shape = kv.shape[:-1] + (HS,)
            q_norm, q_inv = head_norm(own[:, 0:HS])
            q_b = q_norm.astype(BF16)
            keys = kv[..., 0:HS].reshape(TOK, HS)
            values = kv[..., HS : 2 * HS].reshape(TOK, HS)
            raised = jnp.exp(mmt(q_b, keys) * FACTOR)
            probs = raised / jnp.sum(raised, -1, keepdims=True)
            probs_b = probs.astype(BF16)
            part = parts[i].astype(BF16).reshape(own.shape[0], HS)
            grad_probs = mmt(part, values)
            row_dot = jnp.sum(probs * grad_probs, -1, keepdims=True)
            grad_scores = (probs * (grad_probs - row_dot)).astype(BF16)
            dk_x[..., 0:HS] = (mtm(grad_scores, q_b) * FACTOR).reshape(shape)
            dk_x[..., HS : 2 * HS] = mtm(probs_b, part).reshape(shape)
            dk[...] = dk_x[...].astype(BF16)
            G["AT"].put_head(i, 0, mm(probs_b, values).astype(BF16))
            grad_query = mm(grad_scores, keys) * FACTOR
            G["GJ"].put_head(i, 0, head_norm_back(grad_query, q_norm, q_inv).astype(BF16))

    def key_value_back(i, own, value):
        k_norm, k_inv = head_norm(own[:, HS : 2 * HS])
        G["GJ"].put_head(i, HS, head_norm_back(value[:, 0:HS], k_norm, k_inv).astype(BF16))
        G["GJ"].put_head(i, 2 * HS, value[:, HS:].astype(BF16))

    ops["KV d3"] = lambda: key_value_back(0, s["ja"], KV.d3())
    ops["KV d4"] = lambda: key_value_back(1, s["jb"], KV.d4().reshape(64, 2 * HS))

    copies = []

    def share(name, half, got, out):
        def give():
            held[name] = k.send(half(1 - core), got, k.cd)

        def add():
            held[name].wait_recv()
            mine = half(core)
            add_to(mine, got)
            copies.append(pltpu.make_async_copy(mine, out, local.at[6 + len(copies)]))
            copies[-1].start()

        ops["sum " + name] = add
        return give

    def share_wide(name, stream, got, out, base):
        assert ORDER.index("dw " + name) > ORDER.index(stream + " s2") + SETTLE
        at = pl.ds(base, 1536)
        part = s[stream + "0"]
        give = share(
            name,
            lambda c: part.at[pl.ds(2 * c, 2), pl.ds(0, 96)],
            s[got].at[:, :, at],
            out.at[:, :, at],
        )

        def put(t, value):
            for c in range(2):
                half = value[c * 192 : (c + 1) * 192].astype(BF16)
                part[2 * c : 2 * c + 2, 0:96, cols(t)] = half.reshape(2, 96, TILE)

        return put, give

    def rows_tile(name, t):
        return s[name][:, :, cols(t)].reshape(TOK, TILE)

    def per_tile(name, body, n):
        ops[name] = lambda: tiles(n, body)

    def with_hidden(name, stream, base):
        put, give = share_wide(name, stream, "gotdown", sum_down, base)

        def total(t):
            add_rows(oacc, mm(rows_tile(name, t), s["wdown"][tile_at(base, t), :]))

        def weights(t):
            put(t, mm(wide(gg), rows_tile(name, t)))

        def run():
            tiles(2, weights)
            give()

        per_tile("acc " + name, total, 2)
        ops["dw " + name] = run

    def with_grads(name, stream, base):
        put, give = share_wide(name, stream, "gotup", sum_up, base)

        def total(t):
            add_rows(gacc, mmt(rows_tile(name, t), s["wup"][:, tile_at(base, t)]))

        def weights(t):
            put(t, mm(s["nT"][...], rows_tile(name, t)))

        def run():
            tiles(2, weights)
            give()

        per_tile("acc " + name, total, 2)
        ops["dw " + name] = run

    with_hidden("H1", "Fh1", 0)
    with_hidden("H2", "Fh2", 1536)
    with_grads("G1", "Bh1", 0)
    with_grads("G2", "Bh2", 1536)

    def total_attended(t):
        add_rows(oacc, mm(rows_tile("AT", 0), s["wout"][...]))

    def total_joined(h):
        block = s["GJ"][:, :, head_cols(h)].reshape(TOK, 3 * HS)
        add_rows(gacc, mmt(block, s["wqkv"][h]))

    per_tile("acc AT", total_attended, 1)
    per_tile("acc GJ", total_joined, HEADS)

    give_attended = share("AT", lambda c: s["sattn"].at[c], s["gotattn"], sum_attn)
    give_joined = share("GJ", lambda c: s["sqkv"].at[c], s["gotqkv"], sum_qkv)

    def weights_attended():
        both = mm(wide(gg), rows_tile("AT", 0)).astype(BF16)
        for c in range(2):
            for h in range(HEADS):
                s["sattn"][c, h] = both[c * 192 : (c + 1) * 192, h * HS : (h + 1) * HS]
        give_attended()

    ops["dw AT"] = weights_attended

    def zscatter(i, total):
        part = s["zp"].at[i]
        turned = mmt(identity(BLK), total.astype(BF16))
        part[...] = turned.astype(BF16).reshape(4, ZC, TOK)
        ring = RingSum(
            k, k.zs, k.zd, lambda j: part.at[j], *split_rows(48), s["zo"].at[i], s["zn"].at[i]
        )
        return ring, turned

    @op
    def gin():
        average, inverse = s["stat"][0:1], s["stat"][1:2]
        held["zi"], turned = zscatter(1, gacc[...].reshape(TOK, BLK))
        held["zi"].start()
        normal = (wide(fg).astype(F32) - average) * inverse
        packed = row_pack(
            jnp.sum(turned, 0, keepdims=True), jnp.sum(turned * normal, 0, keepdims=True)
        )
        held["bz"] = exchange(k, k.zs, k.zd, s["btz"], packed)

    def weights_joined():
        def body(h):
            block = s["GJ"][:, :, head_cols(h)].reshape(TOK, 3 * HS)
            both = mm(s["nT"][...], block).astype(BF16)
            s["sqkv"][0, h] = both[0:192]
            s["sqkv"][1, h] = both[192:384]

        tiles(HEADS, body)
        give_joined()

    ops["dw GJ"] = weights_joined

    @op
    def zi_mid():
        held["zi"].middle()

    @op
    def back_x():
        held["bx"] = exchange(k, k.xs, k.xd, s["btx"], collect(held["bz"], s["btz"]))

    @op
    def back_y():
        held["by"] = exchange(k, k.ys, k.yd, s["bty"], collect(held["bx"], s["btx"]))

    @op
    def gin_out():
        average, inverse = s["stat"][0:1], s["stat"][1:2]
        summed = held["zi"].total()
        sums = collect(held["by"], s["bty"])
        normal_own = (fg[z].astype(F32) - average) * inverse
        correction = summed - sums[0:1] / D - normal_own * (sums[1:2] / D)
        gin_o[...] = (gg[z].astype(F32) + inverse * correction).astype(BF16)

    @op
    def zl_start():
        held["zl"], _ = zscatter(0, oacc[...].reshape(TOK, BLK))
        held["zl"].start()

    @op
    def zl_mid():
        held["zl"].middle()

    @op
    def layer_out():
        layer_o[...] = (fg[z].astype(F32) + held["zl"].total()).astype(BF16)

    for i, name in enumerate(ORDER):
        ops[name]()
        k.settle(i)

    for copy in copies:
        copy.wait()
    k.settle(len(ORDER) + SETTLE)


def on_device(features, w_qkv, w_up, w_out, w_down, grad_out):
    out_flat = w_out.reshape(768, BLK)
    shapes = scratch()
    any_spec = pl.BlockSpec(memory_space=pl.ANY)
    vmem_spec = pl.BlockSpec(memory_space=pltpu.VMEM)

    grads = ((HEADS, 192, 3 * HS), (2, 96, 3072), (HEADS, 192, HS), (2, 96, 3072))
    names = tuple(shapes)
    outs = pl.pallas_call(
        lambda *refs: kernel(names, *refs),
        out_shape=[jax.ShapeDtypeStruct(shape, BF16) for shape in ((ZC, TOK),) * 2 + grads],
        in_specs=[any_spec] * 6,
        out_specs=[vmem_spec] * 2 + [any_spec] * 4,
        scratch_shapes=list(shapes.values()),
        compiler_params=pltpu.CompilerParams(
            collective_id=0, has_side_effects=True, vmem_limit_bytes=62 * 1024 * 1024
        ),
        cost_estimate=pl.CostEstimate(
            flops=11_000_000_000, bytes_accessed=20_000_000, transcendentals=1_000_000
        ),
    )(features.T, grad_out.T, w_qkv.transpose(1, 0, 2), w_up, out_flat, w_down)

    layer_out, grad_in, *grads = finish(
        [out.reshape(192, 3072) if out.shape[0] == 2 else out for out in outs]
    )
    grad_qkv, grad_up, grad_attn, grad_down = grads
    return (
        layer_out.T,
        grad_in.T,
        grad_qkv.transpose(1, 0, 2),
        grad_up,
        grad_attn.transpose(0, 2, 1),
        grad_down.T,
    )


PIECES = 3


def widen_grads(*refs):
    ins, outs, scr = refs[:6], refs[6:12], refs[12:]
    narrow, whole, small, sem = scr[0:4], scr[4:8], scr[8:10], scr[10]
    reads, writes = [], []

    def piece(ref, p):
        n = ref.shape[0] // PIECES
        return ref.at[pl.ds(p * n, n)]

    def move(src, dst):
        copy = pltpu.make_async_copy(src, dst, sem.at[len(reads) + len(writes)])
        copy.start()
        return copy

    for i in range(4):
        for p in range(PIECES):
            reads.append(move(piece(ins[2 + i], p), piece(narrow[i], p)))
    for i in range(2):
        reads.append(move(ins[i], small[i]))
    turn = iter(reads)
    for i in range(4):
        for p in range(PIECES):
            next(turn).wait()
            into = piece(whole[i], p)
            into[...] = piece(narrow[i], p)[...].astype(F32)
            writes.append(move(into, piece(outs[2 + i], p)))
    for i in range(2):
        next(turn).wait()
        writes.append(move(small[i], outs[i]))
    for copy in writes:
        copy.wait()


def finish(arrays):
    grads = arrays[2:]
    any_spec = pl.BlockSpec(memory_space=pl.ANY)
    return pl.pallas_call(
        widen_grads,
        out_shape=[jax.ShapeDtypeStruct((ZC, TOK), BF16)] * 2
        + [jax.ShapeDtypeStruct(array.shape, F32) for array in grads],
        in_specs=[any_spec] * 6,
        out_specs=[any_spec] * 6,
        scratch_shapes=[pltpu.VMEM(array.shape, BF16) for array in grads]
        + [pltpu.VMEM(array.shape, F32) for array in grads]
        + [pltpu.VMEM((ZC, TOK), BF16)] * 2
        + [pltpu.SemaphoreType.DMA((8 * PIECES + 4,))],
        compiler_params=pltpu.CompilerParams(vmem_limit_bytes=60 * 1024 * 1024),
        cost_estimate=pl.CostEstimate(
            flops=2_000_000, bytes_accessed=11_000_000, transcendentals=0
        ),
    )(*arrays)


def solution(mesh):
    in_specs = (
        P("dp", ("mx", "my")),
        P("mx", "my", None),
        P("mx", "my"),
        P("my", None, "mx"),
        P("my", "mx"),
        P("dp", ("mx", "my")),
    )
    out_specs = (
        P("dp", ("mx", "my")),
        P("dp", ("mx", "my")),
        P(("mx", "dp"), "my", None),
        P(("mx", "dp"), "my"),
        P("my", None, ("mx", "dp")),
        P("my", ("mx", "dp")),
    )
    return jax.shard_map(
        on_device, mesh=mesh, in_specs=in_specs, out_specs=out_specs, check_vma=False
    )
```

```python
import math

import jax
import jax.numpy as jnp
from jax import lax
from jax.experimental import pallas as pl
from jax.experimental.pallas import tpu as pltpu
from jax.sharding import PartitionSpec as P

D = 6144
EPS = 1e-06
F32 = jnp.float32
BF16 = jnp.bfloat16
MESH = pl.DeviceIdType.MESH
HEADS = 6
HS = 128
TOK = 512
OWN = 32
BLK = 384
ZC = 96
FACTOR = 1.0 / math.sqrt(HS)
N_SEND = 52
N_RECV = 91
TILE = 768
SETTLE = 8


def mm(a, b):
    return lax.dot_general(a, b, (((1,), (0,)), ((), ())), preferred_element_type=F32)


def mmt(a, b):
    return lax.dot_general(a, b, (((1,), (1,)), ((), ())), preferred_element_type=F32)


def mtm(a, b):
    return lax.dot_general(a, b, (((0,), (0,)), ((), ())), preferred_element_type=F32)


def gelu_value(values):
    return 0.5 * values * (1.0 + lax.erf(values / math.sqrt(2.0)))


def gelu_slope(values):
    return 0.5 * (1.0 + lax.erf(values / math.sqrt(2.0))) + values * jnp.exp(
        -0.5 * values * values
    ) / math.sqrt(2.0 * math.pi)


def head_norm(values):
    average = jnp.mean(values, -1, keepdims=True)
    spread = jnp.mean(values * values, -1, keepdims=True) - average * average
    inverse = lax.rsqrt(spread + EPS)
    return ((values - average) * inverse, inverse)


def head_norm_back(gradient, normal, inverse):
    first_mean = jnp.mean(gradient, -1, keepdims=True)
    second_mean = jnp.mean(gradient * normal, -1, keepdims=True)
    return inverse * (gradient - first_mean - normal * second_mean)


def identity(n):
    row = lax.broadcasted_iota(jnp.int32, (n, n), 0)
    column = lax.broadcasted_iota(jnp.int32, (n, n), 1)
    return jnp.where(row == column, 1.0, 0.0).astype(BF16)


def add_to(ref, more):
    ref[...] = (ref[...].astype(F32) + more[...].astype(F32)).astype(ref.dtype)


class Message:
    def __init__(self, links, copy, way, sems):
        self.links, self.copy, self.way, self.sems = links, copy, way, sems
        self.began, self.arrived = links.tick(), None

    def wait_recv(self):
        self.copy.wait_recv()
        self.arrived = self.links.tick()


class Links:
    def __init__(self, send, recv):
        self.send_sems, self.recv_sems = send, recv
        self.log, self.started, self.clock, self.turn = [], [], 0, 0
        self.free_send, self.used_send, self.last_on = [], 0, []
        mx = lax.axis_index("mx")
        self.x, self.y = lax.rem(mx, 4), lax.div(mx, 4)
        self.z, self.core = lax.axis_index("my"), lax.axis_index("dp")
        x, y, z = self.x, self.y, self.z
        self.xs = [lax.rem(x + i, 4) for i in range(4)]
        self.ys = [lax.rem(y + i, 4) for i in range(4)]
        self.zs = [lax.rem(z + i, 4) for i in range(4)]
        self.xd = [{"mx": y * 4 + v, "way": ("x", i)} for i, v in enumerate(self.xs)]
        self.yd = [{"mx": v * 4 + x, "way": ("y", i)} for i, v in enumerate(self.ys)]
        self.zd = [{"my": v, "way": ("z", i)} for i, v in enumerate(self.zs)]
        self.cd = {"dp": 1 - self.core, "way": ("core", 0)}

    def tick(self):
        self.clock += 1
        return self.clock

    def ready(self, last, way):
        if last.arrived is None:
            return False
        back = (way[0], (4 - way[1]) % 4)
        return any(
            m.way == back and m.began > last.arrived and m.arrived is not None for m in self.log
        )

    def take_recv(self, way):
        for i, last in enumerate(self.last_on):
            if self.ready(last, way):
                return i
        self.last_on.append(None)
        return len(self.last_on) - 1

    def send(self, src, dst, device):
        way = device["way"]
        to = {axis: v for axis, v in device.items() if axis != "way"}
        if self.free_send:
            i = self.free_send.pop(0)
        else:
            i = self.used_send
            self.used_send += 1
        j = self.take_recv(way)
        copy = pltpu.make_async_remote_copy(
            src_ref=src,
            dst_ref=dst,
            send_sem=self.send_sems.at[i],
            recv_sem=self.recv_sems.at[j],
            device_id=to,
            device_id_type=MESH,
        )
        copy.start()
        message = Message(self, copy, way, (i, j))
        self.last_on[j] = message
        self.log.append(message)
        self.started.append((self.turn, message))
        return message

    def settle(self, turn):
        self.turn = turn + 1
        while self.started and self.started[0][0] <= turn - SETTLE:
            message = self.started.pop(0)[1]
            message.copy.wait_send()
            self.free_send.append(message.sems[0])

    def barrier(self):
        sem = pltpu.get_barrier_semaphore()
        peers = self.xd[1:] + self.yd[1:] + self.zd[1:] + [self.cd]
        for peer in peers:
            peer = {axis: v for axis, v in peer.items() if axis != "way"}
            pl.semaphore_signal(sem, inc=1, device_id=peer, device_id_type=MESH)
        pl.semaphore_wait(sem, len(peers))


def rows_of(start, size):
    return pl.ds(pl.multiple_of(start, 16), size)


class RingSum:
    def __init__(self, links, ring, devices, chunk, first, second, opp, near, exact=None):
        self.k, self.ring, self.dev = links, ring, devices
        self.chunk, self.first, self.second, self.opp, self.near = chunk, first, second, opp, near
        self.exact = exact or chunk

    def start(self):
        far, left, right = (self.chunk(self.ring[i]) for i in (2, 3, 1))
        to_left, to_right = self.near.at[1], self.near.at[0]
        self.far_left = self.k.send(self.first(far), self.opp.at[1], self.dev[3])
        self.far_right = self.k.send(self.second(far), self.opp.at[0], self.dev[1])
        self.near_copies = [
            self.k.send(self.second(left), self.second(to_left), self.dev[3]),
            self.k.send(self.first(right), self.first(to_right), self.dev[1]),
        ]

    def relay(self, side, half, slot, arrived):
        j = self.ring[side]
        part = half(self.chunk(j))
        arrived.wait_recv()
        total = half(self.exact(j))[...].astype(F32) + self.opp[slot].astype(F32)
        part[...] = total.astype(part.dtype)
        self.near_copies.append(self.k.send(part, half(self.near.at[slot]), self.dev[side]))

    def middle(self):
        self.relay(3, self.first, 1, self.far_left)
        self.relay(1, self.second, 0, self.far_right)

    def total(self):
        for copy in self.near_copies:
            copy.wait_recv()
        own = self.exact(self.ring[0])
        return own[...].astype(F32) + self.near[0].astype(F32) + self.near[1].astype(F32)


class RingGather:
    def __init__(self, links, ring, devices, chunk, first, second):
        self.k, self.ring, self.dev = links, ring, devices
        self.chunk, self.first, self.second = chunk, first, second

    def start(self):
        own = self.chunk(self.ring[0])
        self.to_left = self.k.send(own, own, self.dev[3])
        self.to_right = self.k.send(own, own, self.dev[1])

    def middle(self):
        self.to_right.wait_recv()
        part = self.first(self.chunk(self.ring[3]))
        self.on_right = self.k.send(part, part, self.dev[1])
        self.to_left.wait_recv()
        part = self.second(self.chunk(self.ring[1]))
        self.on_left = self.k.send(part, part, self.dev[3])

    def finish(self):
        self.on_right.wait_recv()
        self.on_left.wait_recv()


def split_rows(n):
    return (lambda r: r.at[pl.ds(0, n)]), (lambda r: r.at[pl.ds(n, n)])


class Scatter:
    def __init__(self, links, part, bufs, ca, cb, w):
        k = links
        a, b = pl.ds(0, ca), pl.ds(ca, cb)
        a1o, a1n, b1o, b1n, a2, b2, a2o, a2n, b2o, b2n, *whole = bufs
        part_x, a2_x, b2_x = whole or (part, a2, b2)
        self.mids = ((a2, a2_x), (b2, b2_x))
        if w:

            def a2_chunk(ref):
                return lambda j: ref.at[:, part_of(j, w)]

            def b2_chunk(ref):
                return lambda j: ref.at[pl.ds(lax.rem(j, 2) * 2, 2), :, part_of(lax.div(j, 2), w)]

            a2_split, b2_split = split_rows(64), split_rows(1)
        else:

            def a2_chunk(ref):
                return lambda j: ref.at[rows_of(j * 32, 32), :]

            def b2_chunk(ref):
                return lambda j: ref.at[j]

            a2_split = b2_split = split_rows(16)

        def a1_chunk(ref):
            return lambda j: ref.at[j, :, a]

        def b1_chunk(ref):
            return lambda j: ref.at[:, rows_of(j * 32, 32), b]

        def ring(axis, devices, chunk, split, opp, near, ref, ref_x):
            return RingSum(k, axis, devices, chunk(ref), *split, opp, near, chunk(ref_x))

        self.a1 = ring(k.ys, k.yd, a1_chunk, split_rows(64), a1o, a1n, part, part_x)
        self.b1 = ring(k.xs, k.xd, b1_chunk, split_rows(2), b1o, b1n, part, part_x)
        self.a2 = ring(k.xs, k.xd, a2_chunk, a2_split, a2o, a2n, a2, a2_x)
        self.b2 = ring(k.ys, k.yd, b2_chunk, b2_split, b2o, b2n, b2, b2_x)

    def s1(self):
        self.a1.start()
        self.b1.start()

    def s2(self):
        self.a1.middle()
        self.b1.middle()

    def s3(self):
        for before, after, mids in zip((self.a1, self.b1), (self.a2, self.b2), self.mids):
            total = before.total()
            for mid in mids:
                mid[...] = total.astype(mid.dtype)
            after.start()

    def s4(self):
        self.a2.middle()
        self.b2.middle()

    def fin(self):
        return self.a2.total(), self.b2.total()


def part_of(j, w):
    return pl.ds(pl.multiple_of(j * w, 128), w)


def scatter_scratch(ca, cb, w, exact):
    found = [
        pltpu.VMEM((4, 128, ca + cb), BF16),
        pltpu.VMEM((2, 64, ca), BF16),
        pltpu.VMEM((2, 128, ca), BF16),
        pltpu.VMEM((2, 2, 32, cb), BF16),
        pltpu.VMEM((2, 4, 32, cb), BF16),
        pltpu.VMEM((128, ca), BF16),
        pltpu.VMEM((4, 32, cb), BF16),
    ]
    if w:
        found += [
            pltpu.VMEM((2, 64, w), BF16),
            pltpu.VMEM((2, 128, w), BF16),
            pltpu.VMEM((2, 1, 32, w), BF16),
            pltpu.VMEM((2, 2, 32, w), BF16),
        ]
    else:
        found += [
            pltpu.VMEM((2, 16, ca), BF16),
            pltpu.VMEM((2, 32, ca), BF16),
            pltpu.VMEM((2, 16, cb), BF16),
            pltpu.VMEM((2, 32, cb), BF16),
        ]
    if exact:
        found += [
            pltpu.VMEM((4, 128, ca + cb), F32),
            pltpu.VMEM((128, ca), F32),
            pltpu.VMEM((4, 32, cb), F32),
        ]
    return found


class Gather:
    def __init__(self, links, full, ca, cb, w):
        k = links
        a, b = pl.ds(0, ca), pl.ds(ca, cb)
        x, y = k.x, k.y
        self.full, self.ca, self.w, self.k = full, ca, w, k
        if w:
            a1_chunk, a1_split = (lambda j: full.at[y, :, part_of(j, w)]), split_rows(64)
            b1_chunk, b1_split = (
                lambda j: full.at[
                    pl.ds(lax.rem(j, 2) * 2, 2),
                    rows_of(x * 32, 32),
                    part_of(4 + lax.div(j, 2), w),
                ]
            ), split_rows(1)
        else:
            a1_chunk, a1_split = (lambda j: full.at[y, rows_of(j * 32, 32), a]), split_rows(16)
            b1_chunk, b1_split = (lambda j: full.at[j, rows_of(x * 32, 32), b]), split_rows(16)
        self.a1 = RingGather(k, k.xs, k.xd, a1_chunk, *a1_split)
        self.b1 = RingGather(k, k.ys, k.yd, b1_chunk, *b1_split)
        self.a2 = RingGather(k, k.ys, k.yd, lambda j: full.at[j, :, a], *split_rows(64))
        self.b2 = RingGather(
            k, k.xs, k.xd, lambda j: full.at[:, rows_of(j * 32, 32), b], *split_rows(2)
        )

    def put(self, i, value):
        at = pl.ds(0, self.ca) if i == 0 else pl.ds(self.ca, value.shape[1])
        self.full[self.k.y, rows_of(self.k.x * 32, 32), at] = value

    def put_head(self, i, start, value):
        x, y, n = self.k.x, self.k.y, value.shape[1]
        if i == 0:
            self.full[y, :, pl.ds(pl.multiple_of(x * self.w + start, 128), n)] = value
        else:
            at = pl.ds(pl.multiple_of((4 + lax.div(y, 2)) * self.w + start, 128), n)
            half = pl.ds(lax.rem(y, 2) * 2, 2)
            self.full[half, rows_of(x * 32, 32), at] = value.reshape(2, 32, n)

    def s1(self):
        self.a1.start()
        self.b1.start()

    def s2(self):
        self.a1.middle()
        self.b1.middle()

    def s3(self):
        self.a1.finish()
        self.a2.start()
        self.b1.finish()
        self.b2.start()

    def s4(self):
        self.a2.middle()
        self.b2.middle()

    def fin(self):
        self.a2.finish()
        self.b2.finish()


class KeyValue:
    def __init__(self, links, s):
        k = links
        x, y = k.x, k.y
        self.k = k
        a, b, da, db = s["KVa"], s["KVb"], s["DKa"], s["DKb"]
        self.a, self.b, self.da, self.db, self.mid, self.got = a, b, da, db, s["DKm"], s["DKg"]
        self.mine = pl.ds(lax.rem(y, 2) * 2, 2)
        self.other = pl.ds(2 - lax.rem(y, 2) * 2, 2)
        self.mate = {"mx": (y + 1 - 2 * lax.rem(y, 2)) * 4 + x, "way": ("mate", 0)}
        self.ga = RingGather(k, k.ys, k.yd, lambda j: a.at[j], *split_rows(64))
        self.gb = RingGather(k, k.xs, k.xd, lambda j: b.at[j], *split_rows(2))
        self.ra = RingSum(
            k,
            k.ys,
            k.yd,
            lambda j: da.at[j],
            *split_rows(64),
            s["DKao"],
            s["DKan"],
            lambda j: s["DKax"].at[j],
        )
        self.rb = RingSum(
            k,
            k.xs,
            k.xd,
            lambda j: db.at[j],
            *split_rows(2),
            s["DKbo"],
            s["DKbn"],
            lambda j: s["DKbx"].at[j],
        )

    def s1(self):
        own = self.b.at[self.k.x, self.mine]
        self.pair = self.k.send(own, own, self.mate)
        self.ga.start()

    def s2(self):
        self.pair.wait_recv()
        self.gb.start()
        self.ga.middle()

    def s3(self):
        self.gb.middle()

    def fin(self):
        self.ga.finish()
        self.gb.finish()

    def d1(self):
        self.rb.start()
        self.ra.start()

    def d2(self):
        self.rb.middle()
        self.ra.middle()

    def d3(self):
        self.mid[...] = self.rb.total()
        self.back = self.k.send(self.mid.at[self.other], self.got, self.mate)
        return self.ra.total()

    def d4(self):
        self.back.wait_recv()
        return self.mid[self.mine] + self.got[...]


def tiles(n, body):
    for t in range(n):
        body(t)


def cols(t):
    return pl.ds(pl.multiple_of(t * TILE, TILE), TILE)


def exchange(links, ring, devices, buf, value):
    me = ring[0]
    buf[me] = value
    return [links.send(buf.at[me], buf.at[me], devices[i]) for i in (1, 2, 3)]


def collect(copies, buf):
    for copy in copies:
        copy.wait_recv()
    return (buf[0] + buf[1]) + (buf[2] + buf[3])


def row_pack(first, second):
    row = lax.broadcasted_iota(jnp.int32, (2, TOK), 0)
    return jnp.where(row == 0, first, second)


STREAMS = (
    ("Ba", 512, 256, HS, True),
    ("Bh1", 640, 896, 0, False),
    ("Bh2", 640, 896, 0, False),
    ("Fq", 1536, 768, 3 * HS, True),
    ("Fh1", 640, 896, 0, False),
    ("Fh2", 640, 896, 0, False),
)
GATHERS = (
    ("H1", 640, 896, 0),
    ("H2", 640, 896, 0),
    ("G1", 640, 896, 0),
    ("G2", 640, 896, 0),
    ("AT", 512, 256, HS),
    ("GJ", 1536, 768, 3 * HS),
)


ORDER = (
    "enter",
    "zg mid",
    "zf start",
    "zg_end",
    "load 2",
    "M Ba",
    "Ba s1",
    "load 3",
    "M Bh2",
    "Bh2 s1",
    "zf mid",
    "zf_end",
    "Bh2 s2",
    "Ba s2",
    "M Bh1",
    "stat_y",
    "Bh1 s1",
    "norm",
    "load 5",
    "M Fh2",
    "Fh2 s1",
    "load 4",
    "M Fq",
    "Fq s1",
    "Fh2 s2",
    "Ba s3",
    "Fq s2",
    "M Fh1",
    "Bh2 s3",
    "Fh2 s3",
    "Bh1 s2",
    "Fq s3",
    "Fh2 s4",
    "Bh2 s4",
    "Ba s4",
    "Fq s4",
    "Fh1 s1",
    "act Fh2",
    "deact Bh2",
    "G2 s1",
    "project",
    "KV s1",
    "Fh1 s2",
    "KV s2",
    "G2 s2",
    "H2 s1",
    "Bh1 s3",
    "KV s3",
    "Fh1 s3",
    "G2 s3",
    "KV fin",
    "attend",
    "KV d1",
    "H2 s2",
    "Fh1 s4",
    "Bh1 s4",
    "KV d2",
    "H2 s3",
    "act Fh1",
    "KV d3",
    "deact Bh1",
    "H1 s1",
    "G1 s1",
    "KV d4",
    "H2 s4",
    "GJ s1",
    "G1 s2",
    "G2 s4",
    "H1 s2",
    "GJ s2",
    "G1 s3",
    "AT s1",
    "GJ s3",
    "clear",
    "G1 s4",
    "G2 fin",
    "acc G2",
    "dw G2",
    "AT s2",
    "GJ s4",
    "H1 s3",
    "H2 fin",
    "G1 fin",
    "acc G1",
    "dw G1",
    "AT s3",
    "dw H2",
    "GJ fin",
    "acc GJ",
    "gin",
    "acc H2",
    "H1 s4",
    "dw GJ",
    "sum G2",
    "zi_mid",
    "AT s4",
    "back_x",
    "H1 fin",
    "dw H1",
    "acc H1",
    "AT fin",
    "acc AT",
    "zl_start",
    "sum H2",
    "sum G1",
    "dw AT",
    "back_y",
    "zl_mid",
    "sum GJ",
    "gin_out",
    "sum H1",
    "sum AT",
    "layer_out",
)


def scratch():
    s = {
        "send": pltpu.SemaphoreType.DMA((N_SEND,)),
        "recv": pltpu.SemaphoreType.DMA((N_RECV,)),
        "local": pltpu.SemaphoreType.DMA((17,)),
        "wqkv": pltpu.VMEM((BLK, HEADS * 3 * HS), BF16),
        "wup": pltpu.VMEM((BLK, 3072), BF16),
        "wout": pltpu.VMEM((768, BLK), BF16),
        "wdown": pltpu.VMEM((3072, BLK), BF16),
        "fg": pltpu.VMEM((4, ZC, TOK), BF16),
        "gg": pltpu.VMEM((4, ZC, TOK), BF16),
        "gw": pltpu.VMEM((TOK, BLK), BF16),
        "normed": pltpu.VMEM((TOK, BLK), BF16),
        "nT": pltpu.VMEM((BLK, TOK), BF16),
        "stx": pltpu.VMEM((4, 2, TOK), F32),
        "sty": pltpu.VMEM((4, 2, TOK), F32),
        "btx": pltpu.VMEM((4, 2, TOK), F32),
        "bty": pltpu.VMEM((4, 2, TOK), F32),
        "btz": pltpu.VMEM((4, 2, TOK), F32),
        "stat": pltpu.VMEM((2, TOK), F32),
        "slope": pltpu.VMEM((OWN, 3072), F32),
        "zp": pltpu.VMEM((2, 4, ZC, TOK), BF16),
        "zo": pltpu.VMEM((2, 2, 48, TOK), BF16),
        "zn": pltpu.VMEM((2, 2, ZC, TOK), BF16),
        "sattn": pltpu.VMEM((2, HEADS, 192, HS), BF16),
        "sqkv": pltpu.VMEM((2, HEADS, 192, 3 * HS), BF16),
        "gotdown": pltpu.VMEM((2, 96, 3072), BF16),
        "gotattn": pltpu.VMEM((HEADS, 192, HS), BF16),
        "gotup": pltpu.VMEM((2, 96, 3072), BF16),
        "gotqkv": pltpu.VMEM((HEADS, 192, 3 * HS), BF16),
    }
    for name, ca, cb, w, exact in STREAMS:
        for i, item in enumerate(scatter_scratch(ca, cb, w, exact)):
            s[name + str(i)] = item
    for name, ca, cb, w in GATHERS:
        s[name] = pltpu.VMEM((4, 128, ca + cb), BF16)
    for name, shape, kind in (
        ("KVa", (4, 128, 256), BF16),
        ("KVb", (4, 4, 32, 256), BF16),
        ("DKa", (4, 128, 256), BF16),
        ("DKb", (4, 4, 32, 256), BF16),
        ("DKao", (2, 64, 256), BF16),
        ("DKan", (2, 128, 256), BF16),
        ("DKbo", (2, 2, 32, 256), BF16),
        ("DKbn", (2, 4, 32, 256), BF16),
        ("DKax", (4, 128, 256), F32),
        ("DKbx", (4, 4, 32, 256), F32),
        ("DKm", (4, 32, 256), F32),
        ("DKg", (2, 32, 256), F32),
        ("ja", (128, 3 * HS), F32),
        ("jb", (64, 3 * HS), F32),
    ):
        s[name] = pltpu.VMEM(shape, kind)
    return s


def kernel(names, feat, gout, w_qkv, w_up, w_out, w_down, *rest):
    layer_o, gin_o = rest[:2]
    sum_qkv, sum_up, sum_attn, sum_down = rest[2:6]
    s = dict(zip(names, rest[6:]))
    k = Links(s["send"], s["recv"])
    z, core = k.z, k.core
    local = s["local"]
    fg, gg, gw = s["fg"], s["gg"], s["gw"]

    loads = [
        pltpu.make_async_copy(src, dst, local.at[i])
        for i, (src, dst) in enumerate(
            (
                (gout, gg.at[z]),
                (feat, fg.at[z]),
                (w_out, s["wout"]),
                (w_down, s["wdown"]),
                (w_up, s["wup"]),
            )
            + tuple(
                (w_qkv.at[h], s["wqkv"].at[:, pl.ds(h * 3 * HS, 3 * HS)]) for h in range(HEADS)
            )
        )
    ]
    for load in loads:
        load.start()
    k.barrier()

    def wide(buf):
        return buf[...].reshape(BLK, TOK)

    class GatherZ:
        def __init__(self, buf):
            self.rings = [
                RingGather(
                    k, k.zs, k.zd, lambda j, t=t: buf.at[j, :, pl.ds(t, TOK // 2)], *split_rows(48)
                )
                for t in (0, TOK // 2)
            ]

        def start(self):
            for ring in self.rings:
                ring.start()

        def middle(self):
            for ring in self.rings:
                ring.middle()

        def finish(self):
            for ring in self.rings:
                ring.finish()

    R = {}
    for name, ca, cb, w, exact in STREAMS:
        bufs = [s[name + str(i)] for i in range(1, 14 if exact else 11)]
        R[name] = Scatter(k, s[name + "0"], bufs, ca, cb, w)
    G = {name: Gather(k, s[name], ca, cb, w) for name, ca, cb, w in GATHERS}
    KV = KeyValue(k, s)
    ops = {}
    held = {}
    for table in (R, G):
        for name, stream in table.items():
            for step in ("s1", "s2", "s3", "s4", "fin"):
                ops[name + " " + step] = getattr(stream, step)
    for step in ("s1", "s2", "s3", "fin", "d1", "d2"):
        ops["KV " + step] = getattr(KV, step)
    slope = s["slope"]
    oacc, gacc = (s["Fq11"].at[:, :, pl.ds(i * BLK, BLK)] for i in range(2))

    def add_rows(ref, value):
        ref[...] += value.reshape(4, 128, BLK)

    zf, zg = GatherZ(fg), GatherZ(gg)

    def op(function):
        ops[function.__name__] = function
        return function

    @op
    def enter():
        loads[0].wait()
        zg.start()
        loads[1].wait()

    ops["zf start"] = zf.start
    ops["zg mid"] = zg.middle
    ops["zf mid"] = zf.middle

    @op
    def clear():
        for ref in (oacc, gacc):
            ref[...] = jnp.zeros(ref.shape, F32)

    @op
    def zf_end():
        zf.finish()
        values = wide(fg).astype(F32)
        packed = row_pack(
            jnp.sum(values, 0, keepdims=True), jnp.sum(values * values, 0, keepdims=True)
        )
        held["ex"] = exchange(k, k.xs, k.xd, s["stx"], packed)

    @op
    def zg_end():
        zg.finish()
        gw[...] = mmt(identity(TOK), wide(gg)).astype(BF16)

    @op
    def stat_y():
        held["ey"] = exchange(k, k.ys, k.yd, s["sty"], collect(held["ex"], s["stx"]))

    @op
    def norm():
        stat = collect(held["ey"], s["sty"])
        average = stat[0:1] / D
        spread = stat[1:2] / D - average * average
        inverse = lax.rsqrt(spread + EPS)
        s["stat"][...] = row_pack(average, inverse)
        s["nT"][...] = ((wide(fg).astype(F32) - average) * inverse).astype(BF16)
        s["normed"][...] = mmt(identity(TOK), s["nT"][...]).astype(BF16)

    def tile_at(base, t):
        return pl.ds(pl.multiple_of(base + t * TILE, TILE), TILE)

    def store(name, at, value, n):
        s[name + "0"][:, :, at] = value.astype(BF16).reshape(4, 128, n)
        if name + "11" in s:
            s[name + "11"][:, :, at] = value.reshape(4, 128, n)

    def product(name, fn, n):
        def run():
            def body(t):
                store(name, cols(t), fn(t), TILE)

            tiles(n, body)

        ops["M " + name] = run

    def back(base):
        return lambda t: mmt(gw[...], s["wdown"][tile_at(base, t), :])

    def forth(base):
        return lambda t: mm(s["normed"][...], s["wup"][:, tile_at(base, t)])

    product("Ba", lambda t: mmt(gw[...], s["wout"][...]), 1)
    product("Bh1", back(0), 2)
    product("Bh2", back(1536), 2)
    product("Fh1", forth(0), 2)
    product("Fh2", forth(1536), 2)

    product("Fq", lambda t: mm(s["normed"][...], s["wqkv"][:, cols(t)]), 3)

    @op
    def load_query():
        for load in loads[5:]:
            load.wait()

    ops["load 2"], ops["load 3"], ops["load 5"] = (loads[i].wait for i in (2, 3, 4))
    ops["load 4"] = load_query

    def activate(stream, gather, base):
        for i, value in enumerate(R[stream].fin()):
            G[gather].put(i, gelu_value(value).astype(BF16))
            at = base + i * G[gather].ca
            slope[:, at : at + value.shape[1]] = gelu_slope(value)

    def deactivate(stream, gather, base):
        for i, value in enumerate(R[stream].fin()):
            at = base + i * G[gather].ca
            G[gather].put(i, (value * slope[:, at : at + value.shape[1]]).astype(BF16))

    ops["act Fh1"] = lambda: activate("Fh1", "H1", 0)
    ops["act Fh2"] = lambda: activate("Fh2", "H2", 1536)
    ops["deact Bh1"] = lambda: deactivate("Bh1", "G1", 0)
    ops["deact Bh2"] = lambda: deactivate("Bh2", "G2", 1536)

    @op
    def project():
        ja, jb = R["Fq"].fin()
        s["ja"][...] = ja
        s["jb"][...] = jb.reshape(64, 3 * HS)
        normal, _ = head_norm(s["ja"][:, HS : 2 * HS])
        s["KVa"][k.y, :, 0:HS] = normal.astype(BF16)
        s["KVa"][k.y, :, HS : 2 * HS] = s["ja"][:, 2 * HS :].astype(BF16)
        normal, _ = head_norm(s["jb"][:, HS : 2 * HS])
        s["KVb"][k.x, KV.mine, :, 0:HS] = normal.astype(BF16).reshape(2, 32, HS)
        s["KVb"][k.x, KV.mine, :, HS : 2 * HS] = (
            s["jb"][:, 2 * HS :].astype(BF16).reshape(2, 32, HS)
        )

    @op
    def attend():
        parts = R["Ba"].fin()
        for i, (kv, dk, dk_x, own) in enumerate(
            (
                (s["KVa"], s["DKa"], s["DKax"], s["ja"]),
                (s["KVb"], s["DKb"], s["DKbx"], s["jb"]),
            )
        ):
            shape = kv.shape[:-1] + (HS,)
            q_norm, q_inv = head_norm(own[:, 0:HS])
            q_b = q_norm.astype(BF16)
            keys = kv[..., 0:HS].reshape(TOK, HS)
            values = kv[..., HS : 2 * HS].reshape(TOK, HS)
            raised = jnp.exp(mmt(q_b, keys) * FACTOR)
            probs = raised / jnp.sum(raised, -1, keepdims=True)
            probs_b = probs.astype(BF16)
            part = parts[i].astype(BF16).reshape(own.shape[0], HS)
            grad_probs = mmt(part, values)
            row_dot = jnp.sum(probs * grad_probs, -1, keepdims=True)
            grad_scores = (probs * (grad_probs - row_dot)).astype(BF16)
            dk_x[..., 0:HS] = (mtm(grad_scores, q_b) * FACTOR).reshape(shape)
            dk_x[..., HS : 2 * HS] = mtm(probs_b, part).reshape(shape)
            dk[...] = dk_x[...].astype(BF16)
            G["AT"].put_head(i, 0, mm(probs_b, values).astype(BF16))
            grad_query = mm(grad_scores, keys) * FACTOR
            G["GJ"].put_head(i, 0, head_norm_back(grad_query, q_norm, q_inv).astype(BF16))

    def key_value_back(i, own, value):
        k_norm, k_inv = head_norm(own[:, HS : 2 * HS])
        G["GJ"].put_head(i, HS, head_norm_back(value[:, 0:HS], k_norm, k_inv).astype(BF16))
        G["GJ"].put_head(i, 2 * HS, value[:, HS:].astype(BF16))

    ops["KV d3"] = lambda: key_value_back(0, s["ja"], KV.d3())
    ops["KV d4"] = lambda: key_value_back(1, s["jb"], KV.d4().reshape(64, 2 * HS))

    copies = []

    def share(name, half, got, out):
        def give():
            held[name] = k.send(half(1 - core), got, k.cd)

        def add():
            held[name].wait_recv()
            mine = half(core)
            add_to(mine, got)
            copies.append(pltpu.make_async_copy(mine, out, local.at[11 + len(copies)]))
            copies[-1].start()

        ops["sum " + name] = add
        return give

    def share_wide(name, stream, got, out, base):
        assert ORDER.index("dw " + name) > ORDER.index(stream + " s2") + SETTLE
        at = pl.ds(base, 1536)
        part = s[stream + "0"]
        give = share(
            name,
            lambda c: part.at[pl.ds(2 * c, 2), pl.ds(0, 96)],
            s[got].at[:, :, at],
            out.at[:, :, at],
        )

        def put(t, value):
            for c in range(2):
                half = value[c * 192 : (c + 1) * 192].astype(BF16)
                part[2 * c : 2 * c + 2, 0:96, cols(t)] = half.reshape(2, 96, TILE)

        return put, give

    def rows_tile(name, t):
        return s[name][:, :, cols(t)].reshape(TOK, TILE)

    def whole(name):
        return s[name][...].reshape(TOK, s[name].shape[2])

    def with_hidden(name, stream, base):
        put, give = share_wide(name, stream, "gotdown", sum_down, base)

        def total():
            add_rows(oacc, mm(whole(name), s["wdown"][pl.ds(base, 1536), :]))

        def weights(t):
            put(t, mm(wide(gg), rows_tile(name, t)))

        def run():
            tiles(2, weights)
            give()

        ops["acc " + name] = total
        ops["dw " + name] = run

    def with_grads(name, stream, base):
        put, give = share_wide(name, stream, "gotup", sum_up, base)

        def total():
            add_rows(gacc, mmt(whole(name), s["wup"][:, pl.ds(base, 1536)]))

        def weights(t):
            put(t, mm(s["nT"][...], rows_tile(name, t)))

        def run():
            tiles(2, weights)
            give()

        ops["acc " + name] = total
        ops["dw " + name] = run

    with_hidden("H1", "Fh1", 0)
    with_hidden("H2", "Fh2", 1536)
    with_grads("G1", "Bh1", 0)
    with_grads("G2", "Bh2", 1536)

    ops["acc AT"] = lambda: add_rows(oacc, mm(whole("AT"), s["wout"][...]))
    ops["acc GJ"] = lambda: add_rows(gacc, mmt(whole("GJ"), s["wqkv"][...]))

    give_attended = share("AT", lambda c: s["sattn"].at[c], s["gotattn"], sum_attn)
    give_joined = share("GJ", lambda c: s["sqkv"].at[c], s["gotqkv"], sum_qkv)

    def weights_attended():
        both = mm(wide(gg), rows_tile("AT", 0)).astype(BF16)
        for c in range(2):
            for h in range(HEADS):
                s["sattn"][c, h] = both[c * 192 : (c + 1) * 192, h * HS : (h + 1) * HS]
        give_attended()

    ops["dw AT"] = weights_attended

    def zscatter(i, total):
        part = s["zp"].at[i]
        turned = mmt(identity(BLK), total.astype(BF16))
        part[...] = turned.astype(BF16).reshape(4, ZC, TOK)
        ring = RingSum(
            k, k.zs, k.zd, lambda j: part.at[j], *split_rows(48), s["zo"].at[i], s["zn"].at[i]
        )
        return ring, turned

    @op
    def gin():
        average, inverse = s["stat"][0:1], s["stat"][1:2]
        held["zi"], turned = zscatter(1, gacc[...].reshape(TOK, BLK))
        held["zi"].start()
        normal = (wide(fg).astype(F32) - average) * inverse
        packed = row_pack(
            jnp.sum(turned, 0, keepdims=True), jnp.sum(turned * normal, 0, keepdims=True)
        )
        held["bz"] = exchange(k, k.zs, k.zd, s["btz"], packed)

    def weights_joined():
        for t in range(3):
            both = mm(s["nT"][...], rows_tile("GJ", t)).astype(BF16)
            for c in range(2):
                for i in range(2):
                    s["sqkv"][c, 2 * t + i] = both[
                        c * 192 : (c + 1) * 192, i * 3 * HS : (i + 1) * 3 * HS
                    ]
        give_joined()

    ops["dw GJ"] = weights_joined

    @op
    def zi_mid():
        held["zi"].middle()

    @op
    def back_x():
        held["bx"] = exchange(k, k.xs, k.xd, s["btx"], collect(held["bz"], s["btz"]))

    @op
    def back_y():
        held["by"] = exchange(k, k.ys, k.yd, s["bty"], collect(held["bx"], s["btx"]))

    @op
    def gin_out():
        average, inverse = s["stat"][0:1], s["stat"][1:2]
        summed = held["zi"].total()
        sums = collect(held["by"], s["bty"])
        normal_own = (fg[z].astype(F32) - average) * inverse
        correction = summed - sums[0:1] / D - normal_own * (sums[1:2] / D)
        gin_o[...] = (gg[z].astype(F32) + inverse * correction).astype(BF16)

    @op
    def zl_start():
        held["zl"], _ = zscatter(0, oacc[...].reshape(TOK, BLK))
        held["zl"].start()

    @op
    def zl_mid():
        held["zl"].middle()

    @op
    def layer_out():
        layer_o[...] = (fg[z].astype(F32) + held["zl"].total()).astype(BF16)

    for i, name in enumerate(ORDER):
        ops[name]()
        k.settle(i)

    for copy in copies:
        copy.wait()
    k.settle(len(ORDER) + SETTLE)


def on_device(features, w_qkv, w_up, w_out, w_down, grad_out):
    out_flat = w_out.reshape(768, BLK)
    shapes = scratch()
    any_spec = pl.BlockSpec(memory_space=pl.ANY)
    vmem_spec = pl.BlockSpec(memory_space=pltpu.VMEM)

    grads = ((HEADS, 192, 3 * HS), (2, 96, 3072), (HEADS, 192, HS), (2, 96, 3072))
    names = tuple(shapes)
    outs = pl.pallas_call(
        lambda *refs: kernel(names, *refs),
        out_shape=[jax.ShapeDtypeStruct(shape, BF16) for shape in ((ZC, TOK),) * 2 + grads],
        in_specs=[any_spec] * 6,
        out_specs=[vmem_spec] * 2 + [any_spec] * 4,
        scratch_shapes=list(shapes.values()),
        compiler_params=pltpu.CompilerParams(
            collective_id=0, has_side_effects=True, vmem_limit_bytes=62 * 1024 * 1024
        ),
        cost_estimate=pl.CostEstimate(
            flops=11_000_000_000, bytes_accessed=20_000_000, transcendentals=1_000_000
        ),
    )(features.T, grad_out.T, w_qkv.transpose(1, 0, 2), w_up, out_flat, w_down)

    layer_out, grad_in, *grads = finish(
        [out.reshape(192, 3072) if out.shape[0] == 2 else out for out in outs]
    )
    grad_qkv, grad_up, grad_attn, grad_down = grads
    return (
        layer_out.T,
        grad_in.T,
        grad_qkv.transpose(1, 0, 2),
        grad_up,
        grad_attn.transpose(0, 2, 1),
        grad_down.T,
    )


PIECES = 3


def widen_grads(*refs):
    ins, outs, scr = refs[:6], refs[6:12], refs[12:]
    narrow, whole, small, sem = scr[0:4], scr[4:8], scr[8:10], scr[10]
    reads, writes = [], []

    def piece(ref, p):
        n = ref.shape[0] // PIECES
        return ref.at[pl.ds(p * n, n)]

    def move(src, dst):
        copy = pltpu.make_async_copy(src, dst, sem.at[len(reads) + len(writes)])
        copy.start()
        return copy

    for i in range(4):
        for p in range(PIECES):
            reads.append(move(piece(ins[2 + i], p), piece(narrow[i], p)))
    for i in range(2):
        reads.append(move(ins[i], small[i]))
    turn = iter(reads)
    for i in range(4):
        for p in range(PIECES):
            next(turn).wait()
            into = piece(whole[i], p)
            into[...] = piece(narrow[i], p)[...].astype(F32)
            writes.append(move(into, piece(outs[2 + i], p)))
    for i in range(2):
        next(turn).wait()
        writes.append(move(small[i], outs[i]))
    for copy in writes:
        copy.wait()


def finish(arrays):
    grads = arrays[2:]
    any_spec = pl.BlockSpec(memory_space=pl.ANY)
    return pl.pallas_call(
        widen_grads,
        out_shape=[jax.ShapeDtypeStruct((ZC, TOK), BF16)] * 2
        + [jax.ShapeDtypeStruct(array.shape, F32) for array in grads],
        in_specs=[any_spec] * 6,
        out_specs=[any_spec] * 6,
        scratch_shapes=[pltpu.VMEM(array.shape, BF16) for array in grads]
        + [pltpu.VMEM(array.shape, F32) for array in grads]
        + [pltpu.VMEM((ZC, TOK), BF16)] * 2
        + [pltpu.SemaphoreType.DMA((8 * PIECES + 4,))],
        compiler_params=pltpu.CompilerParams(vmem_limit_bytes=60 * 1024 * 1024),
        cost_estimate=pl.CostEstimate(
            flops=2_000_000, bytes_accessed=11_000_000, transcendentals=0
        ),
    )(*arrays)


def solution(mesh):
    in_specs = (
        P("dp", ("mx", "my")),
        P("mx", "my", None),
        P("mx", "my"),
        P("my", None, "mx"),
        P("my", "mx"),
        P("dp", ("mx", "my")),
    )
    out_specs = (
        P("dp", ("mx", "my")),
        P("dp", ("mx", "my")),
        P(("mx", "dp"), "my", None),
        P(("mx", "dp"), "my"),
        P("my", None, ("mx", "dp")),
        P("my", ("mx", "dp")),
    )
    return jax.shard_map(
        on_device, mesh=mesh, in_specs=in_specs, out_specs=out_specs, check_vma=False
    )
```

```python
import math

import jax
import jax.numpy as jnp
from jax import lax
from jax.experimental import pallas as pl
from jax.experimental.pallas import tpu as pltpu
from jax.sharding import PartitionSpec as P

D = 6144
EPS = 1e-06
F32 = jnp.float32
BF16 = jnp.bfloat16
MESH = pl.DeviceIdType.MESH
HEADS = 6
HS = 128
TOK = 512
OWN = 32
BLK = 384
ZC = 96
FACTOR = 1.0 / math.sqrt(HS)
N_SEND = 52
N_RECV = 91
TILE = 768
SETTLE = 8


def mm(a, b):
    return lax.dot_general(a, b, (((1,), (0,)), ((), ())), preferred_element_type=F32)


def mmt(a, b):
    return lax.dot_general(a, b, (((1,), (1,)), ((), ())), preferred_element_type=F32)


def mtm(a, b):
    return lax.dot_general(a, b, (((0,), (0,)), ((), ())), preferred_element_type=F32)


def gelu_value(values):
    return 0.5 * values * (1.0 + lax.erf(values / math.sqrt(2.0)))


def gelu_slope(values):
    return 0.5 * (1.0 + lax.erf(values / math.sqrt(2.0))) + values * jnp.exp(
        -0.5 * values * values
    ) / math.sqrt(2.0 * math.pi)


def head_norm(values):
    average = jnp.mean(values, -1, keepdims=True)
    spread = jnp.mean(values * values, -1, keepdims=True) - average * average
    inverse = lax.rsqrt(spread + EPS)
    return ((values - average) * inverse, inverse)


def head_norm_back(gradient, normal, inverse):
    first_mean = jnp.mean(gradient, -1, keepdims=True)
    second_mean = jnp.mean(gradient * normal, -1, keepdims=True)
    return inverse * (gradient - first_mean - normal * second_mean)


def identity(n):
    row = lax.broadcasted_iota(jnp.int32, (n, n), 0)
    column = lax.broadcasted_iota(jnp.int32, (n, n), 1)
    return jnp.where(row == column, 1.0, 0.0).astype(BF16)


def add_to(ref, more):
    ref[...] = (ref[...].astype(F32) + more[...].astype(F32)).astype(ref.dtype)


class Message:
    def __init__(self, links, copy, way, sems):
        self.links, self.copy, self.way, self.sems = links, copy, way, sems
        self.began, self.arrived = links.tick(), None

    def wait_recv(self):
        self.copy.wait_recv()
        self.arrived = self.links.tick()


class Links:
    def __init__(self, send, recv):
        self.send_sems, self.recv_sems = send, recv
        self.log, self.started, self.clock, self.turn = [], [], 0, 0
        self.free_send, self.used_send, self.last_on = [], 0, []
        mx = lax.axis_index("mx")
        self.x, self.y = lax.rem(mx, 4), lax.div(mx, 4)
        self.z, self.core = lax.axis_index("my"), lax.axis_index("dp")
        x, y, z = self.x, self.y, self.z
        self.xs = [lax.rem(x + i, 4) for i in range(4)]
        self.ys = [lax.rem(y + i, 4) for i in range(4)]
        self.zs = [lax.rem(z + i, 4) for i in range(4)]
        self.xd = [{"mx": y * 4 + v, "way": ("x", i)} for i, v in enumerate(self.xs)]
        self.yd = [{"mx": v * 4 + x, "way": ("y", i)} for i, v in enumerate(self.ys)]
        self.zd = [{"my": v, "way": ("z", i)} for i, v in enumerate(self.zs)]
        self.cd = {"dp": 1 - self.core, "way": ("core", 0)}

    def tick(self):
        self.clock += 1
        return self.clock

    def ready(self, last, way):
        if last.arrived is None:
            return False
        back = (way[0], (4 - way[1]) % 4)
        return any(
            m.way == back and m.began > last.arrived and m.arrived is not None for m in self.log
        )

    def take_recv(self, way):
        for i, last in enumerate(self.last_on):
            if self.ready(last, way):
                return i
        self.last_on.append(None)
        return len(self.last_on) - 1

    def send(self, src, dst, device):
        way = device["way"]
        to = {axis: v for axis, v in device.items() if axis != "way"}
        if self.free_send:
            i = self.free_send.pop(0)
        else:
            i = self.used_send
            self.used_send += 1
        j = self.take_recv(way)
        copy = pltpu.make_async_remote_copy(
            src_ref=src,
            dst_ref=dst,
            send_sem=self.send_sems.at[i],
            recv_sem=self.recv_sems.at[j],
            device_id=to,
            device_id_type=MESH,
        )
        copy.start()
        message = Message(self, copy, way, (i, j))
        self.last_on[j] = message
        self.log.append(message)
        self.started.append((self.turn, message))
        return message

    def settle(self, turn):
        self.turn = turn + 1
        while self.started and self.started[0][0] <= turn - SETTLE:
            message = self.started.pop(0)[1]
            message.copy.wait_send()
            self.free_send.append(message.sems[0])

    def barrier(self):
        sem = pltpu.get_barrier_semaphore()
        peers = self.xd[1:] + self.yd[1:] + self.zd[1:] + [self.cd]
        for peer in peers:
            peer = {axis: v for axis, v in peer.items() if axis != "way"}
            pl.semaphore_signal(sem, inc=1, device_id=peer, device_id_type=MESH)
        pl.semaphore_wait(sem, len(peers))


def rows_of(start, size):
    return pl.ds(pl.multiple_of(start, 16), size)


class RingSum:
    def __init__(self, links, ring, devices, chunk, first, second, opp, near, exact=None):
        self.k, self.ring, self.dev = links, ring, devices
        self.chunk, self.first, self.second, self.opp, self.near = chunk, first, second, opp, near
        self.exact = exact or chunk

    def start(self):
        far, left, right = (self.chunk(self.ring[i]) for i in (2, 3, 1))
        to_left, to_right = self.near.at[1], self.near.at[0]
        self.far_left = self.k.send(self.first(far), self.opp.at[1], self.dev[3])
        self.far_right = self.k.send(self.second(far), self.opp.at[0], self.dev[1])
        self.near_copies = [
            self.k.send(self.second(left), self.second(to_left), self.dev[3]),
            self.k.send(self.first(right), self.first(to_right), self.dev[1]),
        ]

    def relay(self, side, half, slot, arrived):
        j = self.ring[side]
        part = half(self.chunk(j))
        arrived.wait_recv()
        total = half(self.exact(j))[...].astype(F32) + self.opp[slot].astype(F32)
        part[...] = total.astype(part.dtype)
        self.near_copies.append(self.k.send(part, half(self.near.at[slot]), self.dev[side]))

    def middle(self):
        self.relay(3, self.first, 1, self.far_left)
        self.relay(1, self.second, 0, self.far_right)

    def total(self):
        for copy in self.near_copies:
            copy.wait_recv()
        own = self.exact(self.ring[0])
        return own[...].astype(F32) + self.near[0].astype(F32) + self.near[1].astype(F32)


class RingGather:
    def __init__(self, links, ring, devices, chunk, first, second):
        self.k, self.ring, self.dev = links, ring, devices
        self.chunk, self.first, self.second = chunk, first, second

    def start(self):
        own = self.chunk(self.ring[0])
        self.to_left = self.k.send(own, own, self.dev[3])
        self.to_right = self.k.send(own, own, self.dev[1])

    def middle(self):
        self.to_right.wait_recv()
        part = self.first(self.chunk(self.ring[3]))
        self.on_right = self.k.send(part, part, self.dev[1])
        self.to_left.wait_recv()
        part = self.second(self.chunk(self.ring[1]))
        self.on_left = self.k.send(part, part, self.dev[3])

    def finish(self):
        self.on_right.wait_recv()
        self.on_left.wait_recv()


def split_rows(n):
    return (lambda r: r.at[pl.ds(0, n)]), (lambda r: r.at[pl.ds(n, n)])


class Scatter:
    def __init__(self, links, part, bufs, ca, cb, w):
        k = links
        a, b = pl.ds(0, ca), pl.ds(ca, cb)
        a1o, a1n, b1o, b1n, a2, b2, a2o, a2n, b2o, b2n, *whole = bufs
        part_x, a2_x, b2_x = whole or (part, a2, b2)
        self.mids = ((a2, a2_x), (b2, b2_x))
        if w:

            def a2_chunk(ref):
                return lambda j: ref.at[:, part_of(j, w)]

            def b2_chunk(ref):
                return lambda j: ref.at[pl.ds(lax.rem(j, 2) * 2, 2), :, part_of(lax.div(j, 2), w)]

            a2_split, b2_split = split_rows(64), split_rows(1)
        else:

            def a2_chunk(ref):
                return lambda j: ref.at[rows_of(j * 32, 32), :]

            def b2_chunk(ref):
                return lambda j: ref.at[j]

            a2_split = b2_split = split_rows(16)

        def a1_chunk(ref):
            return lambda j: ref.at[j, :, a]

        def b1_chunk(ref):
            return lambda j: ref.at[:, rows_of(j * 32, 32), b]

        def ring(axis, devices, chunk, split, opp, near, ref, ref_x):
            return RingSum(k, axis, devices, chunk(ref), *split, opp, near, chunk(ref_x))

        self.a1 = ring(k.ys, k.yd, a1_chunk, split_rows(64), a1o, a1n, part, part_x)
        self.b1 = ring(k.xs, k.xd, b1_chunk, split_rows(2), b1o, b1n, part, part_x)
        self.a2 = ring(k.xs, k.xd, a2_chunk, a2_split, a2o, a2n, a2, a2_x)
        self.b2 = ring(k.ys, k.yd, b2_chunk, b2_split, b2o, b2n, b2, b2_x)

    def s1(self):
        self.a1.start()
        self.b1.start()

    def s2(self):
        self.a1.middle()
        self.b1.middle()

    def s3(self):
        for before, after, mids in zip((self.a1, self.b1), (self.a2, self.b2), self.mids):
            total = before.total()
            for mid in mids:
                mid[...] = total.astype(mid.dtype)
            after.start()

    def s4(self):
        self.a2.middle()
        self.b2.middle()

    def fin(self):
        return self.a2.total(), self.b2.total()


def part_of(j, w):
    return pl.ds(pl.multiple_of(j * w, 128), w)


def scatter_scratch(ca, cb, w, exact):
    found = [
        pltpu.VMEM((4, 128, ca + cb), BF16),
        pltpu.VMEM((2, 64, ca), BF16),
        pltpu.VMEM((2, 128, ca), BF16),
        pltpu.VMEM((2, 2, 32, cb), BF16),
        pltpu.VMEM((2, 4, 32, cb), BF16),
        pltpu.VMEM((128, ca), BF16),
        pltpu.VMEM((4, 32, cb), BF16),
    ]
    if w:
        found += [
            pltpu.VMEM((2, 64, w), BF16),
            pltpu.VMEM((2, 128, w), BF16),
            pltpu.VMEM((2, 1, 32, w), BF16),
            pltpu.VMEM((2, 2, 32, w), BF16),
        ]
    else:
        found += [
            pltpu.VMEM((2, 16, ca), BF16),
            pltpu.VMEM((2, 32, ca), BF16),
            pltpu.VMEM((2, 16, cb), BF16),
            pltpu.VMEM((2, 32, cb), BF16),
        ]
    if exact:
        found += [
            pltpu.VMEM((4, 128, ca + cb), F32),
            pltpu.VMEM((128, ca), F32),
            pltpu.VMEM((4, 32, cb), F32),
        ]
    return found


class Gather:
    def __init__(self, links, full, ca, cb, w):
        k = links
        a, b = pl.ds(0, ca), pl.ds(ca, cb)
        x, y = k.x, k.y
        self.full, self.ca, self.w, self.k = full, ca, w, k
        if w:
            a1_chunk, a1_split = (lambda j: full.at[y, :, part_of(j, w)]), split_rows(64)
            b1_chunk, b1_split = (
                lambda j: full.at[
                    pl.ds(lax.rem(j, 2) * 2, 2),
                    rows_of(x * 32, 32),
                    part_of(4 + lax.div(j, 2), w),
                ]
            ), split_rows(1)
        else:
            a1_chunk, a1_split = (lambda j: full.at[y, rows_of(j * 32, 32), a]), split_rows(16)
            b1_chunk, b1_split = (lambda j: full.at[j, rows_of(x * 32, 32), b]), split_rows(16)
        self.a1 = RingGather(k, k.xs, k.xd, a1_chunk, *a1_split)
        self.b1 = RingGather(k, k.ys, k.yd, b1_chunk, *b1_split)
        self.a2 = RingGather(k, k.ys, k.yd, lambda j: full.at[j, :, a], *split_rows(64))
        self.b2 = RingGather(
            k, k.xs, k.xd, lambda j: full.at[:, rows_of(j * 32, 32), b], *split_rows(2)
        )

    def put(self, i, value):
        at = pl.ds(0, self.ca) if i == 0 else pl.ds(self.ca, value.shape[1])
        self.full[self.k.y, rows_of(self.k.x * 32, 32), at] = value

    def put_head(self, i, start, value):
        x, y, n = self.k.x, self.k.y, value.shape[1]
        if i == 0:
            self.full[y, :, pl.ds(pl.multiple_of(x * self.w + start, 128), n)] = value
        else:
            at = pl.ds(pl.multiple_of((4 + lax.div(y, 2)) * self.w + start, 128), n)
            half = pl.ds(lax.rem(y, 2) * 2, 2)
            self.full[half, rows_of(x * 32, 32), at] = value.reshape(2, 32, n)

    def s1(self):
        self.a1.start()
        self.b1.start()

    def s2(self):
        self.a1.middle()
        self.b1.middle()

    def s3(self):
        self.a1.finish()
        self.a2.start()
        self.b1.finish()
        self.b2.start()

    def s4(self):
        self.a2.middle()
        self.b2.middle()

    def fin(self):
        self.a2.finish()
        self.b2.finish()


class KeyValue:
    def __init__(self, links, s):
        k = links
        x, y = k.x, k.y
        self.k = k
        a, b, da, db = s["KVa"], s["KVb"], s["DKa"], s["DKb"]
        self.a, self.b, self.da, self.db, self.mid, self.got = a, b, da, db, s["DKm"], s["DKg"]
        self.mine = pl.ds(lax.rem(y, 2) * 2, 2)
        self.other = pl.ds(2 - lax.rem(y, 2) * 2, 2)
        self.mate = {"mx": (y + 1 - 2 * lax.rem(y, 2)) * 4 + x, "way": ("mate", 0)}
        self.ga = RingGather(k, k.ys, k.yd, lambda j: a.at[j], *split_rows(64))
        self.gb = RingGather(k, k.xs, k.xd, lambda j: b.at[j], *split_rows(2))
        self.ra = RingSum(
            k,
            k.ys,
            k.yd,
            lambda j: da.at[j],
            *split_rows(64),
            s["DKao"],
            s["DKan"],
            lambda j: s["DKax"].at[j],
        )
        self.rb = RingSum(
            k,
            k.xs,
            k.xd,
            lambda j: db.at[j],
            *split_rows(2),
            s["DKbo"],
            s["DKbn"],
            lambda j: s["DKbx"].at[j],
        )

    def s1(self):
        own = self.b.at[self.k.x, self.mine]
        self.pair = self.k.send(own, own, self.mate)
        self.ga.start()

    def s2(self):
        self.pair.wait_recv()
        self.gb.start()
        self.ga.middle()

    def s3(self):
        self.gb.middle()

    def fin(self):
        self.ga.finish()
        self.gb.finish()

    def d1(self):
        self.rb.start()
        self.ra.start()

    def d2(self):
        self.rb.middle()
        self.ra.middle()

    def d3(self):
        self.mid[...] = self.rb.total()
        self.back = self.k.send(self.mid.at[self.other], self.got, self.mate)
        return self.ra.total()

    def d4(self):
        self.back.wait_recv()
        return self.mid[self.mine] + self.got[...]


def tiles(n, body):
    for t in range(n):
        body(t)


def cols(t):
    return pl.ds(pl.multiple_of(t * TILE, TILE), TILE)


def exchange(links, ring, devices, buf, value):
    me = ring[0]
    buf[me] = value
    return [links.send(buf.at[me], buf.at[me], devices[i]) for i in (1, 2, 3)]


def collect(copies, buf):
    for copy in copies:
        copy.wait_recv()
    return (buf[0] + buf[1]) + (buf[2] + buf[3])


def row_pack(first, second):
    row = lax.broadcasted_iota(jnp.int32, (2, TOK), 0)
    return jnp.where(row == 0, first, second)


STREAMS = (
    ("Ba", 512, 256, HS, True),
    ("Bh1", 640, 896, 0, False),
    ("Bh2", 640, 896, 0, False),
    ("Fq", 1536, 768, 3 * HS, True),
    ("Fh1", 640, 896, 0, False),
    ("Fh2", 640, 896, 0, False),
)
GATHERS = (
    ("H1", 640, 896, 0),
    ("H2", 640, 896, 0),
    ("G1", 640, 896, 0),
    ("G2", 640, 896, 0),
    ("AT", 512, 256, HS),
    ("GJ", 1536, 768, 3 * HS),
)


ORDER = (
    "enter",
    "zg mid",
    "zf start",
    "zg_end",
    "load 2",
    "M Ba",
    "Ba s1",
    "load 3",
    "M Bh2",
    "Bh2 s1",
    "zf mid",
    "zf_end",
    "Bh2 s2",
    "Ba s2",
    "M Bh1",
    "stat_y",
    "Bh1 s1",
    "norm",
    "load 5",
    "M Fh2",
    "Fh2 s1",
    "load 4",
    "M Fq",
    "Fq s1",
    "Fh2 s2",
    "Ba s3",
    "Fq s2",
    "M Fh1",
    "Bh2 s3",
    "Fh2 s3",
    "Bh1 s2",
    "Fq s3",
    "Fh2 s4",
    "Bh2 s4",
    "Ba s4",
    "Fq s4",
    "Fh1 s1",
    "act Fh2",
    "deact Bh2",
    "G2 s1",
    "project",
    "KV s1",
    "Fh1 s2",
    "KV s2",
    "G2 s2",
    "H2 s1",
    "Bh1 s3",
    "KV s3",
    "Fh1 s3",
    "G2 s3",
    "KV fin",
    "attend",
    "KV d1",
    "H2 s2",
    "Fh1 s4",
    "Bh1 s4",
    "KV d2",
    "H2 s3",
    "act Fh1",
    "KV d3",
    "deact Bh1",
    "H1 s1",
    "G1 s1",
    "KV d4",
    "H2 s4",
    "GJ s1",
    "G1 s2",
    "G2 s4",
    "H1 s2",
    "GJ s2",
    "G1 s3",
    "AT s1",
    "GJ s3",
    "clear",
    "G1 s4",
    "G2 fin",
    "acc G2",
    "dw G2",
    "AT s2",
    "GJ s4",
    "H1 s3",
    "H2 fin",
    "G1 fin",
    "acc G1",
    "dw G1",
    "AT s3",
    "dw H2",
    "GJ fin",
    "acc GJ",
    "gin",
    "acc H2",
    "H1 s4",
    "dw GJ",
    "sum G2",
    "zi_mid",
    "AT s4",
    "back_x",
    "H1 fin",
    "dw H1",
    "acc H1",
    "AT fin",
    "acc AT",
    "zl_start",
    "sum H2",
    "sum G1",
    "dw AT",
    "back_y",
    "zl_mid",
    "sum GJ",
    "gin_out",
    "sum H1",
    "sum AT",
    "layer_out",
)


def scratch():
    s = {
        "send": pltpu.SemaphoreType.DMA((N_SEND,)),
        "recv": pltpu.SemaphoreType.DMA((N_RECV,)),
        "local": pltpu.SemaphoreType.DMA((17,)),
        "wqkv": pltpu.VMEM((BLK, HEADS * 3 * HS), BF16),
        "wup": pltpu.VMEM((BLK, 3072), BF16),
        "wout": pltpu.VMEM((768, BLK), BF16),
        "wdown": pltpu.VMEM((3072, BLK), BF16),
        "fg": pltpu.VMEM((4, ZC, TOK), BF16),
        "gg": pltpu.VMEM((4, ZC, TOK), BF16),
        "eye": pltpu.VMEM((TOK, TOK), BF16),
        "gw": pltpu.VMEM((TOK, BLK), BF16),
        "normed": pltpu.VMEM((TOK, BLK), BF16),
        "nT": pltpu.VMEM((BLK, TOK), BF16),
        "stx": pltpu.VMEM((4, 2, TOK), F32),
        "sty": pltpu.VMEM((4, 2, TOK), F32),
        "btx": pltpu.VMEM((4, 2, TOK), F32),
        "bty": pltpu.VMEM((4, 2, TOK), F32),
        "btz": pltpu.VMEM((4, 2, TOK), F32),
        "stat": pltpu.VMEM((2, TOK), F32),
        "slope": pltpu.VMEM((OWN, 3072), F32),
        "zp": pltpu.VMEM((2, 4, ZC, TOK), BF16),
        "zo": pltpu.VMEM((2, 2, 48, TOK), BF16),
        "zn": pltpu.VMEM((2, 2, ZC, TOK), BF16),
        "sattn": pltpu.VMEM((2, HEADS, 192, HS), BF16),
        "sqkv": pltpu.VMEM((2, HEADS, 192, 3 * HS), BF16),
        "gotdown": pltpu.VMEM((2, 96, 3072), BF16),
        "gotattn": pltpu.VMEM((HEADS, 192, HS), BF16),
        "gotup": pltpu.VMEM((2, 96, 3072), BF16),
        "gotqkv": pltpu.VMEM((HEADS, 192, 3 * HS), BF16),
    }
    for name, ca, cb, w, exact in STREAMS:
        for i, item in enumerate(scatter_scratch(ca, cb, w, exact)):
            s[name + str(i)] = item
    for name, ca, cb, w in GATHERS:
        s[name] = pltpu.VMEM((4, 128, ca + cb), BF16)
    for name, shape, kind in (
        ("KVa", (4, 128, 256), BF16),
        ("KVb", (4, 4, 32, 256), BF16),
        ("DKa", (4, 128, 256), BF16),
        ("DKb", (4, 4, 32, 256), BF16),
        ("DKao", (2, 64, 256), BF16),
        ("DKan", (2, 128, 256), BF16),
        ("DKbo", (2, 2, 32, 256), BF16),
        ("DKbn", (2, 4, 32, 256), BF16),
        ("DKax", (4, 128, 256), F32),
        ("DKbx", (4, 4, 32, 256), F32),
        ("DKm", (4, 32, 256), F32),
        ("DKg", (2, 32, 256), F32),
        ("ja", (128, 3 * HS), F32),
        ("jb", (64, 3 * HS), F32),
    ):
        s[name] = pltpu.VMEM(shape, kind)
    return s


def kernel(names, feat, gout, w_qkv, w_up, w_out, w_down, *rest):
    layer_o, gin_o = rest[:2]
    sum_qkv, sum_up, sum_attn, sum_down = rest[2:6]
    s = dict(zip(names, rest[6:]))
    k = Links(s["send"], s["recv"])
    z, core = k.z, k.core
    local = s["local"]
    fg, gg, gw = s["fg"], s["gg"], s["gw"]

    loads = [
        pltpu.make_async_copy(src, dst, local.at[i])
        for i, (src, dst) in enumerate(
            (
                (gout, gg.at[z]),
                (feat, fg.at[z]),
                (w_out, s["wout"]),
                (w_down, s["wdown"]),
                (w_up, s["wup"]),
            )
            + tuple(
                (w_qkv.at[h], s["wqkv"].at[:, pl.ds(h * 3 * HS, 3 * HS)]) for h in range(HEADS)
            )
        )
    ]
    for load in loads:
        load.start()
    k.barrier()

    def wide(buf):
        return buf[...].reshape(BLK, TOK)

    class GatherZ:
        def __init__(self, buf):
            self.rings = [
                RingGather(
                    k, k.zs, k.zd, lambda j, t=t: buf.at[j, :, pl.ds(t, TOK // 2)], *split_rows(48)
                )
                for t in (0, TOK // 2)
            ]

        def start(self):
            for ring in self.rings:
                ring.start()

        def middle(self):
            for ring in self.rings:
                ring.middle()

        def finish(self):
            for ring in self.rings:
                ring.finish()

    R = {}
    for name, ca, cb, w, exact in STREAMS:
        bufs = [s[name + str(i)] for i in range(1, 14 if exact else 11)]
        R[name] = Scatter(k, s[name + "0"], bufs, ca, cb, w)
    G = {name: Gather(k, s[name], ca, cb, w) for name, ca, cb, w in GATHERS}
    KV = KeyValue(k, s)
    ops = {}
    held = {}
    for table in (R, G):
        for name, stream in table.items():
            for step in ("s1", "s2", "s3", "s4", "fin"):
                ops[name + " " + step] = getattr(stream, step)
    for step in ("s1", "s2", "s3", "fin", "d1", "d2"):
        ops["KV " + step] = getattr(KV, step)
    slope = s["slope"]
    oacc, gacc = (s["Fq11"].at[:, :, pl.ds(i * BLK, BLK)] for i in range(2))

    def add_rows(ref, value):
        ref[...] += value.reshape(4, 128, BLK)

    zf, zg = GatherZ(fg), GatherZ(gg)

    def op(function):
        ops[function.__name__] = function
        return function

    @op
    def enter():
        loads[0].wait()
        zg.start()
        s["eye"][...] = identity(TOK)
        loads[1].wait()

    ops["zf start"] = zf.start
    ops["zg mid"] = zg.middle
    ops["zf mid"] = zf.middle

    @op
    def clear():
        for ref in (oacc, gacc):
            ref[...] = jnp.zeros(ref.shape, F32)

    @op
    def zf_end():
        zf.finish()
        values = wide(fg).astype(F32)
        packed = row_pack(
            jnp.sum(values, 0, keepdims=True), jnp.sum(values * values, 0, keepdims=True)
        )
        held["ex"] = exchange(k, k.xs, k.xd, s["stx"], packed)

    @op
    def zg_end():
        zg.finish()
        gw[...] = mmt(s["eye"][...], wide(gg)).astype(BF16)

    @op
    def stat_y():
        held["ey"] = exchange(k, k.ys, k.yd, s["sty"], collect(held["ex"], s["stx"]))

    @op
    def norm():
        stat = collect(held["ey"], s["sty"])
        average = stat[0:1] / D
        spread = stat[1:2] / D - average * average
        inverse = lax.rsqrt(spread + EPS)
        s["stat"][...] = row_pack(average, inverse)
        s["nT"][...] = ((wide(fg).astype(F32) - average) * inverse).astype(BF16)
        s["normed"][...] = mmt(s["eye"][...], s["nT"][...]).astype(BF16)

    def tile_at(base, t):
        return pl.ds(pl.multiple_of(base + t * TILE, TILE), TILE)

    def store(name, at, value, n):
        s[name + "0"][:, :, at] = value.astype(BF16).reshape(4, 128, n)
        if name + "11" in s:
            s[name + "11"][:, :, at] = value.reshape(4, 128, n)

    def product(name, fn, n):
        def run():
            def body(t):
                store(name, cols(t), fn(t), TILE)

            tiles(n, body)

        ops["M " + name] = run

    def back(base):
        return lambda t: mmt(gw[...], s["wdown"][tile_at(base, t), :])

    def forth(base):
        return lambda t: mm(s["normed"][...], s["wup"][:, tile_at(base, t)])

    product("Ba", lambda t: mmt(gw[...], s["wout"][...]), 1)
    product("Bh1", back(0), 2)
    product("Bh2", back(1536), 2)
    product("Fh1", forth(0), 2)
    product("Fh2", forth(1536), 2)

    product("Fq", lambda t: mm(s["normed"][...], s["wqkv"][:, cols(t)]), 3)

    @op
    def load_query():
        for load in loads[5:]:
            load.wait()

    ops["load 2"], ops["load 3"], ops["load 5"] = (loads[i].wait for i in (2, 3, 4))
    ops["load 4"] = load_query

    def activate(stream, gather, base):
        for i, value in enumerate(R[stream].fin()):
            G[gather].put(i, gelu_value(value).astype(BF16))
            at = base + i * G[gather].ca
            slope[:, at : at + value.shape[1]] = gelu_slope(value)

    def deactivate(stream, gather, base):
        for i, value in enumerate(R[stream].fin()):
            at = base + i * G[gather].ca
            G[gather].put(i, (value * slope[:, at : at + value.shape[1]]).astype(BF16))

    ops["act Fh1"] = lambda: activate("Fh1", "H1", 0)
    ops["act Fh2"] = lambda: activate("Fh2", "H2", 1536)
    ops["deact Bh1"] = lambda: deactivate("Bh1", "G1", 0)
    ops["deact Bh2"] = lambda: deactivate("Bh2", "G2", 1536)

    @op
    def project():
        ja, jb = R["Fq"].fin()
        s["ja"][...] = ja
        s["jb"][...] = jb.reshape(64, 3 * HS)
        normal, _ = head_norm(s["ja"][:, HS : 2 * HS])
        s["KVa"][k.y, :, 0:HS] = normal.astype(BF16)
        s["KVa"][k.y, :, HS : 2 * HS] = s["ja"][:, 2 * HS :].astype(BF16)
        normal, _ = head_norm(s["jb"][:, HS : 2 * HS])
        s["KVb"][k.x, KV.mine, :, 0:HS] = normal.astype(BF16).reshape(2, 32, HS)
        s["KVb"][k.x, KV.mine, :, HS : 2 * HS] = (
            s["jb"][:, 2 * HS :].astype(BF16).reshape(2, 32, HS)
        )

    @op
    def attend():
        parts = R["Ba"].fin()
        for i, (kv, dk, dk_x, own) in enumerate(
            (
                (s["KVa"], s["DKa"], s["DKax"], s["ja"]),
                (s["KVb"], s["DKb"], s["DKbx"], s["jb"]),
            )
        ):
            shape = kv.shape[:-1] + (HS,)
            q_norm, q_inv = head_norm(own[:, 0:HS])
            q_b = q_norm.astype(BF16)
            keys = kv[..., 0:HS].reshape(TOK, HS)
            values = kv[..., HS : 2 * HS].reshape(TOK, HS)
            raised = jnp.exp(mmt(q_b, keys) * FACTOR)
            probs = raised / jnp.sum(raised, -1, keepdims=True)
            probs_b = probs.astype(BF16)
            part = parts[i].astype(BF16).reshape(own.shape[0], HS)
            grad_probs = mmt(part, values)
            row_dot = jnp.sum(probs * grad_probs, -1, keepdims=True)
            grad_scores = (probs * (grad_probs - row_dot)).astype(BF16)
            dk_x[..., 0:HS] = (mtm(grad_scores, q_b) * FACTOR).reshape(shape)
            dk_x[..., HS : 2 * HS] = mtm(probs_b, part).reshape(shape)
            dk[...] = dk_x[...].astype(BF16)
            G["AT"].put_head(i, 0, mm(probs_b, values).astype(BF16))
            grad_query = mm(grad_scores, keys) * FACTOR
            G["GJ"].put_head(i, 0, head_norm_back(grad_query, q_norm, q_inv).astype(BF16))

    def key_value_back(i, own, value):
        k_norm, k_inv = head_norm(own[:, HS : 2 * HS])
        G["GJ"].put_head(i, HS, head_norm_back(value[:, 0:HS], k_norm, k_inv).astype(BF16))
        G["GJ"].put_head(i, 2 * HS, value[:, HS:].astype(BF16))

    ops["KV d3"] = lambda: key_value_back(0, s["ja"], KV.d3())
    ops["KV d4"] = lambda: key_value_back(1, s["jb"], KV.d4().reshape(64, 2 * HS))

    copies = []

    def share(name, half, got, out):
        def give():
            held[name] = k.send(half(1 - core), got, k.cd)

        def add():
            held[name].wait_recv()
            mine = half(core)
            add_to(mine, got)
            copies.append(pltpu.make_async_copy(mine, out, local.at[11 + len(copies)]))
            copies[-1].start()

        ops["sum " + name] = add
        return give

    def share_wide(name, stream, got, out, base):
        assert ORDER.index("dw " + name) > ORDER.index(stream + " s2") + SETTLE
        at = pl.ds(base, 1536)
        part = s[stream + "0"]
        give = share(
            name,
            lambda c: part.at[pl.ds(2 * c, 2), pl.ds(0, 96)],
            s[got].at[:, :, at],
            out.at[:, :, at],
        )

        def put(t, value):
            for c in range(2):
                half = value[c * 192 : (c + 1) * 192].astype(BF16)
                part[2 * c : 2 * c + 2, 0:96, cols(t)] = half.reshape(2, 96, TILE)

        return put, give

    def rows_tile(name, t):
        return s[name][:, :, cols(t)].reshape(TOK, TILE)

    def whole(name):
        return s[name][...].reshape(TOK, s[name].shape[2])

    def with_hidden(name, stream, base):
        put, give = share_wide(name, stream, "gotdown", sum_down, base)

        def total():
            add_rows(oacc, mm(whole(name), s["wdown"][pl.ds(base, 1536), :]))

        def weights(t):
            put(t, mm(wide(gg), rows_tile(name, t)))

        def run():
            tiles(2, weights)
            give()

        ops["acc " + name] = total
        ops["dw " + name] = run

    def with_grads(name, stream, base):
        put, give = share_wide(name, stream, "gotup", sum_up, base)

        def total():
            add_rows(gacc, mmt(whole(name), s["wup"][:, pl.ds(base, 1536)]))

        def weights(t):
            put(t, mm(s["nT"][...], rows_tile(name, t)))

        def run():
            tiles(2, weights)
            give()

        ops["acc " + name] = total
        ops["dw " + name] = run

    with_hidden("H1", "Fh1", 0)
    with_hidden("H2", "Fh2", 1536)
    with_grads("G1", "Bh1", 0)
    with_grads("G2", "Bh2", 1536)

    ops["acc AT"] = lambda: add_rows(oacc, mm(whole("AT"), s["wout"][...]))
    ops["acc GJ"] = lambda: add_rows(gacc, mmt(whole("GJ"), s["wqkv"][...]))

    give_attended = share("AT", lambda c: s["sattn"].at[c], s["gotattn"], sum_attn)
    give_joined = share("GJ", lambda c: s["sqkv"].at[c], s["gotqkv"], sum_qkv)

    def weights_attended():
        both = mm(wide(gg), rows_tile("AT", 0)).astype(BF16)
        for c in range(2):
            for h in range(HEADS):
                s["sattn"][c, h] = both[c * 192 : (c + 1) * 192, h * HS : (h + 1) * HS]
        give_attended()

    ops["dw AT"] = weights_attended

    def zscatter(i, total):
        part = s["zp"].at[i]
        turned = mmt(s["eye"][0:BLK, 0:BLK], total.astype(BF16))
        part[...] = turned.astype(BF16).reshape(4, ZC, TOK)
        ring = RingSum(
            k, k.zs, k.zd, lambda j: part.at[j], *split_rows(48), s["zo"].at[i], s["zn"].at[i]
        )
        return ring, turned

    @op
    def gin():
        average, inverse = s["stat"][0:1], s["stat"][1:2]
        held["zi"], turned = zscatter(1, gacc[...].reshape(TOK, BLK))
        held["zi"].start()
        normal = (wide(fg).astype(F32) - average) * inverse
        packed = row_pack(
            jnp.sum(turned, 0, keepdims=True), jnp.sum(turned * normal, 0, keepdims=True)
        )
        held["bz"] = exchange(k, k.zs, k.zd, s["btz"], packed)

    def weights_joined():
        for t in range(3):
            both = mm(s["nT"][...], rows_tile("GJ", t)).astype(BF16)
            for c in range(2):
                for i in range(2):
                    s["sqkv"][c, 2 * t + i] = both[
                        c * 192 : (c + 1) * 192, i * 3 * HS : (i + 1) * 3 * HS
                    ]
        give_joined()

    ops["dw GJ"] = weights_joined

    @op
    def zi_mid():
        held["zi"].middle()

    @op
    def back_x():
        held["bx"] = exchange(k, k.xs, k.xd, s["btx"], collect(held["bz"], s["btz"]))

    @op
    def back_y():
        held["by"] = exchange(k, k.ys, k.yd, s["bty"], collect(held["bx"], s["btx"]))

    @op
    def gin_out():
        average, inverse = s["stat"][0:1], s["stat"][1:2]
        summed = held["zi"].total()
        sums = collect(held["by"], s["bty"])
        normal_own = (fg[z].astype(F32) - average) * inverse
        correction = summed - sums[0:1] / D - normal_own * (sums[1:2] / D)
        gin_o[...] = (gg[z].astype(F32) + inverse * correction).astype(BF16)

    @op
    def zl_start():
        held["zl"], _ = zscatter(0, oacc[...].reshape(TOK, BLK))
        held["zl"].start()

    @op
    def zl_mid():
        held["zl"].middle()

    @op
    def layer_out():
        layer_o[...] = (fg[z].astype(F32) + held["zl"].total()).astype(BF16)

    for i, name in enumerate(ORDER):
        ops[name]()
        k.settle(i)

    for copy in copies:
        copy.wait()
    k.settle(len(ORDER) + SETTLE)


def on_device(features, w_qkv, w_up, w_out, w_down, grad_out):
    out_flat = w_out.reshape(768, BLK)
    shapes = scratch()
    any_spec = pl.BlockSpec(memory_space=pl.ANY)
    vmem_spec = pl.BlockSpec(memory_space=pltpu.VMEM)

    grads = ((HEADS, 192, 3 * HS), (2, 96, 3072), (HEADS, 192, HS), (2, 96, 3072))
    names = tuple(shapes)
    outs = pl.pallas_call(
        lambda *refs: kernel(names, *refs),
        out_shape=[jax.ShapeDtypeStruct(shape, BF16) for shape in ((ZC, TOK),) * 2 + grads],
        in_specs=[any_spec] * 6,
        out_specs=[vmem_spec] * 2 + [any_spec] * 4,
        scratch_shapes=list(shapes.values()),
        compiler_params=pltpu.CompilerParams(
            collective_id=0, has_side_effects=True, vmem_limit_bytes=62 * 1024 * 1024
        ),
        cost_estimate=pl.CostEstimate(
            flops=11_000_000_000, bytes_accessed=20_000_000, transcendentals=1_000_000
        ),
    )(features.T, grad_out.T, w_qkv.transpose(1, 0, 2), w_up, out_flat, w_down)

    layer_out, grad_in, *grads = finish(
        [out.reshape(192, 3072) if out.shape[0] == 2 else out for out in outs]
    )
    grad_qkv, grad_up, grad_attn, grad_down = grads
    return (
        layer_out.T,
        grad_in.T,
        grad_qkv.transpose(1, 0, 2),
        grad_up,
        grad_attn.transpose(0, 2, 1),
        grad_down.T,
    )


PIECES = 3


def widen_grads(*refs):
    ins, outs, scr = refs[:6], refs[6:12], refs[12:]
    narrow, whole, small, sem = scr[0:4], scr[4:8], scr[8:10], scr[10]
    reads, writes = [], []

    def piece(ref, p):
        n = ref.shape[0] // PIECES
        return ref.at[pl.ds(p * n, n)]

    def move(src, dst):
        copy = pltpu.make_async_copy(src, dst, sem.at[len(reads) + len(writes)])
        copy.start()
        return copy

    for i in range(4):
        for p in range(PIECES):
            reads.append(move(piece(ins[2 + i], p), piece(narrow[i], p)))
    for i in range(2):
        reads.append(move(ins[i], small[i]))
    turn = iter(reads)
    for i in range(4):
        for p in range(PIECES):
            next(turn).wait()
            into = piece(whole[i], p)
            into[...] = piece(narrow[i], p)[...].astype(F32)
            writes.append(move(into, piece(outs[2 + i], p)))
    for i in range(2):
        next(turn).wait()
        writes.append(move(small[i], outs[i]))
    for copy in writes:
        copy.wait()


def finish(arrays):
    grads = arrays[2:]
    any_spec = pl.BlockSpec(memory_space=pl.ANY)
    return pl.pallas_call(
        widen_grads,
        out_shape=[jax.ShapeDtypeStruct((ZC, TOK), BF16)] * 2
        + [jax.ShapeDtypeStruct(array.shape, F32) for array in grads],
        in_specs=[any_spec] * 6,
        out_specs=[any_spec] * 6,
        scratch_shapes=[pltpu.VMEM(array.shape, BF16) for array in grads]
        + [pltpu.VMEM(array.shape, F32) for array in grads]
        + [pltpu.VMEM((ZC, TOK), BF16)] * 2
        + [pltpu.SemaphoreType.DMA((8 * PIECES + 4,))],
        compiler_params=pltpu.CompilerParams(vmem_limit_bytes=60 * 1024 * 1024),
        cost_estimate=pl.CostEstimate(
            flops=2_000_000, bytes_accessed=11_000_000, transcendentals=0
        ),
    )(*arrays)


def solution(mesh):
    in_specs = (
        P("dp", ("mx", "my")),
        P("mx", "my", None),
        P("mx", "my"),
        P("my", None, "mx"),
        P("my", "mx"),
        P("dp", ("mx", "my")),
    )
    out_specs = (
        P("dp", ("mx", "my")),
        P("dp", ("mx", "my")),
        P(("mx", "dp"), "my", None),
        P(("mx", "dp"), "my"),
        P("my", None, ("mx", "dp")),
        P("my", ("mx", "dp")),
    )
    return jax.shard_map(
        on_device, mesh=mesh, in_specs=in_specs, out_specs=out_specs, check_vma=False
    )
```
